128 devices in a mesh: sections: 4 (over x), cache: 16 (over z, y), heads: 2 (over core).
Axes of the slice: x: 4, y: 4, z: 4, core: 2. Of those that a mesh axis runs over, the one named last changes fastest.
Arguments:
- hidden: bfloat16 [4, 4096, 2048], P('sections', 'cache'), may hold values from -6 to 6
- norm_gain: float32 [4, 2048], P('sections'), may hold values from 0.1 to 1.9
- w_query: bfloat16 [4, 2048, 4096], P('sections', None, 'heads'), may hold values from -0.125 to 0.125
- query_gain: float32 [4, 128], P('sections'), may hold values from 0.1 to 1.9
- w_output: bfloat16 [4, 4096, 2048], P('sections', 'heads'), may hold values from -0.09375 to 0.09375
- key_cache: bfloat16 [4, 512, 64, 512], P('sections', 'cache', None, 'heads'), may hold values from -6 to 6
- value_cache: bfloat16 [4, 512, 64, 512], P('sections', 'cache', None, 'heads'), may hold values from -6 to 6
- key_scale: float32 [4, 512, 4], P('sections', 'cache', 'heads'), may hold values from 0.5 to 120
- value_scale: float32 [4, 512, 4], P('sections', 'cache', 'heads'), may hold values from 0.5 to 2
- page_table: int32 [512], replicated, may hold values from 0 to 511, as said below
- page_tokens: int32 [512], replicated, may hold values from 1 to 64
- page_list: int32 [4, 32, 64], P('sections'), may hold values from 0 to 511, as said below
- list_len: int32 [4, 32], P('sections'), may hold values from 32 to 64, as said below
Outputs:
- mixed: bfloat16 [4, 4096, 2048], P('sections', 'cache', 'heads')
The draws below stay inside these ranges and needn't reach their ends.
Inputs may be any that keep to these rules, and one draw needn't show every extreme that they name: `page_table`: A permutation of the 512 slots; slot // 32 is the cache index that holds the page. `page_list`: the 64 entries of a block are distinct logical pages; among them at most 8 have their slot on any one cache index, and in every block some cache index holds exactly 8 of them. Entries of a list from list_len on are unused; some block uses all 64 entries.
All inputs are finite; a program needn't handle non-finite values.
Results may differ from the reference program's by a relative error of at most 0.008.
The reference program's roundings to bfloat16 on the way (of `normed`, `queries`, `scaled`, `attended` and `updated`) count: a program that leaves them out, or rounds other values in their place, can miss the bound.
Values may be sent and summed in bfloat16 or wider, within the bound.
No kernel may reach another device: no remote copies, remote signals or barrier semaphores. Data moves between devices by JAX's collectives and lax.ppermute only.
A program may use at most 128 MiB of HBM per device.

```python
import math
import jax
import jax.numpy as jnp
from jax import lax

D = 2048
Q_HEADS = 32
KV_HEADS = 4
HEAD_DIM = 128
QBLOCK = 128
PAGE = 64
PAGES_DEV = 32
MOST = 8
LIST = 64
PAGES = 512
BLOCKS = 32
ROWS = 4096
N_SECTIONS = 4
N_CACHE = 16


def page_layout(key):
    slot_of_page = jax.random.permutation(jax.random.fold_in(key, 11), PAGES).astype(jnp.int32)
    page_of_slot = jnp.argsort(slot_of_page).astype(jnp.int32)
    remaining = LIST - MOST
    base_count = remaining // (N_CACHE - 1)
    leftover = remaining % (N_CACHE - 1)
    pair_count = (N_CACHE - 1) // 2
    headroom = base_count // 2
    shard_ids = jnp.arange(N_CACHE, dtype=jnp.int32)
    slot_ids = jnp.arange(PAGES, dtype=jnp.int32)
    slot_shard = slot_ids // PAGES_DEV

    def one_list(block_key):
        busy_shard = jax.random.randint(jax.random.fold_in(block_key, 1), (), 0, N_CACHE)
        spread = jax.random.permutation(jax.random.fold_in(block_key, 2), N_CACHE - 1).astype(jnp.int32)
        others = base_count + (spread < leftover).astype(jnp.int32)
        amounts = jax.random.randint(jax.random.fold_in(block_key, 3), (pair_count,), 0, headroom + 1).astype(jnp.int32)
        moves = jnp.zeros((N_CACHE - 1,), jnp.int32)
        moves = moves.at[0:2 * pair_count:2].add(amounts).at[1:2 * pair_count:2].add(-amounts)
        others = others + moves
        position = jnp.clip(shard_ids - (shard_ids > busy_shard).astype(jnp.int32), 0, N_CACHE - 2)
        quota = jnp.where(shard_ids == busy_shard, MOST, others[position])
        ranking = jax.random.permutation(jax.random.fold_in(block_key, 4), PAGES).astype(jnp.int32)
        sorted_order = jnp.argsort(slot_shard * PAGES + ranking)
        within = jnp.argsort(sorted_order).astype(jnp.int32) - slot_shard * PAGES_DEV
        chosen = (within < quota[slot_shard]).astype(jnp.int32)
        shuffle = jax.random.permutation(jax.random.fold_in(block_key, 5), PAGES).astype(jnp.int32)
        picked = jnp.argsort((1 - chosen) * PAGES + shuffle)[:LIST]
        return page_of_slot[picked]
    block_keys = jax.vmap(lambda index: jax.random.fold_in(key, index))(jnp.arange(N_SECTIONS * BLOCKS))
    lists = jax.vmap(one_list)(block_keys).reshape(N_SECTIONS, BLOCKS, LIST)
    return (slot_of_page, lists)


def draw_page_table(key, part):
    return page_layout(key)[0].astype(jnp.int32)


def draw_page_list(key, part):
    return page_layout(key)[1].astype(jnp.int32)


def draw_list_len(key, part):
    lengths = jax.random.randint(jax.random.fold_in(key, 21), (N_SECTIONS * BLOCKS,), LIST // 2, LIST + 1)
    full_block = jax.random.randint(jax.random.fold_in(key, 22), (), 0, N_SECTIONS * BLOCKS)
    flat = jnp.where(jnp.arange(N_SECTIONS * BLOCKS) == full_block, LIST, lengths)
    return flat.reshape(N_SECTIONS, BLOCKS).astype(jnp.int32)


def draw_key_scale(key, part):
    shape = (N_SECTIONS, PAGES, KV_HEADS)
    scales = jnp.exp(jax.random.uniform(jax.random.fold_in(key, 31), shape, jnp.float32, math.log(0.5), math.log(2.0)))
    return scales.astype(jnp.float32)


def place_ends(drawn, own_key, smallest, high):
    dims = drawn.shape
    spot = [jax.random.randint(jax.random.fold_in(own_key, axis), (), 0, dims[axis]) for axis in range(len(dims))]
    drawn = drawn.at[tuple(spot)].set(smallest)
    longest = dims.index(max(dims))
    spot[longest] = (spot[longest] + 1) % dims[longest]
    return drawn.at[tuple(spot)].set(high)


def block_scale(own_key, shape, shards, low, largest):
    loudness = 1.0
    for dim, shards_of in shards:
        steps = jax.random.uniform(jax.random.fold_in(jax.random.fold_in(own_key, 6), dim), (shards_of,), jnp.float32, low / len(shards), largest / len(shards))
        loudness = loudness * jnp.repeat(jnp.exp(steps), shape[dim] // shards_of).reshape((-1,) + (1,) * (len(shape) - 1 - dim))
    return loudness


def normal_values(stream_key, dims, width, reach, cuts=(), held_as=jnp.bfloat16):
    values = jax.random.normal(stream_key, dims, jnp.float32) * width
    if len(cuts) > 0:
        values = block_scale(stream_key, dims, cuts, -0.22, 0.18) * values
    return jnp.clip(values, min=-reach, max=reach).astype(held_as)


def setup_inputs(seed: int = 0) -> dict:
    streams_of = jax.random.split(jax.random.key(seed), 14)
    return {
        "hidden": normal_values(streams_of[0], (N_SECTIONS, ROWS, D), 1.0, 6.0, ((0, 4), (1, 16))),
        "norm_gain": jnp.clip(1.0 + 0.18 * jax.random.normal(streams_of[1], (N_SECTIONS, D), jnp.float32), 0.1, 1.9),
        "w_query": normal_values(streams_of[2], (N_SECTIONS, D, Q_HEADS * HEAD_DIM), D ** -0.5, 0.125, ((0, 4), (2, 2))),
        "query_gain": jnp.clip(1.0 + 0.18 * jax.random.normal(streams_of[3], (N_SECTIONS, HEAD_DIM), jnp.float32), 0.1, 1.9),
        "w_output": normal_values(streams_of[4], (N_SECTIONS, Q_HEADS * HEAD_DIM, D), (Q_HEADS * HEAD_DIM) ** -0.5, 0.09375, ((0, 4), (1, 2))),
        "key_cache": normal_values(streams_of[5], (N_SECTIONS, PAGES, PAGE, KV_HEADS * HEAD_DIM), 1.0, 6.0, ((0, 4), (1, 16), (3, 2))),
        "value_cache": normal_values(streams_of[6], (N_SECTIONS, PAGES, PAGE, KV_HEADS * HEAD_DIM), 1.0, 6.0, ((0, 4), (1, 16), (3, 2))),
        "key_scale": draw_key_scale(jax.random.fold_in(streams_of[13], 71), 0),
        "value_scale": jnp.clip(jnp.exp(math.log(2.0) - 1.3862944 * jax.random.uniform(streams_of[8], (N_SECTIONS, PAGES, KV_HEADS), jnp.float32) ** block_scale(streams_of[8], (N_SECTIONS, PAGES, KV_HEADS), ((0, 4), (1, 16), (2, 2)), -0.2, 0.2)), 0.5, 2.0),
        "page_table": draw_page_table(jax.random.fold_in(streams_of[13], 71), 0),
        "page_tokens": place_ends(jax.random.randint(streams_of[10], (PAGES,), 1, PAGE + 1), jax.random.fold_in(streams_of[10], 1), 1, PAGE).astype(jnp.int32),
        "page_list": draw_page_list(jax.random.fold_in(streams_of[13], 71), 0),
        "list_len": draw_list_len(jax.random.fold_in(streams_of[13], 71), 0),
    }


tiny_eps = 1e-06
masked_score = -1e+30

def one_section(hidden_rows, gain_row, query_weight, head_gain, output_weight, key_pages, value_pages, key_scales, value_scales, page_table, page_tokens, lists, lengths):
    inputs = hidden_rows.astype(jnp.float32)
    inverse = lax.rsqrt(lax.optimization_barrier(jnp.mean(inputs * inputs, axis=-1, keepdims=True)) + tiny_eps)
    normed = (inputs * inverse * gain_row).astype(jnp.bfloat16)
    projected = jnp.dot(normed, query_weight, preferred_element_type=jnp.float32).reshape(ROWS, Q_HEADS, HEAD_DIM)
    head_inverse = lax.rsqrt(lax.optimization_barrier(jnp.mean(projected * projected, axis=-1, keepdims=True)) + tiny_eps)
    queries = (projected * head_inverse * head_gain / math.sqrt(HEAD_DIM)).astype(jnp.bfloat16)
    group_size = Q_HEADS // KV_HEADS
    queries = queries.reshape(BLOCKS, QBLOCK, KV_HEADS, group_size, HEAD_DIM)

    def one_block(block_args):
        block_queries, entries, length = block_args
        slots = page_table[entries]
        counts = page_tokens[entries]
        key_rows = key_pages[slots].reshape(LIST * PAGE, KV_HEADS, HEAD_DIM).astype(jnp.float32)
        value_rows = value_pages[slots].reshape(LIST * PAGE, KV_HEADS, HEAD_DIM).astype(jnp.float32)
        key_factor = jnp.repeat(key_scales[slots], PAGE, axis=0).T
        value_factor = jnp.repeat(value_scales[slots], PAGE, axis=0).T
        entry_ids = jnp.arange(LIST, dtype=jnp.int32)
        token_ids = jnp.arange(PAGE, dtype=jnp.int32)
        live_mask = ((entry_ids[:, None] < length) & (token_ids[None, :] < counts[:, None])).reshape(LIST * PAGE)
        scores = jnp.einsum('rgjd,tgd->gjrt', block_queries.astype(jnp.float32), key_rows) * key_factor[:, None, None, :]
        scores = jnp.where(live_mask, scores, masked_score)
        top_score = lax.optimization_barrier(jnp.max(scores, axis=-1, keepdims=True))
        weights = jnp.where(live_mask, jnp.exp(scores - top_score), 0.0)
        totals = lax.optimization_barrier(jnp.sum(weights, axis=-1))
        rounded = lax.optimization_barrier((weights * value_factor[:, None, None, :]).astype(jnp.bfloat16))
        scaled = rounded.astype(jnp.float32)
        attended = jnp.einsum('gjrt,tgd->rgjd', scaled, value_rows) / jnp.transpose(totals, (2, 0, 1))[..., None]
        return attended.astype(jnp.bfloat16).reshape(QBLOCK, Q_HEADS * HEAD_DIM)
    attention = lax.map(one_block, (queries, lists, lengths)).reshape(ROWS, Q_HEADS * HEAD_DIM)
    updated = jnp.dot(attention, output_weight, preferred_element_type=jnp.float32) + inputs
    return updated.astype(jnp.bfloat16)

def reference(hidden, norm_gain, w_query, query_gain, w_output, key_cache, value_cache, key_scale, value_scale, page_table, page_tokens, page_list, list_len):
    results = []
    for section_id in range(N_SECTIONS):
        results.append(one_section(hidden[section_id], norm_gain[section_id], w_query[section_id], query_gain[section_id], w_output[section_id], key_cache[section_id], value_cache[section_id], key_scale[section_id], value_scale[section_id], page_table, page_tokens, page_list[section_id], list_len[section_id]))
    stacked = jnp.stack(results, axis=0)
    return jnp.roll(stacked, 1, axis=0)
```

```python
import functools
import math

import jax
import jax.numpy as jnp
from jax import lax
from jax.experimental import pallas as pl
from jax.experimental.pallas import tpu as pltpu
from jax.sharding import PartitionSpec as P

QBLOCK = 128
QB_DEV = 2
MOST = 8
GRANULE = 16
CHUNK = 512
QTILE = 256

tiny_eps = 1e-06
masked_score = -1e30
lowest = -1e38


def lookup(entries, table):
    places = jnp.arange(table.shape[0], dtype=jnp.int32)
    return jnp.sum(jnp.where(entries[..., None] == places, table, 0), axis=-1)


def ranked(chosen):
    listed = chosen.shape[-1]
    order = jnp.arange(listed, dtype=jnp.int32)
    before = order[:, None] < order[None, :]
    ranks = jnp.sum(jnp.where(before & chosen[..., :, None], 1, 0), axis=-2)
    wanted = jnp.arange(MOST, dtype=jnp.int32)
    return (ranks[..., None, :] == wanted[:, None]) & chosen[..., None, :]


def pick(picks, values):
    return jnp.sum(jnp.where(picks, values[..., None, :], 0), axis=-1)


def pack_kernel(cnt_ref, rows_ref, page_ref, k_ref, v_ref, out_ref, buf, sems, *, page_len):
    homes, height, _ = out_ref.shape
    head_size = k_ref.shape[1]

    def copy_of(home, slot):
        return pltpu.make_async_copy(buf.at[slot, pl.ds(0, height), :], out_ref.at[home], sems.at[slot])

    def one_home(home, carry):
        slot = lax.rem(home, 2)

        @pl.when(home >= 2)
        def _():
            copy_of(home - 2, slot).wait()

        row = jnp.int32(0)
        for b in range(QB_DEV):
            block = home * QB_DEV + b

            def one_page(j, row, block=block):
                at = block * MOST + j
                here = pl.multiple_of(page_ref[at] * page_len, page_len)
                there = pl.multiple_of(row, GRANULE)
                buf[slot, pl.ds(there, page_len), 0:head_size] = k_ref[pl.ds(here, page_len), :]
                buf[slot, pl.ds(there, page_len), head_size : 2 * head_size] = v_ref[pl.ds(here, page_len), :]
                return row + rows_ref[at]

            row = lax.fori_loop(0, cnt_ref[block], one_page, row)
        copy_of(home, slot).start()
        return carry

    lax.fori_loop(0, homes, one_home, 0)
    copy_of(homes - 2, 0).wait()
    copy_of(homes - 1, 1).wait()


def pack(cnt, rows, pages, key_rows, value_rows, g, homes, height, page_len, head_size):
    tokens = key_rows.shape[0]
    return pl.pallas_call(
        functools.partial(pack_kernel, page_len=page_len),
        grid_spec=pltpu.PrefetchScalarGridSpec(
            num_scalar_prefetch=3,
            grid=(1,),
            in_specs=[
                pl.BlockSpec((tokens, head_size), lambda i, *_: (0, g)),
                pl.BlockSpec((tokens, head_size), lambda i, *_: (0, g)),
            ],
            out_specs=pl.BlockSpec(memory_space=pl.ANY),
            scratch_shapes=[
                pltpu.VMEM((2, height + page_len, 2 * head_size), jnp.bfloat16),
                pltpu.SemaphoreType.DMA((2,)),
            ],
        ),
        out_shape=jax.ShapeDtypeStruct((homes, height, 2 * head_size), jnp.bfloat16),
        compiler_params=pltpu.CompilerParams(vmem_limit_bytes=24 << 20),
        cost_estimate=pl.CostEstimate(
            flops=0, transcendentals=0, bytes_accessed=homes * height * 4 * head_size + tokens * 4 * head_size
        ),
    )(cnt, rows, pages, key_rows, value_rows)


def attend_kernel(
    cnt_ref, first_ref, height_ref, rows_ref, live_ref, kscale_ref, vscale_ref,
    qt_ref, recv_ref, out_ref,
    kv, kcol, vcol, bias, acc, top, total, sems, *, page_len,
):
    sources = recv_ref.shape[0]
    head_size, width = qt_ref.shape

    def copy_of(s, at):
        n = pl.multiple_of(height_ref[s], GRANULE)
        start = pl.multiple_of(first_ref[s], GRANULE)
        at = pl.multiple_of(at, GRANULE)
        return pltpu.make_async_copy(
            recv_ref.at[s, pl.ds(start, n), :], kv.at[pl.ds(at, n), :], sems.at[s]
        )

    def start_one(s, at):
        @pl.when(height_ref[s] > 0)
        def _():
            copy_of(s, at).start()

        return at + height_ref[s]

    def wait_one(s, at):
        @pl.when(height_ref[s] > 0)
        def _():
            copy_of(s, at).wait()

        return at + height_ref[s]

    used = lax.fori_loop(0, sources, start_one, jnp.int32(0))
    token = lax.broadcasted_iota(jnp.int32, (page_len, 128), 0)

    def columns_of(s, at):
        def one_page(j, at):
            e = s * MOST + j
            here = pl.ds(pl.multiple_of(at, GRANULE), page_len)
            kcol[here, :] = jnp.full((page_len, 128), kscale_ref[e], jnp.float32)
            vcol[here, :] = jnp.full((page_len, 128), vscale_ref[e], jnp.float32)
            bias[here, :] = jnp.where(token < live_ref[e], 0.0, masked_score)
            return at + rows_ref[e]

        return lax.fori_loop(0, cnt_ref[s], one_page, at)

    lax.fori_loop(0, sources, columns_of, jnp.int32(0))
    rest = pl.ds(pl.multiple_of(used, GRANULE), CHUNK)
    kcol[rest, :] = jnp.zeros((CHUNK, 128), jnp.float32)
    vcol[rest, :] = jnp.zeros((CHUNK, 128), jnp.float32)
    bias[rest, :] = jnp.full((CHUNK, 128), masked_score, jnp.float32)
    kv[rest, :] = jnp.zeros((CHUNK, 2 * head_size), jnp.bfloat16)
    acc[...] = jnp.zeros_like(acc)
    total[...] = jnp.zeros_like(total)
    top[...] = jnp.full_like(top, lowest)
    lax.fori_loop(0, sources, wait_one, jnp.int32(0))

    def chunk(c, carry):
        here = pl.ds(pl.multiple_of(c * CHUNK, CHUNK), CHUNK)
        keys = kv[here, 0:head_size]
        values = kv[here, head_size : 2 * head_size].T
        for i in range(width // QTILE):
            cols = pl.ds(i * QTILE, QTILE)
            score = jnp.dot(keys, qt_ref[:, cols], preferred_element_type=jnp.float32)
            kc, bc, vc = kcol[here, :], bias[here, :], vcol[here, :]
            wide = lambda x: jnp.concatenate([x] * (QTILE // 128), axis=1)
            score = score * wide(kc) + wide(bc)
            old = top[0:1, cols]
            new = jnp.maximum(old, jnp.max(score, axis=0, keepdims=True))
            weight = jnp.exp2(score - new)
            fade = jnp.exp2(old - new)
            total[0:1, cols] = total[0:1, cols] * fade + jnp.sum(weight, axis=0, keepdims=True)
            scaled = (weight * wide(vc)).astype(jnp.bfloat16)
            acc[:, cols] = acc[:, cols] * fade + jnp.dot(values, scaled, preferred_element_type=jnp.float32)
            top[0:1, cols] = new
        return carry

    lax.fori_loop(0, (used + CHUNK - 1) // CHUNK, chunk, 0)
    for h in range(width // QBLOCK):
        cols = slice(h * QBLOCK, (h + 1) * QBLOCK)
        out_ref[:, h * head_size : (h + 1) * head_size] = (acc[:, cols] / total[0:1, cols]).T.astype(jnp.bfloat16)


def attend(plan, qt, received, page_len, most_rows):
    head_size, width = qt.shape
    sources = received.shape[0]
    rows_held = most_rows + CHUNK + page_len
    out_width = width // QBLOCK * head_size
    return pl.pallas_call(
        functools.partial(attend_kernel, page_len=page_len),
        grid_spec=pltpu.PrefetchScalarGridSpec(
            num_scalar_prefetch=7,
            grid=(1,),
            in_specs=[
                pl.BlockSpec((head_size, width), lambda i, *_: (0, 0)),
                pl.BlockSpec(memory_space=pl.ANY),
            ],
            out_specs=pl.BlockSpec((QBLOCK, out_width), lambda i, *_: (0, 0)),
            scratch_shapes=[
                pltpu.VMEM((rows_held, 2 * head_size), jnp.bfloat16),
                pltpu.VMEM((rows_held, 128), jnp.float32),
                pltpu.VMEM((rows_held, 128), jnp.float32),
                pltpu.VMEM((rows_held, 128), jnp.float32),
                pltpu.VMEM((head_size, width), jnp.float32),
                pltpu.VMEM((8, width), jnp.float32),
                pltpu.VMEM((8, width), jnp.float32),
                pltpu.SemaphoreType.DMA((sources,)),
            ],
        ),
        out_shape=jax.ShapeDtypeStruct((QBLOCK, out_width), jnp.bfloat16),
        compiler_params=pltpu.CompilerParams(vmem_limit_bytes=40 << 20),
        cost_estimate=pl.CostEstimate(
            flops=4 * width * most_rows * head_size,
            transcendentals=width * most_rows,
            bytes_accessed=most_rows * 4 * head_size + width * head_size * 4,
        ),
    )(*plan, qt, received)


def body(
    hidden,
    norm_gain,
    w_query,
    query_gain,
    w_output,
    key_cache,
    value_cache,
    key_scale,
    value_scale,
    page_table,
    page_tokens,
    page_list,
    list_len,
):
    row_count, model_width = hidden.shape[1:]
    head_size = query_gain.shape[1]
    kv_local = key_scale.shape[2]
    heads_local = w_query.shape[2] // head_size
    group_size = heads_local // kv_local
    pages_dev, page_len = key_cache.shape[1:3]
    listed = page_list.shape[2]
    shard_count = lax.axis_size("cache")
    own_shard = lax.axis_index("cache")
    height = QB_DEV * MOST * page_len

    entry = lookup(page_list[0], page_table * 128 + page_tokens)
    slots, counts = entry // 128, entry % 128
    used = jnp.arange(listed, dtype=jnp.int32) < list_len[0][:, None]
    rows = (counts + GRANULE - 1) // GRANULE * GRANULE
    mine = (slots // pages_dev == own_shard) & used
    picks = ranked(mine)
    send_cnt = jnp.sum(mine.astype(jnp.int32), axis=-1)
    send_rows = pick(picks, rows).reshape(-1)
    send_page = pick(picks, slots % pages_dev).reshape(-1)

    key_rows = key_cache[0].reshape(pages_dev * page_len, -1)
    value_rows = value_cache[0].reshape(pages_dev * page_len, -1)
    received = []
    for g in range(kv_local):
        out = pack(
            send_cnt, send_rows, send_page, key_rows, value_rows, g, shard_count, height, page_len, head_size
        )
        if g > 0:
            out, received[-1] = lax.optimization_barrier((out, received[-1]))
        received.append(lax.all_to_all(out, "cache", split_axis=0, concat_axis=0, tiled=True))

    scales = lax.all_gather(jnp.concatenate([key_scale[0], value_scale[0]], axis=1), "cache", axis=0, tiled=True)
    first_block = own_shard * QB_DEV

    def own(x):
        return lax.dynamic_slice_in_dim(x, first_block, QB_DEV, 0)

    own_slots, own_counts, own_rows, own_used = own(slots), own(counts), own(rows), own(used)
    sources = jnp.arange(shard_count, dtype=jnp.int32)
    theirs = (own_slots[:, None, :] // pages_dev == sources[:, None]) & own_used[:, None, :]
    own_picks = ranked(theirs)
    got_cnt = jnp.sum(theirs.astype(jnp.int32), axis=-1)
    got_height = jnp.sum(jnp.where(theirs, own_rows[:, None, :], 0), axis=-1)
    got_first = jnp.stack([jnp.zeros_like(got_height[0]), got_height[0]])
    got_rows = pick(own_picks, own_rows[:, None, :]).reshape(QB_DEV, -1)
    got_live = pick(own_picks, own_counts[:, None, :]).reshape(QB_DEV, -1)
    places = jnp.arange(scales.shape[0], dtype=jnp.int32)
    at_place = own_slots[..., None] == places
    got_scales = [
        pick(own_picks, jnp.sum(jnp.where(at_place, scales[:, k], 0.0), axis=-1)[:, None, :]).reshape(QB_DEV, -1)
        for k in range(2 * kv_local)
    ]

    inputs = hidden[0].astype(jnp.float32)
    inverse = lax.rsqrt(jnp.mean(inputs * inputs, axis=-1, keepdims=True) + tiny_eps)
    normed = (inputs * inverse * norm_gain[0]).astype(jnp.bfloat16)
    projected = jnp.dot(normed, w_query[0], preferred_element_type=jnp.float32)
    projected = projected.reshape(QB_DEV, QBLOCK, kv_local, group_size, head_size)
    head_inverse = lax.rsqrt(jnp.mean(projected * projected, axis=-1, keepdims=True) + tiny_eps)
    queries = (projected * head_inverse * query_gain[0] / math.sqrt(head_size)).astype(jnp.bfloat16)
    queries = jnp.transpose(queries, (0, 2, 4, 3, 1)).reshape(QB_DEV, kv_local, head_size, group_size * QBLOCK)

    span = group_size * head_size
    heads_index = lax.axis_index("heads")
    half_width = model_width // lax.axis_size("heads")
    devices = lax.axis_size("sections")
    partial = [None] * QB_DEV
    for g in range(kv_local):
        for b in range(QB_DEV):
            plan = (
                got_cnt[b],
                got_first[b],
                got_height[b],
                got_rows[b],
                got_live[b],
                got_scales[g][b] * math.log2(math.e),
                got_scales[kv_local + g][b],
            )
            attended = attend(plan, queries[b, g], received[g], page_len, listed * page_len)
            term = jnp.dot(attended, w_output[0, g * span : (g + 1) * span], preferred_element_type=jnp.float32)
            partial[b] = term if g == 0 else partial[b] + term
    moved = []
    for b in range(QB_DEV):
        whole = partial[b]
        away = lax.dynamic_slice_in_dim(whole, (1 - heads_index) * half_width, half_width, 1)
        came = lax.ppermute(away.astype(jnp.bfloat16), "heads", [(0, 1), (1, 0)])
        kept = lax.dynamic_slice_in_dim(whole, heads_index * half_width, half_width, 1)
        residual = lax.dynamic_slice(
            inputs, (b * QBLOCK, heads_index * half_width), (QBLOCK, half_width)
        )
        result = (kept + came.astype(jnp.float32) + residual).astype(jnp.bfloat16)
        moved.append(lax.ppermute(result, "sections", [((i - 1) % devices, i) for i in range(devices)]))
    return jnp.concatenate(moved, axis=0)[None]


def solution(mesh):
    return jax.shard_map(
        body,
        mesh=mesh,
        in_specs=(
            P("sections", "cache", None),
            P("sections", None),
            P("sections", None, "heads"),
            P("sections", None),
            P("sections", "heads", None),
            P("sections", "cache", None, "heads"),
            P("sections", "cache", None, "heads"),
            P("sections", "cache", "heads"),
            P("sections", "cache", "heads"),
            P(),
            P(),
            P("sections", None, None),
            P("sections", None),
        ),
        out_specs=P("sections", "cache", "heads"),
        check_vma=False,
    )
```

```python
import functools
import math

import jax
import jax.numpy as jnp
from jax import lax
from jax.experimental import pallas as pl
from jax.experimental.pallas import tpu as pltpu
from jax.sharding import PartitionSpec as P

QBLOCK = 128
QB_DEV = 2
MOST = 8
GRANULE = 16
HEIGHTS = (448, 512, 544, 576, 608, 672, 800)
CHUNK = 512
QTILE = 256

tiny_eps = 1e-06
masked_score = -1e30
lowest = -1e38


def lookup(entries, table):
    places = jnp.arange(table.shape[0], dtype=jnp.int32)
    return jnp.sum(jnp.where(entries[..., None] == places, table, 0), axis=-1)


def pick(picks, values):
    return jnp.sum(jnp.where(picks, values[..., None, :], 0), axis=-1)


def pack_kernel(from_ref, cnt_ref, rows_ref, page_ref, k_ref, v_ref, out_ref, buf, sems, *, page_len):
    homes, height, _ = out_ref.shape
    head_size = k_ref.shape[1]

    def copy_of(home, slot):
        return pltpu.make_async_copy(buf.at[slot, pl.ds(0, height), :], out_ref.at[home], sems.at[slot])

    def one_home(home, carry):
        slot = lax.rem(home, 2)

        @pl.when(home >= 2)
        def _():
            copy_of(home - 2, slot).wait()

        row = jnp.int32(0)
        for b in range(QB_DEV):
            block = home * QB_DEV + b

            def one_page(j, row, block=block):
                at = block * MOST + j
                here = pl.multiple_of(page_ref[at] * page_len, page_len)
                there = pl.multiple_of(row, GRANULE)
                buf[slot, pl.ds(there, page_len), 0:head_size] = k_ref[pl.ds(here, page_len), :]
                buf[slot, pl.ds(there, page_len), head_size : 2 * head_size] = v_ref[pl.ds(here, page_len), :]
                return row + rows_ref[at]

            row = lax.fori_loop(from_ref[block], cnt_ref[block], one_page, row)
        copy_of(home, slot).start()
        return carry

    lax.fori_loop(0, homes, one_home, 0)
    copy_of(homes - 2, 0).wait()
    copy_of(homes - 1, 1).wait()


def pack(plan, key_rows, value_rows, g, homes, height, page_len, head_size):
    tokens = key_rows.shape[0]
    return pl.pallas_call(
        functools.partial(pack_kernel, page_len=page_len),
        grid_spec=pltpu.PrefetchScalarGridSpec(
            num_scalar_prefetch=4,
            grid=(1,),
            in_specs=[
                pl.BlockSpec((tokens, head_size), lambda i, *_: (0, g)),
                pl.BlockSpec((tokens, head_size), lambda i, *_: (0, g)),
            ],
            out_specs=pl.BlockSpec(memory_space=pl.ANY),
            scratch_shapes=[
                pltpu.VMEM((2, height + page_len, 2 * head_size), jnp.bfloat16),
                pltpu.SemaphoreType.DMA((2,)),
            ],
        ),
        out_shape=jax.ShapeDtypeStruct((homes, height, 2 * head_size), jnp.bfloat16),
        compiler_params=pltpu.CompilerParams(vmem_limit_bytes=24 << 20),
        cost_estimate=pl.CostEstimate(
            flops=0, transcendentals=0, bytes_accessed=homes * height * 4 * head_size + tokens * 4 * head_size
        ),
    )(*plan, key_rows, value_rows)


def attend_kernel(
    cnt_ref, first_ref, height_ref, rows_ref, live_ref, kscale_ref, vscale_ref,
    qt_ref, recv_ref, out_ref,
    kv, kcol, vcol, bias, acc, top, total, sems, *, page_len,
):
    sources = recv_ref.shape[0]
    head_size, width = qt_ref.shape

    def copy_of(s, at):
        n = pl.multiple_of(height_ref[s], GRANULE)
        start = pl.multiple_of(first_ref[s], GRANULE)
        at = pl.multiple_of(at, GRANULE)
        return pltpu.make_async_copy(
            recv_ref.at[s, pl.ds(start, n), :], kv.at[pl.ds(at, n), :], sems.at[s]
        )

    def start_one(s, at):
        @pl.when(height_ref[s] > 0)
        def _():
            copy_of(s, at).start()

        return at + height_ref[s]

    def wait_one(s, at):
        @pl.when(height_ref[s] > 0)
        def _():
            copy_of(s, at).wait()

        return at + height_ref[s]

    used = lax.fori_loop(0, sources, start_one, jnp.int32(0))
    token = lax.broadcasted_iota(jnp.int32, (page_len, 128), 0)

    def columns_of(s, at):
        def one_page(j, at):
            e = s * MOST + j
            here = pl.ds(pl.multiple_of(at, GRANULE), page_len)
            kcol[here, :] = jnp.full((page_len, 128), kscale_ref[e], jnp.float32)
            vcol[here, :] = jnp.full((page_len, 128), vscale_ref[e], jnp.float32)
            bias[here, :] = jnp.where(token < live_ref[e], 0.0, masked_score)
            return at + rows_ref[e]

        return lax.fori_loop(0, cnt_ref[s], one_page, at)

    lax.fori_loop(0, sources, columns_of, jnp.int32(0))
    rest = pl.ds(pl.multiple_of(used, GRANULE), CHUNK)
    kcol[rest, :] = jnp.zeros((CHUNK, 128), jnp.float32)
    vcol[rest, :] = jnp.zeros((CHUNK, 128), jnp.float32)
    bias[rest, :] = jnp.full((CHUNK, 128), masked_score, jnp.float32)
    kv[rest, :] = jnp.zeros((CHUNK, 2 * head_size), jnp.bfloat16)
    acc[...] = jnp.zeros_like(acc)
    total[...] = jnp.zeros_like(total)
    top[...] = jnp.full_like(top, lowest)
    lax.fori_loop(0, sources, wait_one, jnp.int32(0))

    def chunk(c, carry):
        here = pl.ds(pl.multiple_of(c * CHUNK, CHUNK), CHUNK)
        keys = kv[here, 0:head_size]
        values = kv[here, head_size : 2 * head_size].T
        for i in range(width // QTILE):
            cols = pl.ds(i * QTILE, QTILE)
            score = jnp.dot(keys, qt_ref[:, cols], preferred_element_type=jnp.float32)
            kc, bc, vc = kcol[here, :], bias[here, :], vcol[here, :]
            wide = lambda x: jnp.concatenate([x] * (QTILE // 128), axis=1)
            score = score * wide(kc) + wide(bc)
            old = top[0:1, cols]
            new = jnp.maximum(old, jnp.max(score, axis=0, keepdims=True))
            weight = jnp.exp2(score - new)
            fade = jnp.exp2(old - new)
            total[0:1, cols] = total[0:1, cols] * fade + jnp.sum(weight, axis=0, keepdims=True)
            scaled = (weight * wide(vc)).astype(jnp.bfloat16)
            acc[:, cols] = acc[:, cols] * fade + jnp.dot(values, scaled, preferred_element_type=jnp.float32)
            top[0:1, cols] = new
        return carry

    lax.fori_loop(0, (used + CHUNK - 1) // CHUNK, chunk, 0)
    for h in range(width // QBLOCK):
        cols = slice(h * QBLOCK, (h + 1) * QBLOCK)
        out_ref[:, h * head_size : (h + 1) * head_size] = (acc[:, cols] / total[0:1, cols]).T.astype(jnp.bfloat16)


def attend(plan, qt, received, page_len, most_rows):
    head_size, width = qt.shape
    sources = received.shape[0]
    rows_held = most_rows + CHUNK + page_len
    out_width = width // QBLOCK * head_size
    return pl.pallas_call(
        functools.partial(attend_kernel, page_len=page_len),
        grid_spec=pltpu.PrefetchScalarGridSpec(
            num_scalar_prefetch=7,
            grid=(1,),
            in_specs=[
                pl.BlockSpec((head_size, width), lambda i, *_: (0, 0)),
                pl.BlockSpec(memory_space=pl.ANY),
            ],
            out_specs=pl.BlockSpec((QBLOCK, out_width), lambda i, *_: (0, 0)),
            scratch_shapes=[
                pltpu.VMEM((rows_held, 2 * head_size), jnp.bfloat16),
                pltpu.VMEM((rows_held, 128), jnp.float32),
                pltpu.VMEM((rows_held, 128), jnp.float32),
                pltpu.VMEM((rows_held, 128), jnp.float32),
                pltpu.VMEM((head_size, width), jnp.float32),
                pltpu.VMEM((8, width), jnp.float32),
                pltpu.VMEM((8, width), jnp.float32),
                pltpu.SemaphoreType.DMA((sources,)),
            ],
        ),
        out_shape=jax.ShapeDtypeStruct((QBLOCK, out_width), jnp.bfloat16),
        compiler_params=pltpu.CompilerParams(vmem_limit_bytes=40 << 20),
        cost_estimate=pl.CostEstimate(
            flops=4 * width * most_rows * head_size,
            transcendentals=width * most_rows,
            bytes_accessed=most_rows * 4 * head_size + width * head_size * 4,
        ),
    )(*plan, qt, received)


def section(
    hidden, norm_gain, w_query, query_gain, w_output, key_rows, value_rows, send_plan, plans, *, height, page_len, listed
):
    model_width = hidden.shape[1]
    head_size = query_gain.shape[0]
    kv_local = len(plans)
    group_size = w_query.shape[1] // head_size // kv_local
    homes = lax.axis_size("cache")
    received = []
    for g in range(kv_local):
        out = pack(send_plan, key_rows, value_rows, g, homes, height, page_len, head_size)
        if g > 0:
            out, received[-1] = lax.optimization_barrier((out, received[-1]))
        received.append(lax.all_to_all(out, "cache", split_axis=0, concat_axis=0, tiled=True))

    inputs = hidden.astype(jnp.float32)
    inverse = lax.rsqrt(jnp.mean(inputs * inputs, axis=-1, keepdims=True) + tiny_eps)
    normed = (inputs * inverse * norm_gain).astype(jnp.bfloat16)
    projected = jnp.dot(normed, w_query, preferred_element_type=jnp.float32)
    projected = projected.reshape(QB_DEV, QBLOCK, kv_local, group_size, head_size)
    head_inverse = lax.rsqrt(jnp.mean(projected * projected, axis=-1, keepdims=True) + tiny_eps)
    queries = (projected * head_inverse * query_gain / math.sqrt(head_size)).astype(jnp.bfloat16)
    queries = jnp.transpose(queries, (0, 2, 4, 3, 1)).reshape(QB_DEV, kv_local, head_size, group_size * QBLOCK)

    span = group_size * head_size
    heads_index = lax.axis_index("heads")
    half_width = model_width // lax.axis_size("heads")
    devices = lax.axis_size("sections")
    partial, away, moved = [None] * QB_DEV, [None] * QB_DEV, []
    for g in range(kv_local):
        for b in range(QB_DEV):
            asking = queries[b, g]
            if g == kv_local - 1 and b > 0:
                asking, away[b - 1] = lax.optimization_barrier((asking, away[b - 1]))
            attended = attend(plans[g][b], asking, received[g], page_len, listed * page_len)
            term = jnp.dot(attended, w_output[g * span : (g + 1) * span], preferred_element_type=jnp.float32)
            partial[b] = term if g == 0 else partial[b] + term
            other = lax.dynamic_slice_in_dim(partial[b], (1 - heads_index) * half_width, half_width, 1)
            away[b] = other.astype(jnp.bfloat16)
    result = None
    for b in range(QB_DEV):
        came = lax.ppermute(away[b], "heads", [(0, 1), (1, 0)])
        if result is not None:
            came, _ = lax.optimization_barrier((came, result))
        kept = lax.dynamic_slice_in_dim(partial[b], heads_index * half_width, half_width, 1)
        residual = lax.dynamic_slice(inputs, (b * QBLOCK, heads_index * half_width), (QBLOCK, half_width))
        result = (kept + came.astype(jnp.float32) + residual).astype(jnp.bfloat16)
        moved.append(lax.ppermute(result, "sections", [((i - 1) % devices, i) for i in range(devices)]))
    return jnp.concatenate(moved, axis=0)


def body(
    hidden,
    norm_gain,
    w_query,
    query_gain,
    w_output,
    key_cache,
    value_cache,
    key_scale,
    value_scale,
    page_table,
    page_tokens,
    page_list,
    list_len,
):
    kv_local = key_scale.shape[2]
    pages_dev, page_len = key_cache.shape[1:3]
    listed = page_list.shape[2]
    shard_count = lax.axis_size("cache")
    own_shard = lax.axis_index("cache")

    entry = lookup(page_list[0], page_table * 128 + page_tokens)
    slots, counts = entry // 128, entry % 128
    used = jnp.arange(listed, dtype=jnp.int32) < list_len[0][:, None]
    rows = (counts + GRANULE - 1) // GRANULE * GRANULE
    homes = shard_count
    twin_slots = jnp.where(used, slots, -1).reshape(homes, QB_DEV, listed)[:, ::-1].reshape(-1, listed)
    both = jnp.any(slots[:, :, None] == twin_slots[:, None, :], axis=-1)
    second = (jnp.arange(homes * QB_DEV) % QB_DEV == 1)[:, None]
    shard, place = slots // pages_dev, slots % pages_dev
    order = jnp.where(used, place + jnp.where(both == second, 0, pages_dev), -1)
    earlier = (
        (shard[:, :, None] == shard[:, None, :])
        & used[:, :, None]
        & (order[:, :, None] < order[:, None, :])
    )
    rank = jnp.sum(jnp.where(earlier, 1, 0), axis=1)
    once = used & ~(both & second)
    sources = jnp.arange(shard_count, dtype=jnp.int32)
    at_source = shard[:, None, :] == sources[:, None]
    asked = jnp.sum(jnp.where(at_source & once[:, None, :], rows[:, None, :], 0), axis=-1)
    need = jnp.max(asked.reshape(homes, QB_DEV, shard_count).sum(axis=1))
    wanted = jnp.arange(MOST, dtype=jnp.int32)

    mine = (shard == own_shard) & used
    picks = mine[:, None, :] & (rank[:, None, :] == wanted[:, None])
    send_plan = (
        jnp.sum(jnp.where(mine & ~once, 1, 0), axis=-1),
        jnp.sum(jnp.where(mine, 1, 0), axis=-1),
        pick(picks, rows).reshape(-1),
        pick(picks, place).reshape(-1),
    )

    both_scales = jnp.concatenate([key_scale[0], value_scale[0]], axis=1)
    told = jnp.concatenate([both_scales, jnp.full((1, 2 * kv_local), need.astype(jnp.float32))], axis=0)
    told = lax.all_gather(told, ("sections", "cache"), axis=0)
    agreed = jnp.max(told[:, pages_dev, 0]).astype(jnp.int32)
    told = told.reshape(-1, shard_count, pages_dev + 1, 2 * kv_local)
    scales = lax.dynamic_index_in_dim(told, lax.axis_index("sections"), 0, keepdims=False)
    scales = scales[:, :pages_dev].reshape(-1, 2 * kv_local)

    first_block = own_shard * QB_DEV

    def own(x):
        return lax.dynamic_slice_in_dim(x, first_block, QB_DEV, 0)

    own_slots, own_counts, own_rows, own_both = own(slots), own(counts), own(rows), own(both)
    theirs = own(at_source) & own(used)[:, None, :]
    own_picks = theirs[:, :, None, :] & (own(rank)[:, None, None, :] == wanted[:, None])
    got_cnt = jnp.sum(jnp.where(theirs, 1, 0), axis=-1)
    got_height = jnp.sum(jnp.where(theirs, own_rows[:, None, :], 0), axis=-1)
    alone = jnp.sum(jnp.where(theirs & ~own_both[:, None, :], own_rows[:, None, :], 0), axis=-1)
    got_first = jnp.stack([jnp.zeros_like(alone[0]), alone[0]])
    got_rows = pick(own_picks, own_rows[:, None, :]).reshape(QB_DEV, -1)
    got_live = pick(own_picks, own_counts[:, None, :]).reshape(QB_DEV, -1)
    places = jnp.arange(scales.shape[0], dtype=jnp.int32)
    at_place = own_slots[..., None] == places
    got_scales = [
        pick(own_picks, jnp.sum(jnp.where(at_place, scales[:, k], 0.0), axis=-1)[:, None, :]).reshape(QB_DEV, -1)
        for k in range(2 * kv_local)
    ]
    plans = [
        [
            (
                got_cnt[b],
                got_first[b],
                got_height[b],
                got_rows[b],
                got_live[b],
                got_scales[g][b] * math.log2(math.e),
                got_scales[kv_local + g][b],
            )
            for b in range(QB_DEV)
        ]
        for g in range(kv_local)
    ]
    key_rows = key_cache[0].reshape(pages_dev * page_len, -1)
    value_rows = value_cache[0].reshape(pages_dev * page_len, -1)
    operands = (
        hidden[0], norm_gain[0], w_query[0], query_gain[0], w_output[0], key_rows, value_rows, send_plan, plans,
    )
    heights = tuple(h for h in HEIGHTS if h < QB_DEV * MOST * page_len) + (QB_DEV * MOST * page_len,)
    branch = jnp.sum(jnp.where(agreed > jnp.array(heights[:-1], jnp.int32), 1, 0))
    moved = lax.switch(
        branch,
        [functools.partial(section, height=h, page_len=page_len, listed=listed) for h in heights],
        *operands,
    )
    return moved[None]


def solution(mesh):
    return jax.shard_map(
        body,
        mesh=mesh,
        in_specs=(
            P("sections", "cache", None),
            P("sections", None),
            P("sections", None, "heads"),
            P("sections", None),
            P("sections", "heads", None),
            P("sections", "cache", None, "heads"),
            P("sections", "cache", None, "heads"),
            P("sections", "cache", "heads"),
            P("sections", "cache", "heads"),
            P(),
            P(),
            P("sections", None, None),
            P("sections", None),
        ),
        out_specs=P("sections", "cache", "heads"),
        check_vma=False,
    )
```

```python
import functools
import math

import jax
import jax.numpy as jnp
from jax import lax
from jax.experimental import pallas as pl
from jax.experimental.pallas import tpu as pltpu
from jax.sharding import PartitionSpec as P

QBLOCK = 128
QB_DEV = 2
MOST = 8
GRANULE = 16
HEIGHTS = (448, 512, 544, 576, 608, 672, 800)
CHUNK = 512
QTILE = 256

tiny_eps = 1e-06
masked_score = -1e30
lowest = -1e38


def lookup(entries, table):
    places = jnp.arange(table.shape[0], dtype=jnp.int32)
    return jnp.sum(jnp.where(entries[..., None] == places, table, 0), axis=-1)


def pick(picks, values):
    return jnp.sum(jnp.where(picks, values[..., None, :], 0), axis=-1)


def pack_kernel(from_ref, cnt_ref, rows_ref, page_ref, k_ref, v_ref, out_ref, buf, sems, *, page_len):
    homes, height, _ = out_ref.shape
    head_size = k_ref.shape[1]

    def copy_of(home, slot):
        return pltpu.make_async_copy(buf.at[slot, pl.ds(0, height), :], out_ref.at[home], sems.at[slot])

    def one_home(home, carry):
        slot = lax.rem(home, 2)

        @pl.when(home >= 2)
        def _():
            copy_of(home - 2, slot).wait()

        row = jnp.int32(0)
        for b in range(QB_DEV):
            block = home * QB_DEV + b

            def one_page(j, row, block=block):
                at = block * MOST + j
                here = pl.multiple_of(page_ref[at] * page_len, page_len)
                there = pl.multiple_of(row, GRANULE)
                buf[slot, pl.ds(there, page_len), 0:head_size] = k_ref[pl.ds(here, page_len), :]
                buf[slot, pl.ds(there, page_len), head_size : 2 * head_size] = v_ref[pl.ds(here, page_len), :]
                return row + rows_ref[at]

            row = lax.fori_loop(from_ref[block], cnt_ref[block], one_page, row)
        copy_of(home, slot).start()
        return carry

    lax.fori_loop(0, homes, one_home, 0)
    copy_of(homes - 2, 0).wait()
    copy_of(homes - 1, 1).wait()


def pack(plan, key_rows, value_rows, g, homes, height, page_len, head_size):
    tokens = key_rows.shape[0]
    return pl.pallas_call(
        functools.partial(pack_kernel, page_len=page_len),
        grid_spec=pltpu.PrefetchScalarGridSpec(
            num_scalar_prefetch=4,
            grid=(1,),
            in_specs=[
                pl.BlockSpec((tokens, head_size), lambda i, *_: (0, g)),
                pl.BlockSpec((tokens, head_size), lambda i, *_: (0, g)),
            ],
            out_specs=pl.BlockSpec(memory_space=pltpu.HBM),
            scratch_shapes=[
                pltpu.VMEM((2, height + page_len, 2 * head_size), jnp.bfloat16),
                pltpu.SemaphoreType.DMA((2,)),
            ],
        ),
        out_shape=jax.ShapeDtypeStruct((homes, height, 2 * head_size), jnp.bfloat16),
        compiler_params=pltpu.CompilerParams(vmem_limit_bytes=60 << 20),
        cost_estimate=pl.CostEstimate(
            flops=0, transcendentals=0, bytes_accessed=homes * height * 4 * head_size + tokens * 4 * head_size
        ),
    )(*plan, key_rows, value_rows)


def attend_kernel(
    cnt_ref, first_ref, height_ref, rows_ref, live_ref, kscale_ref, vscale_ref,
    qt_ref, recv_ref, out_ref,
    kv, kcol, vcol, bias, acc, top, total, sems, *, page_len,
):
    sources = recv_ref.shape[0]
    head_size, width = qt_ref.shape

    def copy_of(s, at):
        n = pl.multiple_of(height_ref[s], GRANULE)
        start = pl.multiple_of(first_ref[s], GRANULE)
        at = pl.multiple_of(at, GRANULE)
        return pltpu.make_async_copy(
            recv_ref.at[s, pl.ds(start, n), :], kv.at[pl.ds(at, n), :], sems.at[s]
        )

    def start_one(s, at):
        @pl.when(height_ref[s] > 0)
        def _():
            copy_of(s, at).start()

        return at + height_ref[s]

    def wait_one(s, at):
        @pl.when(height_ref[s] > 0)
        def _():
            copy_of(s, at).wait()

        return at + height_ref[s]

    used = lax.fori_loop(0, sources, start_one, jnp.int32(0))
    token = lax.broadcasted_iota(jnp.int32, (page_len, 128), 0)

    def columns_of(s, at):
        def one_page(j, at):
            e = s * MOST + j
            here = pl.ds(pl.multiple_of(at, GRANULE), page_len)
            kcol[here, :] = jnp.full((page_len, 128), kscale_ref[e], jnp.float32)
            vcol[here, :] = jnp.full((page_len, 128), vscale_ref[e], jnp.float32)
            bias[here, :] = jnp.where(token < live_ref[e], 0.0, masked_score)
            return at + rows_ref[e]

        return lax.fori_loop(0, cnt_ref[s], one_page, at)

    lax.fori_loop(0, sources, columns_of, jnp.int32(0))
    rest = pl.ds(pl.multiple_of(used, GRANULE), CHUNK)
    kcol[rest, :] = jnp.zeros((CHUNK, 128), jnp.float32)
    vcol[rest, :] = jnp.zeros((CHUNK, 128), jnp.float32)
    bias[rest, :] = jnp.full((CHUNK, 128), masked_score, jnp.float32)
    kv[rest, :] = jnp.zeros((CHUNK, 2 * head_size), jnp.bfloat16)
    acc[...] = jnp.zeros_like(acc)
    total[...] = jnp.zeros_like(total)
    top[...] = jnp.full_like(top, lowest)
    lax.fori_loop(0, sources, wait_one, jnp.int32(0))

    def chunk(c, carry):
        here = pl.ds(pl.multiple_of(c * CHUNK, CHUNK), CHUNK)
        keys = kv[here, 0:head_size]
        values = kv[here, head_size : 2 * head_size].T
        for i in range(width // QTILE):
            cols = pl.ds(i * QTILE, QTILE)
            score = jnp.dot(keys, qt_ref[:, cols], preferred_element_type=jnp.float32)
            kc, bc, vc = kcol[here, :], bias[here, :], vcol[here, :]
            wide = lambda x: jnp.concatenate([x] * (QTILE // 128), axis=1)
            score = score * wide(kc) + wide(bc)
            old = top[0:1, cols]
            new = jnp.maximum(old, jnp.max(score, axis=0, keepdims=True))
            weight = jnp.exp2(score - new)
            fade = jnp.exp2(old - new)
            total[0:1, cols] = total[0:1, cols] * fade + jnp.sum(weight, axis=0, keepdims=True)
            scaled = (weight * wide(vc)).astype(jnp.bfloat16)
            acc[:, cols] = acc[:, cols] * fade + jnp.dot(values, scaled, preferred_element_type=jnp.float32)
            top[0:1, cols] = new
        return carry

    lax.fori_loop(0, (used + CHUNK - 1) // CHUNK, chunk, 0)
    for h in range(width // QBLOCK):
        cols = slice(h * QBLOCK, (h + 1) * QBLOCK)
        out_ref[:, h * head_size : (h + 1) * head_size] = (acc[:, cols] / total[0:1, cols]).T.astype(jnp.bfloat16)


def attend(plan, qt, received, page_len, most_rows):
    head_size, width = qt.shape
    sources = received.shape[0]
    rows_held = most_rows + CHUNK + page_len
    out_width = width // QBLOCK * head_size
    return pl.pallas_call(
        functools.partial(attend_kernel, page_len=page_len),
        grid_spec=pltpu.PrefetchScalarGridSpec(
            num_scalar_prefetch=7,
            grid=(1,),
            in_specs=[
                pl.BlockSpec((head_size, width), lambda i, *_: (0, 0)),
                pl.BlockSpec(memory_space=pltpu.HBM),
            ],
            out_specs=pl.BlockSpec((QBLOCK, out_width), lambda i, *_: (0, 0)),
            scratch_shapes=[
                pltpu.VMEM((rows_held, 2 * head_size), jnp.bfloat16),
                pltpu.VMEM((rows_held, 128), jnp.float32),
                pltpu.VMEM((rows_held, 128), jnp.float32),
                pltpu.VMEM((rows_held, 128), jnp.float32),
                pltpu.VMEM((head_size, width), jnp.float32),
                pltpu.VMEM((8, width), jnp.float32),
                pltpu.VMEM((8, width), jnp.float32),
                pltpu.SemaphoreType.DMA((sources,)),
            ],
        ),
        out_shape=jax.ShapeDtypeStruct((QBLOCK, out_width), jnp.bfloat16),
        compiler_params=pltpu.CompilerParams(vmem_limit_bytes=40 << 20),
        cost_estimate=pl.CostEstimate(
            flops=4 * width * most_rows * head_size,
            transcendentals=width * most_rows,
            bytes_accessed=most_rows * 4 * head_size + width * head_size * 4,
        ),
    )(*plan, qt, received)


def section(
    hidden, norm_gain, w_query, query_gain, w_output, key_rows, value_rows, send_plan, plans, *, height, page_len, listed
):
    model_width = hidden.shape[1]
    head_size = query_gain.shape[0]
    kv_local = len(plans)
    group_size = w_query.shape[1] // head_size // kv_local
    homes = lax.axis_size("cache")
    received = []
    for g in range(kv_local):
        out = pack(send_plan, key_rows, value_rows, g, homes, height, page_len, head_size)
        if g > 0:
            out, received[-1] = lax.optimization_barrier((out, received[-1]))
        received.append(lax.all_to_all(out, "cache", split_axis=0, concat_axis=0, tiled=True))

    inputs = hidden.astype(jnp.float32)
    inverse = lax.rsqrt(jnp.mean(inputs * inputs, axis=-1, keepdims=True) + tiny_eps)
    normed = (inputs * inverse * norm_gain).astype(jnp.bfloat16)
    projected = jnp.dot(normed, w_query, preferred_element_type=jnp.float32)
    projected = projected.reshape(QB_DEV, QBLOCK, kv_local, group_size, head_size)
    head_inverse = lax.rsqrt(jnp.mean(projected * projected, axis=-1, keepdims=True) + tiny_eps)
    queries = (projected * head_inverse * query_gain / math.sqrt(head_size)).astype(jnp.bfloat16)
    queries = jnp.transpose(queries, (0, 2, 4, 3, 1)).reshape(QB_DEV, kv_local, head_size, group_size * QBLOCK)

    span = group_size * head_size
    heads_index = lax.axis_index("heads")
    half_width = model_width // lax.axis_size("heads")
    devices = lax.axis_size("sections")
    partial, came, moved = [None] * QB_DEV, [None] * QB_DEV, []
    for g in range(kv_local):
        for b in range(QB_DEV):
            attended = attend(plans[g][b], queries[b, g], received[g], page_len, listed * page_len)
            if g == kv_local - 1 and b > 0:
                attended, came[b - 1] = lax.optimization_barrier((attended, came[b - 1]))
            term = jnp.dot(attended, w_output[g * span : (g + 1) * span], preferred_element_type=jnp.float32)
            partial[b] = term if g == 0 else partial[b] + term
            if g == kv_local - 1:
                away = lax.dynamic_slice_in_dim(partial[b], (1 - heads_index) * half_width, half_width, 1)
                came[b] = lax.ppermute(away.astype(jnp.bfloat16), "heads", [(0, 1), (1, 0)])
    result = None
    for b in range(QB_DEV):
        if result is not None:
            came[b], _ = lax.optimization_barrier((came[b], result))
        kept = lax.dynamic_slice_in_dim(partial[b], heads_index * half_width, half_width, 1)
        residual = lax.dynamic_slice(inputs, (b * QBLOCK, heads_index * half_width), (QBLOCK, half_width))
        result = (kept + came[b].astype(jnp.float32) + residual).astype(jnp.bfloat16)
        moved.append(lax.ppermute(result, "sections", [((i - 1) % devices, i) for i in range(devices)]))
    return jnp.concatenate(moved, axis=0)


def body(
    hidden,
    norm_gain,
    w_query,
    query_gain,
    w_output,
    key_cache,
    value_cache,
    key_scale,
    value_scale,
    page_table,
    page_tokens,
    page_list,
    list_len,
):
    kv_local = key_scale.shape[2]
    pages_dev, page_len = key_cache.shape[1:3]
    listed = page_list.shape[2]
    shard_count = lax.axis_size("cache")
    own_shard = lax.axis_index("cache")

    told = jnp.concatenate([key_scale[0], value_scale[0]], axis=1).reshape(1, 1, -1)
    told = jnp.broadcast_to(told, (shard_count, *told.shape[1:]))
    told = lax.all_to_all(told, "cache", split_axis=0, concat_axis=0, tiled=True)
    scales = told.reshape(shard_count * pages_dev, 2 * kv_local)

    entry = lookup(page_list[0], page_table * 128 + page_tokens)
    slots, counts = entry // 128, entry % 128
    used = jnp.arange(listed, dtype=jnp.int32) < list_len[0][:, None]
    rows = (counts + GRANULE - 1) // GRANULE * GRANULE
    homes = shard_count
    twin_slots = jnp.where(used, slots, -1).reshape(homes, QB_DEV, listed)[:, ::-1].reshape(-1, listed)
    both = jnp.any(slots[:, :, None] == twin_slots[:, None, :], axis=-1)
    second = (jnp.arange(homes * QB_DEV) % QB_DEV == 1)[:, None]
    shard, place = slots // pages_dev, slots % pages_dev
    order = jnp.where(used, place + jnp.where(both == second, 0, pages_dev), -1)
    earlier = (
        (shard[:, :, None] == shard[:, None, :])
        & used[:, :, None]
        & (order[:, :, None] < order[:, None, :])
    )
    rank = jnp.sum(jnp.where(earlier, 1, 0), axis=1)
    once = used & ~(both & second)
    sources = jnp.arange(shard_count, dtype=jnp.int32)
    at_source = shard[:, None, :] == sources[:, None]
    asked = jnp.sum(jnp.where(at_source & once[:, None, :], rows[:, None, :], 0), axis=-1)
    need = jnp.max(asked.reshape(homes, QB_DEV, shard_count).sum(axis=1))
    wanted = jnp.arange(MOST, dtype=jnp.int32)

    mine = (shard == own_shard) & used
    picks = mine[:, None, :] & (rank[:, None, :] == wanted[:, None])
    send_plan = (
        jnp.sum(jnp.where(mine & ~once, 1, 0), axis=-1),
        jnp.sum(jnp.where(mine, 1, 0), axis=-1),
        pick(picks, rows).reshape(-1),
        pick(picks, place).reshape(-1),
    )

    devices = lax.axis_size("sections")
    agreed = need.astype(jnp.int32)[None]
    for step in range(1, devices):
        route = [(i, (i + step) % devices) for i in range(devices)]
        agreed = jnp.maximum(agreed, lax.ppermute(need.astype(jnp.int32)[None], "sections", route))
    agreed = agreed[0]

    first_block = own_shard * QB_DEV

    def own(x):
        return lax.dynamic_slice_in_dim(x, first_block, QB_DEV, 0)

    own_slots, own_counts, own_rows, own_both = own(slots), own(counts), own(rows), own(both)
    theirs = own(at_source) & own(used)[:, None, :]
    own_picks = theirs[:, :, None, :] & (own(rank)[:, None, None, :] == wanted[:, None])
    got_cnt = jnp.sum(jnp.where(theirs, 1, 0), axis=-1)
    got_height = jnp.sum(jnp.where(theirs, own_rows[:, None, :], 0), axis=-1)
    alone = jnp.sum(jnp.where(theirs & ~own_both[:, None, :], own_rows[:, None, :], 0), axis=-1)
    got_first = jnp.stack([jnp.zeros_like(alone[0]), alone[0]])
    got_rows = pick(own_picks, own_rows[:, None, :]).reshape(QB_DEV, -1)
    got_live = pick(own_picks, own_counts[:, None, :]).reshape(QB_DEV, -1)
    places = jnp.arange(scales.shape[0], dtype=jnp.int32)
    at_place = own_slots[..., None] == places
    got_scales = [
        pick(own_picks, jnp.sum(jnp.where(at_place, scales[:, k], 0.0), axis=-1)[:, None, :]).reshape(QB_DEV, -1)
        for k in range(2 * kv_local)
    ]
    plans = [
        [
            (
                got_cnt[b],
                got_first[b],
                got_height[b],
                got_rows[b],
                got_live[b],
                got_scales[g][b] * math.log2(math.e),
                got_scales[kv_local + g][b],
            )
            for b in range(QB_DEV)
        ]
        for g in range(kv_local)
    ]
    key_rows = key_cache[0].reshape(pages_dev * page_len, -1)
    value_rows = value_cache[0].reshape(pages_dev * page_len, -1)
    operands = (
        hidden[0], norm_gain[0], w_query[0], query_gain[0], w_output[0], key_rows, value_rows, send_plan, plans,
    )
    heights = tuple(h for h in HEIGHTS if h < QB_DEV * MOST * page_len) + (QB_DEV * MOST * page_len,)
    branch = jnp.sum(jnp.where(agreed > jnp.array(heights[:-1], jnp.int32), 1, 0))
    moved = lax.switch(
        branch,
        [functools.partial(section, height=h, page_len=page_len, listed=listed) for h in heights],
        *operands,
    )
    return moved[None]


def solution(mesh):
    return jax.shard_map(
        body,
        mesh=mesh,
        in_specs=(
            P("sections", "cache", None),
            P("sections", None),
            P("sections", None, "heads"),
            P("sections", None),
            P("sections", "heads", None),
            P("sections", "cache", None, "heads"),
            P("sections", "cache", None, "heads"),
            P("sections", "cache", "heads"),
            P("sections", "cache", "heads"),
            P(),
            P(),
            P("sections", None, None),
            P("sections", None),
        ),
        out_specs=P("sections", "cache", "heads"),
        check_vma=False,
    )
```

```python
import functools
import math

import jax
import jax.numpy as jnp
from jax import lax
from jax.experimental import pallas as pl
from jax.experimental.pallas import tpu as pltpu
from jax.sharding import PartitionSpec as P

QBLOCK = 128
QB_DEV = 2
MOST = 8
GRANULE = 16
HEIGHTS = (448, 512, 544, 576, 608, 672, 800)
CHUNK = 512
QTILE = 256

tiny_eps = 1e-06
masked_score = -1e30
lowest = -1e38


def lookup(entries, table):
    places = jnp.arange(table.shape[0], dtype=jnp.int32)
    return jnp.sum(jnp.where(entries[..., None] == places, table, 0), axis=-1)


def pick(picks, values):
    return jnp.sum(jnp.where(picks, values[..., None, :], 0), axis=-1)


def pack_kernel(rows_ref, page_ref, *refs, page_len, height):
    *head_refs, k_ref, v_ref, out_ref, buf, sems = refs
    homes, sent, _ = out_ref.shape
    head_size = k_ref.shape[1]
    for slot in range(2):
        for head_ref in head_refs:
            buf[slot, pl.ds(page_len + height, GRANULE), :] = head_ref[...]

    def copies_of(home, slot):
        copies = [(0, height)] + [(page_len + height, GRANULE)] * len(head_refs)
        starts = (0, height)
        return [
            pltpu.make_async_copy(
                buf.at[slot, pl.ds(here, n), :], out_ref.at[home, pl.ds(there, n), :], sems.at[slot, i]
            )
            for i, ((here, n), there) in enumerate(zip(copies, starts))
        ]

    def one_home(home, carry):
        slot = lax.rem(home, 2)

        @pl.when(home >= 2)
        def _():
            for copy in copies_of(home - 2, slot):
                copy.wait()

        row = jnp.int32(0)
        for j in range(QB_DEV * MOST):
            at = home * (QB_DEV * MOST) + j
            here = pl.multiple_of(page_ref[at] * page_len, page_len)
            there = pl.multiple_of(row, GRANULE)
            buf[slot, pl.ds(there, page_len), 0:head_size] = k_ref[pl.ds(here, page_len), :]
            buf[slot, pl.ds(there, page_len), head_size : 2 * head_size] = v_ref[pl.ds(here, page_len), :]
            row = row + rows_ref[at]
        for copy in copies_of(home, slot):
            copy.start()
        return carry

    lax.fori_loop(0, homes, one_home, 0)
    for home in (homes - 2, homes - 1):
        for copy in copies_of(home, home % 2):
            copy.wait()


def pack(plan, heads, key_rows, value_rows, g, homes, height, page_len, head_size):
    tokens = key_rows.shape[0]
    sent = height + GRANULE * len(heads)
    return pl.pallas_call(
        functools.partial(pack_kernel, page_len=page_len, height=height),
        grid_spec=pltpu.PrefetchScalarGridSpec(
            num_scalar_prefetch=2,
            grid=(1,),
            in_specs=[pl.BlockSpec(h.shape, lambda i, *_: (0, 0)) for h in heads]
            + [
                pl.BlockSpec((tokens, head_size), lambda i, *_: (0, g)),
                pl.BlockSpec((tokens, head_size), lambda i, *_: (0, g)),
            ],
            out_specs=pl.BlockSpec(memory_space=pltpu.HBM),
            scratch_shapes=[
                pltpu.VMEM((2, height + page_len + GRANULE, 2 * head_size), jnp.bfloat16),
                pltpu.SemaphoreType.DMA((2, 2)),
            ],
        ),
        out_shape=jax.ShapeDtypeStruct((homes, sent, 2 * head_size), jnp.bfloat16),
        compiler_params=pltpu.CompilerParams(vmem_limit_bytes=60 << 20),
        cost_estimate=pl.CostEstimate(
            flops=0, transcendentals=0, bytes_accessed=homes * sent * 4 * head_size + tokens * 4 * head_size
        ),
    )(*plan, *heads, key_rows, value_rows)


def attend_kernel(
    cnt_ref, first_ref, height_ref, rows_ref, live_ref, kscale_ref, vscale_ref,
    qt_ref, recv_ref, out_ref,
    kv, kcol, vcol, bias, acc, top, total, sems, *, page_len,
):
    sources = recv_ref.shape[0]
    head_size, width = qt_ref.shape[1:]
    lists = pl.program_id(0) * sources

    def copy_of(s, at):
        n = pl.multiple_of(height_ref[lists + s], GRANULE)
        start = pl.multiple_of(first_ref[lists + s], GRANULE)
        at = pl.multiple_of(at, GRANULE)
        return pltpu.make_async_copy(
            recv_ref.at[s, pl.ds(start, n), :], kv.at[pl.ds(at, n), :], sems.at[s]
        )

    def start_one(s, at):
        @pl.when(height_ref[lists + s] > 0)
        def _():
            copy_of(s, at).start()

        return at + height_ref[lists + s]

    def wait_one(s, at):
        @pl.when(height_ref[lists + s] > 0)
        def _():
            copy_of(s, at).wait()

        return at + height_ref[lists + s]

    used = lax.fori_loop(0, sources, start_one, jnp.int32(0))
    token = lax.broadcasted_iota(jnp.int32, (page_len, 128), 0)

    def columns_of(s, at):
        def one_page(j, at):
            e = (lists + s) * MOST + j
            here = pl.ds(pl.multiple_of(at, GRANULE), page_len)
            kcol[here, :] = jnp.full((page_len, 128), kscale_ref[e], jnp.float32)
            vcol[here, :] = jnp.full((page_len, 128), vscale_ref[e], jnp.float32)
            bias[here, :] = jnp.where(token < live_ref[e], 0.0, masked_score)
            return at + rows_ref[e]

        return lax.fori_loop(0, cnt_ref[lists + s], one_page, at)

    lax.fori_loop(0, sources, columns_of, jnp.int32(0))
    rest = pl.ds(pl.multiple_of(used, GRANULE), CHUNK)
    kcol[rest, :] = jnp.zeros((CHUNK, 128), jnp.float32)
    vcol[rest, :] = jnp.zeros((CHUNK, 128), jnp.float32)
    bias[rest, :] = jnp.full((CHUNK, 128), masked_score, jnp.float32)
    kv[rest, :] = jnp.zeros((CHUNK, 2 * head_size), jnp.bfloat16)
    acc[...] = jnp.zeros_like(acc)
    total[...] = jnp.zeros_like(total)
    top[...] = jnp.full_like(top, lowest)
    lax.fori_loop(0, sources, wait_one, jnp.int32(0))

    def chunk(c, carry):
        here = pl.ds(pl.multiple_of(c * CHUNK, CHUNK), CHUNK)
        keys = kv[here, 0:head_size]
        values = kv[here, head_size : 2 * head_size].T
        for i in range(width // QTILE):
            cols = pl.ds(i * QTILE, QTILE)
            score = jnp.dot(keys, qt_ref[0, :, cols], preferred_element_type=jnp.float32)
            kc, bc, vc = kcol[here, :], bias[here, :], vcol[here, :]
            wide = lambda x: jnp.concatenate([x] * (QTILE // 128), axis=1)
            score = score * wide(kc) + wide(bc)
            old = top[0:1, cols]
            new = jnp.maximum(old, jnp.max(score, axis=0, keepdims=True))
            weight = jnp.exp2(score - new)
            fade = jnp.exp2(old - new)
            total[0:1, cols] = total[0:1, cols] * fade + jnp.sum(weight, axis=0, keepdims=True)
            scaled = (weight * wide(vc)).astype(jnp.bfloat16)
            acc[:, cols] = acc[:, cols] * fade + jnp.dot(values, scaled, preferred_element_type=jnp.float32)
            top[0:1, cols] = new
        return carry

    lax.fori_loop(0, (used + CHUNK - 1) // CHUNK, chunk, 0)
    for h in range(width // QBLOCK):
        cols = slice(h * QBLOCK, (h + 1) * QBLOCK)
        out_ref[:, h * head_size : (h + 1) * head_size] = (acc[:, cols] / total[0:1, cols]).T.astype(jnp.bfloat16)


def attend(plan, qt, received, page_len, most_rows):
    blocks, head_size, width = qt.shape
    sources = received.shape[0]
    rows_held = most_rows + CHUNK + page_len
    out_width = width // QBLOCK * head_size
    return pl.pallas_call(
        functools.partial(attend_kernel, page_len=page_len),
        grid_spec=pltpu.PrefetchScalarGridSpec(
            num_scalar_prefetch=7,
            grid=(blocks,),
            in_specs=[
                pl.BlockSpec((1, head_size, width), lambda b, *_: (b, 0, 0)),
                pl.BlockSpec(memory_space=pltpu.HBM),
            ],
            out_specs=pl.BlockSpec((QBLOCK, out_width), lambda b, *_: (b, 0)),
            scratch_shapes=[
                pltpu.VMEM((rows_held, 2 * head_size), jnp.bfloat16),
                pltpu.VMEM((rows_held, 128), jnp.float32),
                pltpu.VMEM((rows_held, 128), jnp.float32),
                pltpu.VMEM((rows_held, 128), jnp.float32),
                pltpu.VMEM((head_size, width), jnp.float32),
                pltpu.VMEM((8, width), jnp.float32),
                pltpu.VMEM((8, width), jnp.float32),
                pltpu.SemaphoreType.DMA((sources,)),
            ],
        ),
        out_shape=jax.ShapeDtypeStruct((blocks * QBLOCK, out_width), jnp.bfloat16),
        compiler_params=pltpu.CompilerParams(vmem_limit_bytes=40 << 20),
        cost_estimate=pl.CostEstimate(
            flops=4 * blocks * width * most_rows * head_size,
            transcendentals=blocks * width * most_rows,
            bytes_accessed=blocks * (most_rows + width) * 4 * head_size,
        ),
    )(*plan, qt, received)


def in_three(x):
    high = lax.reduce_precision(x, 8, 7)
    middle = lax.reduce_precision(x - high, 8, 7)
    low = x - high - middle
    return jnp.stack([t.astype(jnp.bfloat16) for t in (high, middle, low)])


def gather_attended(
    hidden, norm_gain, w_query, query_gain, key_rows, value_rows, told, send_plan, plan, own_picks, own_slots,
    *, height, page_len
):
    head_size = query_gain.shape[0]
    kv_local = key_rows.shape[1] // head_size
    group_size = w_query.shape[1] // head_size // kv_local
    homes = lax.axis_size("cache")
    listed = own_slots.shape[-1]
    received = []
    for g in range(kv_local):
        heads = (told,) if g == 0 else ()
        out = pack(send_plan, heads, key_rows, value_rows, g, homes, height, page_len, head_size)
        if g > 0:
            out, received[-1] = lax.optimization_barrier((out, received[-1]))
        received.append(lax.all_to_all(out, "cache", split_axis=0, concat_axis=0, tiled=True))

    inputs = hidden.astype(jnp.float32)
    inverse = lax.rsqrt(jnp.mean(inputs * inputs, axis=-1, keepdims=True) + tiny_eps)
    normed = (inputs * inverse * norm_gain).astype(jnp.bfloat16)
    projected = jnp.dot(normed, w_query, preferred_element_type=jnp.float32)
    projected = projected.reshape(QB_DEV, QBLOCK, kv_local, group_size, head_size)
    head_inverse = lax.rsqrt(jnp.mean(projected * projected, axis=-1, keepdims=True) + tiny_eps)
    queries = (projected * head_inverse * query_gain / math.sqrt(head_size)).astype(jnp.bfloat16)
    queries = jnp.transpose(queries, (2, 0, 4, 3, 1)).reshape(kv_local, QB_DEV, head_size, group_size * QBLOCK)

    terms = received[0][:, height : height + 3, :].astype(jnp.float32)
    scales = (terms[:, 0] + terms[:, 1]) + terms[:, 2]
    pages_dev = key_rows.shape[0] // page_len
    scales = scales[:, : 2 * kv_local * pages_dev].reshape(homes, 2 * kv_local, pages_dev)
    scales = jnp.swapaxes(scales, 0, 1).reshape(2 * kv_local, homes * pages_dev)
    at_place = own_slots[..., None] == jnp.arange(homes * pages_dev, dtype=jnp.int32)
    found = [jnp.sum(jnp.where(at_place, scales[k], 0.0), axis=-1) for k in range(2 * kv_local)]
    found = [pick(own_picks, f[:, None, :]).reshape(-1) for f in found]
    attended = []
    for g in range(kv_local):
        scaled = (found[g] * math.log2(math.e), found[kv_local + g])
        attended.append(attend((*plan, *scaled), queries[g], received[g], page_len, listed * page_len))
    return tuple(attended)


def body(
    hidden,
    norm_gain,
    w_query,
    query_gain,
    w_output,
    key_cache,
    value_cache,
    key_scale,
    value_scale,
    page_table,
    page_tokens,
    page_list,
    list_len,
):
    kv_local = key_scale.shape[2]
    pages_dev, page_len = key_cache.shape[1:3]
    listed = page_list.shape[2]
    shard_count = lax.axis_size("cache")
    own_shard = lax.axis_index("cache")

    told = jnp.concatenate([key_scale[0].T, value_scale[0].T], axis=0).reshape(-1)
    told = in_three(told)
    told = jnp.pad(told, ((0, GRANULE - 3), (0, key_cache.shape[3] // kv_local * 2 - told.shape[1])))

    entry = lookup(page_list[0], page_table * 128 + page_tokens)
    slots, counts = entry // 128, entry % 128
    used = jnp.arange(listed, dtype=jnp.int32) < list_len[0][:, None]
    rows = (counts + GRANULE - 1) // GRANULE * GRANULE
    homes = shard_count
    twin_slots = jnp.where(used, slots, -1).reshape(homes, QB_DEV, listed)[:, ::-1].reshape(-1, listed)
    both = jnp.any(slots[:, :, None] == twin_slots[:, None, :], axis=-1)
    second = (jnp.arange(homes * QB_DEV) % QB_DEV == 1)[:, None]
    shard, place = slots // pages_dev, slots % pages_dev
    order = jnp.where(used, place + jnp.where(both == second, 0, pages_dev), -1)
    earlier = (
        (shard[:, :, None] == shard[:, None, :])
        & used[:, :, None]
        & (order[:, :, None] < order[:, None, :])
    )
    rank = jnp.sum(jnp.where(earlier, 1, 0), axis=1)
    once = used & ~(both & second)
    sources = jnp.arange(shard_count, dtype=jnp.int32)
    at_source = shard[:, None, :] == sources[:, None]
    asked = jnp.sum(jnp.where(at_source & once[:, None, :], rows[:, None, :], 0), axis=-1)
    need = jnp.max(asked.reshape(homes, QB_DEV, shard_count).sum(axis=1))
    wanted = jnp.arange(MOST, dtype=jnp.int32)

    mine = (shard == own_shard) & once
    shared = jnp.sum(jnp.where(mine & both, 1, 0), axis=-1).reshape(homes, QB_DEV)[:, :1]
    behind = jnp.concatenate([jnp.zeros_like(shared), shared], axis=1).reshape(-1)
    picks = mine[:, None, :] & ((rank - behind[:, None])[:, None, :] == wanted[:, None])
    send_plan = (pick(picks, rows).reshape(-1), pick(picks, place).reshape(-1))

    devices = lax.axis_size("sections")
    agreed = need.astype(jnp.int32)[None]
    for step in range(1, devices):
        route = [(i, (i + step) % devices) for i in range(devices)]
        agreed = jnp.maximum(agreed, lax.ppermute(need.astype(jnp.int32)[None], "sections", route))
    agreed = agreed[0]

    first_block = own_shard * QB_DEV

    def own(x):
        return lax.dynamic_slice_in_dim(x, first_block, QB_DEV, 0)

    own_slots, own_counts, own_rows, own_both = own(slots), own(counts), own(rows), own(both)
    theirs = own(at_source) & own(used)[:, None, :]
    own_picks = theirs[:, :, None, :] & (own(rank)[:, None, None, :] == wanted[:, None])
    got_cnt = jnp.sum(jnp.where(theirs, 1, 0), axis=-1)
    got_height = jnp.sum(jnp.where(theirs, own_rows[:, None, :], 0), axis=-1)
    alone = jnp.sum(jnp.where(theirs & ~own_both[:, None, :], own_rows[:, None, :], 0), axis=-1)
    got_first = jnp.stack([jnp.zeros_like(alone[0]), alone[0]])
    got_rows = pick(own_picks, own_rows[:, None, :])
    got_live = pick(own_picks, own_counts[:, None, :])
    plan = tuple(x.reshape(-1) for x in (got_cnt, got_first, got_height, got_rows, got_live))
    key_rows = key_cache[0].reshape(pages_dev * page_len, -1)
    value_rows = value_cache[0].reshape(pages_dev * page_len, -1)
    most = QB_DEV * MOST * page_len
    heights = tuple(h for h in HEIGHTS if h < most) + (most,)
    branch = jnp.sum(jnp.where(agreed > jnp.array(heights[:-1], jnp.int32), 1, 0))
    send_plan, told, branch = lax.optimization_barrier((send_plan, told, branch))
    attended = lax.switch(
        branch,
        [functools.partial(gather_attended, height=h, page_len=page_len) for h in heights],
        hidden[0], norm_gain[0], w_query[0], query_gain[0], key_rows, value_rows, told, send_plan, plan,
        own_picks, own_slots,
    )

    span = attended[0].shape[1]
    model_width = hidden.shape[2]
    heads_index = lax.axis_index("heads")
    half_width = model_width // lax.axis_size("heads")
    came, kept = [], []
    for b in range(QB_DEV):
        rows_here = slice(b * QBLOCK, (b + 1) * QBLOCK)
        both_heads = jnp.concatenate([a[rows_here] for a in attended], axis=1)
        if b > 0:
            both_heads, came[b - 1] = lax.optimization_barrier((both_heads, came[b - 1]))
        whole = jnp.dot(both_heads, w_output[0], preferred_element_type=jnp.float32)
        away = lax.dynamic_slice_in_dim(whole, (1 - heads_index) * half_width, half_width, 1)
        came.append(lax.ppermute(away.astype(jnp.bfloat16), "heads", [(0, 1), (1, 0)]))
        kept.append(lax.dynamic_slice_in_dim(whole, heads_index * half_width, half_width, 1))
    moved, result = [], None
    for b in range(QB_DEV):
        if result is not None:
            came[b], _ = lax.optimization_barrier((came[b], result))
        residual = lax.dynamic_slice(
            hidden[0], (b * QBLOCK, heads_index * half_width), (QBLOCK, half_width)
        ).astype(jnp.float32)
        result = (kept[b] + came[b].astype(jnp.float32) + residual).astype(jnp.bfloat16)
        moved.append(lax.ppermute(result, "sections", [((i - 1) % devices, i) for i in range(devices)]))
    return jnp.concatenate(moved, axis=0)[None]


def solution(mesh):
    return jax.shard_map(
        body,
        mesh=mesh,
        in_specs=(
            P("sections", "cache", None),
            P("sections", None),
            P("sections", None, "heads"),
            P("sections", None),
            P("sections", "heads", None),
            P("sections", "cache", None, "heads"),
            P("sections", "cache", None, "heads"),
            P("sections", "cache", "heads"),
            P("sections", "cache", "heads"),
            P(),
            P(),
            P("sections", None, None),
            P("sections", None),
        ),
        out_specs=P("sections", "cache", "heads"),
        check_vma=False,
    )
```

```python
import functools
import math

import jax
import jax.numpy as jnp
from jax import lax
from jax.experimental import pallas as pl
from jax.experimental.pallas import tpu as pltpu
from jax.sharding import PartitionSpec as P

QBLOCK = 128
QB_DEV = 2
MOST = 8
GRANULE = 16
HEIGHTS = (544, 576, 672)
BUFFERS = 8
CHUNK = 512
QTILE = 256

tiny_eps = 1e-06
masked_score = -1e30
lowest = -1e38


def lookup(entries, table):
    places = jnp.arange(table.shape[0], dtype=jnp.int32)
    return jnp.sum(jnp.where(entries[..., None] == places, table, 0), axis=-1)


def pick(picks, values):
    return jnp.sum(jnp.where(picks, values[..., None, :], 0), axis=-1)


def pack_kernel(rows_ref, page_ref, *refs, page_len, height):
    *head_refs, k_ref, v_ref, out_ref, buf, sems = refs
    homes, sent, _ = out_ref.shape
    head_size = k_ref.shape[1]
    for slot in range(BUFFERS):
        for head_ref in head_refs:
            buf[slot, pl.ds(page_len + height, GRANULE), :] = head_ref[...]

    def copies_of(home, slot):
        copies = [(0, height)] + [(page_len + height, GRANULE)] * len(head_refs)
        starts = (0, height)
        return [
            pltpu.make_async_copy(
                buf.at[slot, pl.ds(here, n), :], out_ref.at[home, pl.ds(there, n), :], sems.at[slot, i]
            )
            for i, ((here, n), there) in enumerate(zip(copies, starts))
        ]

    def one_home(home, carry):
        slot = lax.rem(home, BUFFERS)

        @pl.when(home >= BUFFERS)
        def _():
            for copy in copies_of(home - BUFFERS, slot):
                copy.wait()

        row = jnp.int32(0)
        for j in range(QB_DEV * MOST):
            at = home * (QB_DEV * MOST) + j
            here = pl.multiple_of(page_ref[at] * page_len, page_len)
            there = pl.multiple_of(row, GRANULE)
            buf[slot, pl.ds(there, page_len), 0:head_size] = k_ref[pl.ds(here, page_len), :]
            buf[slot, pl.ds(there, page_len), head_size : 2 * head_size] = v_ref[pl.ds(here, page_len), :]
            row = row + rows_ref[at]
        for copy in copies_of(home, slot):
            copy.start()
        return carry

    lax.fori_loop(0, homes, one_home, 0)
    for home in range(homes - BUFFERS, homes):
        for copy in copies_of(home, home % BUFFERS):
            copy.wait()


def pack(plan, heads, key_rows, value_rows, g, homes, height, page_len, head_size):
    tokens = key_rows.shape[0]
    sent = height + GRANULE * len(heads)
    return pl.pallas_call(
        functools.partial(pack_kernel, page_len=page_len, height=height),
        grid_spec=pltpu.PrefetchScalarGridSpec(
            num_scalar_prefetch=2,
            grid=(1,),
            in_specs=[pl.BlockSpec(h.shape, lambda i, *_: (0, 0)) for h in heads]
            + [
                pl.BlockSpec((tokens, head_size), lambda i, *_: (0, g)),
                pl.BlockSpec((tokens, head_size), lambda i, *_: (0, g)),
            ],
            out_specs=pl.BlockSpec(memory_space=pltpu.HBM),
            scratch_shapes=[
                pltpu.VMEM((BUFFERS, height + page_len + GRANULE, 2 * head_size), jnp.bfloat16),
                pltpu.SemaphoreType.DMA((BUFFERS, 2)),
            ],
        ),
        out_shape=jax.ShapeDtypeStruct((homes, sent, 2 * head_size), jnp.bfloat16),
        compiler_params=pltpu.CompilerParams(vmem_limit_bytes=24 << 20),
        cost_estimate=pl.CostEstimate(
            flops=0, transcendentals=0, bytes_accessed=homes * sent * 4 * head_size + tokens * 4 * head_size
        ),
    )(*plan, *heads, key_rows, value_rows)


def attend_kernel(
    cnt_ref, first_ref, height_ref, rows_ref, live_ref, kscale_ref, vscale_ref,
    qt_ref, recv_ref, out_ref,
    kv, kcol, vcol, bias, acc, top, total, sems, *, page_len,
):
    sources = recv_ref.shape[0]
    head_size, width = qt_ref.shape[1:]
    lists = pl.program_id(0) * sources

    def copy_of(s, at):
        n = pl.multiple_of(height_ref[lists + s], GRANULE)
        start = pl.multiple_of(first_ref[lists + s], GRANULE)
        at = pl.multiple_of(at, GRANULE)
        return pltpu.make_async_copy(
            recv_ref.at[s, pl.ds(start, n), :], kv.at[pl.ds(at, n), :], sems.at[s]
        )

    def start_one(s, at):
        @pl.when(height_ref[lists + s] > 0)
        def _():
            copy_of(s, at).start()

        return at + height_ref[lists + s]

    def wait_one(s, at):
        @pl.when(height_ref[lists + s] > 0)
        def _():
            copy_of(s, at).wait()

        return at + height_ref[lists + s]

    used = lax.fori_loop(0, sources, start_one, jnp.int32(0))
    token = lax.broadcasted_iota(jnp.int32, (page_len, 128), 0)

    def columns_of(s, at):
        def one_page(j, at):
            e = (lists + s) * MOST + j
            here = pl.ds(pl.multiple_of(at, GRANULE), page_len)
            kcol[here, :] = jnp.full((page_len, 128), kscale_ref[e], jnp.float32)
            vcol[here, :] = jnp.full((page_len, 128), vscale_ref[e], jnp.float32)
            bias[here, :] = jnp.where(token < live_ref[e], 0.0, masked_score)
            return at + rows_ref[e]

        return lax.fori_loop(0, cnt_ref[lists + s], one_page, at)

    lax.fori_loop(0, sources, columns_of, jnp.int32(0))
    rest = pl.ds(pl.multiple_of(used, GRANULE), CHUNK)
    kcol[rest, :] = jnp.zeros((CHUNK, 128), jnp.float32)
    vcol[rest, :] = jnp.zeros((CHUNK, 128), jnp.float32)
    bias[rest, :] = jnp.full((CHUNK, 128), masked_score, jnp.float32)
    kv[rest, :] = jnp.zeros((CHUNK, 2 * head_size), jnp.bfloat16)
    acc[...] = jnp.zeros_like(acc)
    total[...] = jnp.zeros_like(total)
    top[...] = jnp.full_like(top, lowest)
    lax.fori_loop(0, sources, wait_one, jnp.int32(0))

    def chunk(c, carry):
        here = pl.ds(pl.multiple_of(c * CHUNK, CHUNK), CHUNK)
        keys = kv[here, 0:head_size]
        values = kv[here, head_size : 2 * head_size].T
        for i in range(width // QTILE):
            cols = pl.ds(i * QTILE, QTILE)
            score = jnp.dot(keys, qt_ref[0, :, cols], preferred_element_type=jnp.float32)
            kc, bc, vc = kcol[here, :], bias[here, :], vcol[here, :]
            wide = lambda x: jnp.concatenate([x] * (QTILE // 128), axis=1)
            score = score * wide(kc) + wide(bc)
            old = top[0:1, cols]
            new = jnp.maximum(old, jnp.max(score, axis=0, keepdims=True))
            weight = jnp.exp2(score - new)
            fade = jnp.exp2(old - new)
            total[0:1, cols] = total[0:1, cols] * fade + jnp.sum(weight, axis=0, keepdims=True)
            scaled = (weight * wide(vc)).astype(jnp.bfloat16)
            acc[:, cols] = acc[:, cols] * fade + jnp.dot(values, scaled, preferred_element_type=jnp.float32)
            top[0:1, cols] = new
        return carry

    lax.fori_loop(0, (used + CHUNK - 1) // CHUNK, chunk, 0)
    for h in range(width // QBLOCK):
        cols = slice(h * QBLOCK, (h + 1) * QBLOCK)
        out_ref[:, h * head_size : (h + 1) * head_size] = (acc[:, cols] / total[0:1, cols]).T.astype(jnp.bfloat16)


def attend(plan, qt, received, page_len, most_rows):
    blocks, head_size, width = qt.shape
    sources = received.shape[0]
    rows_held = most_rows + CHUNK + page_len
    out_width = width // QBLOCK * head_size
    return pl.pallas_call(
        functools.partial(attend_kernel, page_len=page_len),
        grid_spec=pltpu.PrefetchScalarGridSpec(
            num_scalar_prefetch=7,
            grid=(blocks,),
            in_specs=[
                pl.BlockSpec((1, head_size, width), lambda b, *_: (b, 0, 0)),
                pl.BlockSpec(memory_space=pltpu.HBM),
            ],
            out_specs=pl.BlockSpec((QBLOCK, out_width), lambda b, *_: (b, 0)),
            scratch_shapes=[
                pltpu.VMEM((rows_held, 2 * head_size), jnp.bfloat16),
                pltpu.VMEM((rows_held, 128), jnp.float32),
                pltpu.VMEM((rows_held, 128), jnp.float32),
                pltpu.VMEM((rows_held, 128), jnp.float32),
                pltpu.VMEM((head_size, width), jnp.float32),
                pltpu.VMEM((8, width), jnp.float32),
                pltpu.VMEM((8, width), jnp.float32),
                pltpu.SemaphoreType.DMA((sources,)),
            ],
        ),
        out_shape=jax.ShapeDtypeStruct((blocks * QBLOCK, out_width), jnp.bfloat16),
        compiler_params=pltpu.CompilerParams(vmem_limit_bytes=24 << 20),
        cost_estimate=pl.CostEstimate(
            flops=4 * blocks * width * most_rows * head_size,
            transcendentals=blocks * width * most_rows,
            bytes_accessed=blocks * (most_rows + width) * 4 * head_size,
        ),
    )(*plan, qt, received)


def query_kernel(x_ref, gain_ref, w_ref, head_gain_ref, out_ref, normed):
    head_size = out_ref.shape[2]

    @pl.when(pl.program_id(0) == 0)
    def _():
        x = x_ref[...].astype(jnp.float32)
        inverse = lax.rsqrt(jnp.mean(x * x, axis=-1, keepdims=True) + tiny_eps)
        normed[...] = (x * inverse * gain_ref[...]).astype(jnp.bfloat16)

    projected = jnp.dot(normed[...], w_ref[...], preferred_element_type=jnp.float32)
    for h in range(w_ref.shape[1] // head_size):
        one = projected[:, h * head_size : (h + 1) * head_size]
        inverse = lax.rsqrt(jnp.mean(one * one, axis=-1, keepdims=True) + tiny_eps)
        query = (one * inverse * head_gain_ref[...] / math.sqrt(head_size)).T.astype(jnp.bfloat16)
        for b in range(QB_DEV):
            cols = slice(b * QBLOCK, (b + 1) * QBLOCK)
            out_ref[0, b, :, h * QBLOCK : (h + 1) * QBLOCK] = query[:, cols]


def project_queries(hidden, norm_gain, w_query, query_gain, kv_local):
    row_count, model_width = hidden.shape
    head_size = query_gain.shape[0]
    group_size = w_query.shape[1] // head_size // kv_local
    tile = 2 * head_size
    tiles = group_size // 2
    return pl.pallas_call(
        query_kernel,
        grid=(kv_local * tiles,),
        in_specs=[
            pl.BlockSpec((row_count, model_width), lambda i: (0, 0)),
            pl.BlockSpec((1, model_width), lambda i: (0, 0)),
            pl.BlockSpec((model_width, tile), lambda i: (0, i)),
            pl.BlockSpec((1, head_size), lambda i: (0, 0)),
        ],
        out_specs=pl.BlockSpec(
            (1, QB_DEV, head_size, 2 * QBLOCK), lambda i: (i // tiles, 0, 0, i % tiles)
        ),
        out_shape=jax.ShapeDtypeStruct((kv_local, QB_DEV, head_size, group_size * QBLOCK), jnp.bfloat16),
        scratch_shapes=[pltpu.VMEM((row_count, model_width), jnp.bfloat16)],
        compiler_params=pltpu.CompilerParams(vmem_limit_bytes=24 << 20),
        cost_estimate=pl.CostEstimate(
            flops=2 * row_count * model_width * w_query.shape[1],
            transcendentals=0,
            bytes_accessed=2 * (w_query.size + 2 * hidden.size),
        ),
    )(hidden, norm_gain[None], w_query, query_gain[None])


def output_kernel(half_ref, *refs):
    *attended, w_ref, out_ref = refs
    span = attended[0].shape[1]
    total = jnp.dot(attended[0][...], w_ref[0:span, :], preferred_element_type=jnp.float32)
    for k in range(1, len(attended)):
        here = slice(k * span, (k + 1) * span)
        total = total + jnp.dot(attended[k][...], w_ref[here, :], preferred_element_type=jnp.float32)
    out_ref[...] = total.astype(out_ref.dtype)


def project_output(attended, w_output, half, halves, out_type):
    row_count, span = attended[0].shape
    depth, columns = w_output.shape
    tile = 256
    tiles = columns // halves // tile
    return pl.pallas_call(
        output_kernel,
        grid_spec=pltpu.PrefetchScalarGridSpec(
            num_scalar_prefetch=1,
            grid=(tiles,),
            in_specs=[pl.BlockSpec((row_count, span), lambda i, half: (0, 0)) for _ in attended]
            + [pl.BlockSpec((depth, tile), lambda i, half: (0, half[0] * tiles + i))],
            out_specs=pl.BlockSpec((row_count, tile), lambda i, half: (0, i)),
        ),
        out_shape=jax.ShapeDtypeStruct((row_count, columns // halves), out_type),
        compiler_params=pltpu.CompilerParams(vmem_limit_bytes=60 << 20),
        cost_estimate=pl.CostEstimate(
            flops=2 * row_count * depth * columns // halves,
            transcendentals=0,
            bytes_accessed=2 * depth * columns // halves + 8 * row_count * columns,
        ),
    )(half.astype(jnp.int32)[None], *attended, w_output)


def in_three(x):
    high = lax.reduce_precision(x, 8, 7)
    middle = lax.reduce_precision(x - high, 8, 7)
    low = x - high - middle
    return jnp.stack([t.astype(jnp.bfloat16) for t in (high, middle, low)])


def gather_attended(
    hidden, norm_gain, w_query, query_gain, key_rows, value_rows, told, send_plan, plan, own_picks, own_slots,
    *, height, page_len
):
    head_size = query_gain.shape[0]
    kv_local = key_rows.shape[1] // head_size
    homes = lax.axis_size("cache")
    listed = own_slots.shape[-1]
    received = []
    for g in range(kv_local):
        heads = (told,) if g == 0 else ()
        out = pack(send_plan, heads, key_rows, value_rows, g, homes, height, page_len, head_size)
        if g > 0:
            out, received[-1] = lax.optimization_barrier((out, received[-1]))
        received.append(lax.all_to_all(out, "cache", split_axis=0, concat_axis=0, tiled=True))

    queries = project_queries(hidden, norm_gain, w_query, query_gain, kv_local)

    terms = received[0][:, height : height + 3, :].astype(jnp.float32)
    scales = (terms[:, 0] + terms[:, 1]) + terms[:, 2]
    pages_dev = key_rows.shape[0] // page_len
    scales = scales[:, : 2 * kv_local * pages_dev].reshape(homes, 2 * kv_local, pages_dev)
    scales = jnp.swapaxes(scales, 0, 1).reshape(2 * kv_local, homes * pages_dev)
    at_place = own_slots[..., None] == jnp.arange(homes * pages_dev, dtype=jnp.int32)
    found = [jnp.sum(jnp.where(at_place, scales[k], 0.0), axis=-1) for k in range(2 * kv_local)]
    found = [pick(own_picks, f[:, None, :]).reshape(-1) for f in found]
    attended = []
    for g in range(kv_local):
        scaled = (found[g] * math.log2(math.e), found[kv_local + g])
        attended.append(attend((*plan, *scaled), queries[g], received[g], page_len, listed * page_len))
    return tuple(attended)


def body(
    hidden,
    norm_gain,
    w_query,
    query_gain,
    w_output,
    key_cache,
    value_cache,
    key_scale,
    value_scale,
    page_table,
    page_tokens,
    page_list,
    list_len,
):
    kv_local = key_scale.shape[2]
    pages_dev, page_len = key_cache.shape[1:3]
    listed = page_list.shape[2]
    shard_count = lax.axis_size("cache")
    own_shard = lax.axis_index("cache")

    told = jnp.concatenate([key_scale[0].T, value_scale[0].T], axis=0).reshape(-1)
    told = in_three(told)
    told = jnp.pad(told, ((0, GRANULE - 3), (0, key_cache.shape[3] // kv_local * 2 - told.shape[1])))

    entry = lookup(page_list[0], page_table * 128 + page_tokens)
    slots, counts = entry // 128, entry % 128
    used = jnp.arange(listed, dtype=jnp.int32) < list_len[0][:, None]
    rows = (counts + GRANULE - 1) // GRANULE * GRANULE
    homes = shard_count
    twin_slots = jnp.where(used, slots, -1).reshape(homes, QB_DEV, listed)[:, ::-1].reshape(-1, listed)
    both = jnp.any(slots[:, :, None] == twin_slots[:, None, :], axis=-1)
    second = (jnp.arange(homes * QB_DEV) % QB_DEV == 1)[:, None]
    shard, place = slots // pages_dev, slots % pages_dev
    order = jnp.where(used, place + jnp.where(both == second, 0, pages_dev), -1)
    earlier = (
        (shard[:, :, None] == shard[:, None, :])
        & used[:, :, None]
        & (order[:, :, None] < order[:, None, :])
    )
    rank = jnp.sum(jnp.where(earlier, 1, 0), axis=1)
    once = used & ~(both & second)
    sources = jnp.arange(shard_count, dtype=jnp.int32)
    at_source = shard[:, None, :] == sources[:, None]
    asked = jnp.sum(jnp.where(at_source & once[:, None, :], rows[:, None, :], 0), axis=-1)
    need = jnp.max(asked.reshape(homes, QB_DEV, shard_count).sum(axis=1))
    wanted = jnp.arange(MOST, dtype=jnp.int32)

    mine = (shard == own_shard) & once
    shared = jnp.sum(jnp.where(mine & both, 1, 0), axis=-1).reshape(homes, QB_DEV)[:, :1]
    behind = jnp.concatenate([jnp.zeros_like(shared), shared], axis=1).reshape(-1)
    picks = mine[:, None, :] & ((rank - behind[:, None])[:, None, :] == wanted[:, None])
    send_plan = (pick(picks, rows).reshape(-1), pick(picks, place).reshape(-1))

    devices = lax.axis_size("sections")
    agreed = need.astype(jnp.int32)[None]
    for step in range(1, devices):
        route = [(i, (i + step) % devices) for i in range(devices)]
        agreed = jnp.maximum(agreed, lax.ppermute(need.astype(jnp.int32)[None], "sections", route))
    agreed = agreed[0]

    first_block = own_shard * QB_DEV

    def own(x):
        return lax.dynamic_slice_in_dim(x, first_block, QB_DEV, 0)

    own_slots, own_counts, own_rows, own_both = own(slots), own(counts), own(rows), own(both)
    theirs = own(at_source) & own(used)[:, None, :]
    own_picks = theirs[:, :, None, :] & (own(rank)[:, None, None, :] == wanted[:, None])
    got_cnt = jnp.sum(jnp.where(theirs, 1, 0), axis=-1)
    got_height = jnp.sum(jnp.where(theirs, own_rows[:, None, :], 0), axis=-1)
    alone = jnp.sum(jnp.where(theirs & ~own_both[:, None, :], own_rows[:, None, :], 0), axis=-1)
    got_first = jnp.stack([jnp.zeros_like(alone[0]), alone[0]])
    got_rows = pick(own_picks, own_rows[:, None, :])
    got_live = pick(own_picks, own_counts[:, None, :])
    plan = tuple(x.reshape(-1) for x in (got_cnt, got_first, got_height, got_rows, got_live))
    key_rows = key_cache[0].reshape(pages_dev * page_len, -1)
    value_rows = value_cache[0].reshape(pages_dev * page_len, -1)
    most = QB_DEV * MOST * page_len
    heights = tuple(h for h in HEIGHTS if h < most) + (most,)
    branch = jnp.sum(jnp.where(agreed > jnp.array(heights[:-1], jnp.int32), 1, 0))
    send_plan, told, branch = lax.optimization_barrier((send_plan, told, branch))
    attended = lax.switch(
        branch,
        [functools.partial(gather_attended, height=h, page_len=page_len) for h in heights],
        hidden[0], norm_gain[0], w_query[0], query_gain[0], key_rows, value_rows, told, send_plan, plan,
        own_picks, own_slots,
    )

    heads_index = lax.axis_index("heads")
    halves = lax.axis_size("heads")
    half_width = hidden.shape[2] // halves
    away = project_output(attended, w_output[0], 1 - heads_index, halves, jnp.bfloat16)
    came = lax.ppermute(away, "heads", [(0, 1), (1, 0)])
    kept = project_output(attended, w_output[0], heads_index, halves, jnp.float32)
    residual = lax.dynamic_slice_in_dim(hidden[0], heads_index * half_width, half_width, 1).astype(jnp.float32)
    result = (kept + came.astype(jnp.float32) + residual).astype(jnp.bfloat16)
    return lax.ppermute(result[None], "sections", [((i - 1) % devices, i) for i in range(devices)])


def solution(mesh):
    return jax.shard_map(
        body,
        mesh=mesh,
        in_specs=(
            P("sections", "cache", None),
            P("sections", None),
            P("sections", None, "heads"),
            P("sections", None),
            P("sections", "heads", None),
            P("sections", "cache", None, "heads"),
            P("sections", "cache", None, "heads"),
            P("sections", "cache", "heads"),
            P("sections", "cache", "heads"),
            P(),
            P(),
            P("sections", None, None),
            P("sections", None),
        ),
        out_specs=P("sections", "cache", "heads"),
        check_vma=False,
    )
```

```python
import functools
import math

import jax
import jax.numpy as jnp
from jax import lax
from jax.experimental import pallas as pl
from jax.experimental.pallas import tpu as pltpu
from jax.sharding import PartitionSpec as P

QBLOCK = 128
QB_DEV = 2
MOST = 8
GRANULE = 16
HEIGHTS = (576, 656)
BUFFERS = 8
CHUNK = 512
QTILE = 256

tiny_eps = 1e-06
masked_score = -1e30
lowest = -1e38


def lookup(entries, table):
    places = jnp.arange(table.shape[0], dtype=jnp.int32)
    return jnp.sum(jnp.where(entries[..., None] == places, table, 0), axis=-1)


def pick(picks, values):
    return jnp.sum(jnp.where(picks, values[..., None, :], 0), axis=-1)


def pack_kernel(rows_ref, page_ref, *refs, page_len, height):
    *head_refs, k_ref, v_ref, out_ref, buf, sems = refs
    homes, sent, _ = out_ref.shape
    head_size = k_ref.shape[1]
    for slot in range(BUFFERS):
        for head_ref in head_refs:
            buf[slot, pl.ds(page_len + height, GRANULE), :] = head_ref[...]

    def copies_of(home, slot):
        copies = [(0, height)] + [(page_len + height, GRANULE)] * len(head_refs)
        starts = (0, height)
        return [
            pltpu.make_async_copy(
                buf.at[slot, pl.ds(here, n), :], out_ref.at[home, pl.ds(there, n), :], sems.at[slot, i]
            )
            for i, ((here, n), there) in enumerate(zip(copies, starts))
        ]

    def one_home(home, carry):
        slot = lax.rem(home, BUFFERS)

        @pl.when(home >= BUFFERS)
        def _():
            for copy in copies_of(home - BUFFERS, slot):
                copy.wait()

        row = jnp.int32(0)
        for j in range(QB_DEV * MOST):
            at = home * (QB_DEV * MOST) + j
            here = pl.multiple_of(page_ref[at] * page_len, page_len)
            there = pl.multiple_of(row, GRANULE)
            buf[slot, pl.ds(there, page_len), 0:head_size] = k_ref[pl.ds(here, page_len), :]
            buf[slot, pl.ds(there, page_len), head_size : 2 * head_size] = v_ref[pl.ds(here, page_len), :]
            row = row + rows_ref[at]
        for copy in copies_of(home, slot):
            copy.start()
        return carry

    lax.fori_loop(0, homes, one_home, 0)
    for home in range(homes - BUFFERS, homes):
        for copy in copies_of(home, home % BUFFERS):
            copy.wait()


def pack(plan, heads, key_rows, value_rows, g, homes, height, page_len, head_size):
    tokens = key_rows.shape[0]
    sent = height + GRANULE * len(heads)
    return pl.pallas_call(
        functools.partial(pack_kernel, page_len=page_len, height=height),
        grid_spec=pltpu.PrefetchScalarGridSpec(
            num_scalar_prefetch=2,
            grid=(1,),
            in_specs=[pl.BlockSpec(h.shape, lambda i, *_: (0, 0)) for h in heads]
            + [
                pl.BlockSpec((tokens, head_size), lambda i, *_: (0, g)),
                pl.BlockSpec((tokens, head_size), lambda i, *_: (0, g)),
            ],
            out_specs=pl.BlockSpec(memory_space=pltpu.HBM),
            scratch_shapes=[
                pltpu.VMEM((BUFFERS, height + page_len + GRANULE, 2 * head_size), jnp.bfloat16),
                pltpu.SemaphoreType.DMA((BUFFERS, 2)),
            ],
        ),
        out_shape=jax.ShapeDtypeStruct((homes, sent, 2 * head_size), jnp.bfloat16),
        compiler_params=pltpu.CompilerParams(vmem_limit_bytes=60 << 20),
        cost_estimate=pl.CostEstimate(
            flops=0, transcendentals=0, bytes_accessed=homes * sent * 4 * head_size + tokens * 4 * head_size
        ),
    )(*plan, *heads, key_rows, value_rows)


def attend_kernel(
    cnt_ref, first_ref, height_ref, rows_ref, live_ref, kscale_ref, vscale_ref,
    qt_ref, recv_ref, out_ref,
    kv, kcol, vcol, bias, acc, top, total, sems, *, page_len, first_block,
):
    sources = recv_ref.shape[0]
    head_size, width = qt_ref.shape[1:]
    lists = (pl.program_id(0) + first_block) * sources

    def copy_of(s, at):
        n = pl.multiple_of(height_ref[lists + s], GRANULE)
        start = pl.multiple_of(first_ref[lists + s], GRANULE)
        at = pl.multiple_of(at, GRANULE)
        return pltpu.make_async_copy(
            recv_ref.at[s, pl.ds(start, n), :], kv.at[pl.ds(at, n), :], sems.at[s]
        )

    def start_one(s, at):
        @pl.when(height_ref[lists + s] > 0)
        def _():
            copy_of(s, at).start()

        return at + height_ref[lists + s]

    def wait_one(s, at):
        @pl.when(height_ref[lists + s] > 0)
        def _():
            copy_of(s, at).wait()

        return at + height_ref[lists + s]

    used = lax.fori_loop(0, sources, start_one, jnp.int32(0))
    token = lax.broadcasted_iota(jnp.int32, (page_len, 128), 0)

    def columns_of(s, at):
        def one_page(j, at):
            e = (lists + s) * MOST + j
            here = pl.ds(pl.multiple_of(at, GRANULE), page_len)
            kcol[here, :] = jnp.full((page_len, 128), kscale_ref[e], jnp.float32)
            vcol[here, :] = jnp.full((page_len, 128), vscale_ref[e], jnp.float32)
            bias[here, :] = jnp.where(token < live_ref[e], 0.0, masked_score)
            return at + rows_ref[e]

        return lax.fori_loop(0, cnt_ref[lists + s], one_page, at)

    lax.fori_loop(0, sources, columns_of, jnp.int32(0))
    rest = pl.ds(pl.multiple_of(used, GRANULE), CHUNK)
    kcol[rest, :] = jnp.zeros((CHUNK, 128), jnp.float32)
    vcol[rest, :] = jnp.zeros((CHUNK, 128), jnp.float32)
    bias[rest, :] = jnp.full((CHUNK, 128), masked_score, jnp.float32)
    kv[rest, :] = jnp.zeros((CHUNK, 2 * head_size), jnp.bfloat16)
    acc[...] = jnp.zeros_like(acc)
    total[...] = jnp.zeros_like(total)
    top[...] = jnp.full_like(top, lowest)
    lax.fori_loop(0, sources, wait_one, jnp.int32(0))

    def chunk(c, carry):
        here = pl.ds(pl.multiple_of(c * CHUNK, CHUNK), CHUNK)
        keys = kv[here, 0:head_size]
        values = kv[here, head_size : 2 * head_size].T
        def one_tile(i, carry):
            cols = pl.ds(pl.multiple_of(i * QTILE, QTILE), QTILE)
            score = jnp.dot(keys, qt_ref[0, :, cols], preferred_element_type=jnp.float32)
            kc, bc, vc = kcol[here, :], bias[here, :], vcol[here, :]
            wide = lambda x: jnp.concatenate([x] * (QTILE // 128), axis=1)
            score = score * wide(kc) + wide(bc)
            old = top[0:1, cols]
            new = jnp.maximum(old, jnp.max(score, axis=0, keepdims=True))
            weight = jnp.exp2(score - new)
            fade = jnp.exp2(old - new)
            total[0:1, cols] = total[0:1, cols] * fade + jnp.sum(weight, axis=0, keepdims=True)
            scaled = (weight * wide(vc)).astype(jnp.bfloat16)
            acc[:, cols] = acc[:, cols] * fade + jnp.dot(values, scaled, preferred_element_type=jnp.float32)
            top[0:1, cols] = new
            return carry

        return lax.fori_loop(0, width // QTILE, one_tile, carry)

    lax.fori_loop(0, (used + CHUNK - 1) // CHUNK, chunk, 0)
    for h in range(width // QBLOCK):
        cols = slice(h * QBLOCK, (h + 1) * QBLOCK)
        out_ref[:, h * head_size : (h + 1) * head_size] = (acc[:, cols] / total[0:1, cols]).T.astype(jnp.bfloat16)


def attend(plan, qt, received, first_block, blocks, page_len, most_rows):
    head_size, width = qt.shape[1:]
    sources = received.shape[0]
    rows_held = most_rows + CHUNK + page_len
    out_width = width // QBLOCK * head_size
    return pl.pallas_call(
        functools.partial(attend_kernel, page_len=page_len, first_block=first_block),
        grid_spec=pltpu.PrefetchScalarGridSpec(
            num_scalar_prefetch=7,
            grid=(blocks,),
            in_specs=[
                pl.BlockSpec((1, head_size, width), lambda b, *_: (b + first_block, 0, 0)),
                pl.BlockSpec(memory_space=pltpu.HBM),
            ],
            out_specs=pl.BlockSpec((QBLOCK, out_width), lambda b, *_: (b, 0)),
            scratch_shapes=[
                pltpu.VMEM((rows_held, 2 * head_size), jnp.bfloat16),
                pltpu.VMEM((rows_held, 128), jnp.float32),
                pltpu.VMEM((rows_held, 128), jnp.float32),
                pltpu.VMEM((rows_held, 128), jnp.float32),
                pltpu.VMEM((head_size, width), jnp.float32),
                pltpu.VMEM((8, width), jnp.float32),
                pltpu.VMEM((8, width), jnp.float32),
                pltpu.SemaphoreType.DMA((sources,)),
            ],
        ),
        out_shape=jax.ShapeDtypeStruct((blocks * QBLOCK, out_width), jnp.bfloat16),
        compiler_params=pltpu.CompilerParams(vmem_limit_bytes=24 << 20),
        cost_estimate=pl.CostEstimate(
            flops=4 * blocks * width * most_rows * head_size,
            transcendentals=blocks * width * most_rows,
            bytes_accessed=blocks * (most_rows + width) * 4 * head_size,
        ),
    )(*plan, qt, received)


def query_kernel(x_ref, gain_ref, w_ref, head_gain_ref, out_ref, normed):
    head_size = out_ref.shape[2]

    @pl.when(pl.program_id(0) == 0)
    def _():
        x = x_ref[...].astype(jnp.float32)
        inverse = lax.rsqrt(jnp.mean(x * x, axis=-1, keepdims=True) + tiny_eps)
        normed[...] = (x * inverse * gain_ref[...]).astype(jnp.bfloat16)

    projected = jnp.dot(normed[...], w_ref[...], preferred_element_type=jnp.float32)
    for h in range(w_ref.shape[1] // head_size):
        one = projected[:, h * head_size : (h + 1) * head_size]
        inverse = lax.rsqrt(jnp.mean(one * one, axis=-1, keepdims=True) + tiny_eps)
        query = (one * inverse * head_gain_ref[...] / math.sqrt(head_size)).T.astype(jnp.bfloat16)
        for b in range(QB_DEV):
            cols = slice(b * QBLOCK, (b + 1) * QBLOCK)
            out_ref[0, b, :, h * QBLOCK : (h + 1) * QBLOCK] = query[:, cols]


def project_queries(hidden, norm_gain, w_query, query_gain, kv_local):
    row_count, model_width = hidden.shape
    head_size = query_gain.shape[0]
    group_size = w_query.shape[1] // head_size // kv_local
    tile = 2 * head_size
    tiles = group_size // 2
    return pl.pallas_call(
        query_kernel,
        grid=(kv_local * tiles,),
        in_specs=[
            pl.BlockSpec((row_count, model_width), lambda i: (0, 0)),
            pl.BlockSpec((1, model_width), lambda i: (0, 0)),
            pl.BlockSpec((model_width, tile), lambda i: (0, i)),
            pl.BlockSpec((1, head_size), lambda i: (0, 0)),
        ],
        out_specs=pl.BlockSpec(
            (1, QB_DEV, head_size, 2 * QBLOCK), lambda i: (i // tiles, 0, 0, i % tiles)
        ),
        out_shape=jax.ShapeDtypeStruct((kv_local, QB_DEV, head_size, group_size * QBLOCK), jnp.bfloat16),
        scratch_shapes=[pltpu.VMEM((row_count, model_width), jnp.bfloat16)],
        compiler_params=pltpu.CompilerParams(vmem_limit_bytes=24 << 20),
        cost_estimate=pl.CostEstimate(
            flops=2 * row_count * model_width * w_query.shape[1],
            transcendentals=0,
            bytes_accessed=2 * (w_query.size + 2 * hidden.size),
        ),
    )(hidden, norm_gain[None], w_query, query_gain[None])


def term_kernel(att_ref, w_ref, *refs):
    *so_far, out_ref = refs
    total = jnp.dot(att_ref[...], w_ref[...], preferred_element_type=jnp.float32)
    for ref in so_far:
        total = total + ref[...]
    out_ref[...] = total


def output_term(attended, w_output, g, sofar, block):
    row_count, span = attended.shape
    columns = w_output.shape[1]
    tile = 512
    more = [] if sofar is None else [sofar]
    return pl.pallas_call(
        term_kernel,
        grid=(columns // tile,),
        in_specs=[
            pl.BlockSpec((row_count, span), lambda i: (0, 0)),
            pl.BlockSpec((span, tile), lambda i: (g, i)),
        ]
        + [pl.BlockSpec((row_count, tile), lambda i: (block, i)) for _ in more],
        out_specs=pl.BlockSpec((row_count, tile), lambda i: (0, i)),
        out_shape=jax.ShapeDtypeStruct((row_count, columns), jnp.float32),
        compiler_params=pltpu.CompilerParams(vmem_limit_bytes=24 << 20),
        cost_estimate=pl.CostEstimate(
            flops=2 * row_count * span * columns, transcendentals=0, bytes_accessed=2 * span * columns
        ),
    )(attended, w_output, *more)


def in_three(x):
    high = lax.reduce_precision(x, 8, 7)
    middle = lax.reduce_precision(x - high, 8, 7)
    low = x - high - middle
    return jnp.stack([t.astype(jnp.bfloat16) for t in (high, middle, low)])


def home_plan(slots, counts, rows, used, both, rank, shard):
    shard_count = lax.axis_size("cache")
    first_block = lax.axis_index("cache") * QB_DEV

    def own(x):
        return lax.dynamic_slice_in_dim(x, first_block, QB_DEV, 0)

    own_counts, own_rows = own(counts)[:, None, :], own(rows)[:, None, :]
    sources = jnp.arange(shard_count, dtype=jnp.int32)
    theirs = (own(shard)[:, None, :] == sources[:, None]) & own(used)[:, None, :]
    wanted = jnp.arange(MOST, dtype=jnp.int32)
    picks = theirs[:, :, None, :] & (own(rank)[:, None, None, :] == wanted[:, None])
    got_cnt = jnp.sum(jnp.where(theirs, 1, 0), axis=-1)
    got_height = jnp.sum(jnp.where(theirs, own_rows, 0), axis=-1)
    alone = jnp.sum(jnp.where(theirs & ~own(both)[:, None, :], own_rows, 0), axis=-1)
    got_first = jnp.stack([jnp.zeros_like(alone[0]), alone[0]])
    plan = (got_cnt, got_first, got_height, pick(picks, own_rows), pick(picks, own_counts))
    return tuple(x.reshape(-1) for x in plan), picks, own(slots)


def one_section(
    hidden, norm_gain, w_query, query_gain, w_output, key_rows, value_rows, told, send_plan, lists, *, height, page_len
):
    model_width = hidden.shape[1]
    head_size = query_gain.shape[0]
    kv_local = key_rows.shape[1] // head_size
    homes = lax.axis_size("cache")
    received = []
    for g in range(kv_local):
        heads = (told,) if g == 0 else ()
        out = pack(send_plan, heads, key_rows, value_rows, g, homes, height, page_len, head_size)
        if g > 0:
            out, received[-1] = lax.optimization_barrier((out, received[-1]))
        received.append(lax.all_to_all(out, "cache", split_axis=0, concat_axis=0, tiled=True))

    queries = project_queries(hidden, norm_gain, w_query, query_gain, kv_local)
    plan, own_picks, own_slots = home_plan(*lists)
    listed = own_slots.shape[-1]

    terms = received[0][:, height : height + 3, :].astype(jnp.float32)
    scales = (terms[:, 0] + terms[:, 1]) + terms[:, 2]
    pages_dev = key_rows.shape[0] // page_len
    scales = scales[:, : 2 * kv_local * pages_dev].reshape(homes, 2 * kv_local, pages_dev)
    scales = jnp.swapaxes(scales, 0, 1).reshape(2 * kv_local, homes * pages_dev)
    at_place = own_slots[..., None] == jnp.arange(homes * pages_dev, dtype=jnp.int32)
    found = [jnp.sum(jnp.where(at_place, scales[k], 0.0), axis=-1) for k in range(2 * kv_local)]
    found = [pick(own_picks, f[:, None, :]).reshape(-1) for f in found]

    heads_index = lax.axis_index("heads")
    half_width = model_width // lax.axis_size("heads")
    devices = lax.axis_size("sections")
    sofar = None
    for g in range(kv_local - 1):
        full_plan = (*plan, found[g] * math.log2(math.e), found[kv_local + g])
        attended = attend(full_plan, queries[g], received[g], 0, QB_DEV, page_len, listed * page_len)
        sofar = output_term(attended, w_output, g, sofar, 0)

    g = kv_local - 1
    full_plan = (*plan, found[g] * math.log2(math.e), found[kv_local + g])
    whole, came = [None] * QB_DEV, [None] * QB_DEV
    for b in range(QB_DEV):
        attended = attend(full_plan, queries[g], received[g], b, 1, page_len, listed * page_len)
        if b > 0:
            attended, came[b - 1] = lax.optimization_barrier((attended, came[b - 1]))
        whole[b] = output_term(attended, w_output, g, sofar, b)
        away = lax.dynamic_slice_in_dim(whole[b], (1 - heads_index) * half_width, half_width, 1)
        came[b] = lax.ppermute(away.astype(jnp.bfloat16), "heads", [(0, 1), (1, 0)])
    moved, result = [], None
    for b in range(QB_DEV):
        if result is not None:
            came[b], _ = lax.optimization_barrier((came[b], result))
        kept = lax.dynamic_slice_in_dim(whole[b], heads_index * half_width, half_width, 1)
        residual = lax.dynamic_slice(hidden, (b * QBLOCK, heads_index * half_width), (QBLOCK, half_width))
        result = (kept + came[b].astype(jnp.float32) + residual.astype(jnp.float32)).astype(jnp.bfloat16)
        moved.append(lax.ppermute(result, "sections", [((i - 1) % devices, i) for i in range(devices)]))
    return jnp.concatenate(moved, axis=0)


def body(
    hidden,
    norm_gain,
    w_query,
    query_gain,
    w_output,
    key_cache,
    value_cache,
    key_scale,
    value_scale,
    page_table,
    page_tokens,
    page_list,
    list_len,
):
    kv_local = key_scale.shape[2]
    pages_dev, page_len = key_cache.shape[1:3]
    listed = page_list.shape[2]
    shard_count = lax.axis_size("cache")
    own_shard = lax.axis_index("cache")

    told = jnp.concatenate([key_scale[0].T, value_scale[0].T], axis=0).reshape(-1)
    told = in_three(told)
    told = jnp.pad(told, ((0, GRANULE - 3), (0, key_cache.shape[3] // kv_local * 2 - told.shape[1])))

    entry = lookup(page_list[0], page_table * 128 + page_tokens)
    slots, counts = entry // 128, entry % 128
    used = jnp.arange(listed, dtype=jnp.int32) < list_len[0][:, None]
    rows = (counts + GRANULE - 1) // GRANULE * GRANULE
    homes = shard_count
    twin_slots = jnp.where(used, slots, -1).reshape(homes, QB_DEV, listed)[:, ::-1].reshape(-1, listed)
    both = jnp.any(slots[:, :, None] == twin_slots[:, None, :], axis=-1)
    second = (jnp.arange(homes * QB_DEV) % QB_DEV == 1)[:, None]
    shard, place = slots // pages_dev, slots % pages_dev
    order = jnp.where(used, place + jnp.where(both == second, 0, pages_dev), -1)
    earlier = (
        (shard[:, :, None] == shard[:, None, :])
        & used[:, :, None]
        & (order[:, :, None] < order[:, None, :])
    )
    rank = jnp.sum(jnp.where(earlier, 1, 0), axis=1)
    once = used & ~(both & second)
    sources = jnp.arange(shard_count, dtype=jnp.int32)
    at_source = shard[:, None, :] == sources[:, None]
    asked = jnp.sum(jnp.where(at_source & once[:, None, :], rows[:, None, :], 0), axis=-1)
    need = jnp.max(asked.reshape(homes, QB_DEV, shard_count).sum(axis=1))
    wanted = jnp.arange(MOST, dtype=jnp.int32)

    mine = (shard == own_shard) & once
    shared = jnp.sum(jnp.where(mine & both, 1, 0), axis=-1).reshape(homes, QB_DEV)[:, :1]
    behind = jnp.concatenate([jnp.zeros_like(shared), shared], axis=1).reshape(-1)
    picks = mine[:, None, :] & ((rank - behind[:, None])[:, None, :] == wanted[:, None])
    send_plan = (pick(picks, rows).reshape(-1), pick(picks, place).reshape(-1))

    devices = lax.axis_size("sections")
    agreed = need.astype(jnp.int32)[None]
    for step in range(1, devices):
        route = [(i, (i + step) % devices) for i in range(devices)]
        agreed = jnp.maximum(agreed, lax.ppermute(need.astype(jnp.int32)[None], "sections", route))
    agreed = agreed[0]

    key_rows = key_cache[0].reshape(pages_dev * page_len, -1)
    value_rows = value_cache[0].reshape(pages_dev * page_len, -1)
    most = QB_DEV * MOST * page_len
    heights = tuple(h for h in HEIGHTS if h < most) + (most,)
    branch = jnp.sum(jnp.where(agreed > jnp.array(heights[:-1], jnp.int32), 1, 0))
    send_plan, told, branch = lax.optimization_barrier((send_plan, told, branch))
    moved = lax.switch(
        branch,
        [functools.partial(one_section, height=h, page_len=page_len) for h in heights],
        hidden[0], norm_gain[0], w_query[0], query_gain[0], w_output[0], key_rows, value_rows, told, send_plan,
        (slots, counts, rows, used, both, rank, shard),
    )
    return moved[None]


def solution(mesh):
    return jax.shard_map(
        body,
        mesh=mesh,
        in_specs=(
            P("sections", "cache", None),
            P("sections", None),
            P("sections", None, "heads"),
            P("sections", None),
            P("sections", "heads", None),
            P("sections", "cache", None, "heads"),
            P("sections", "cache", None, "heads"),
            P("sections", "cache", "heads"),
            P("sections", "cache", "heads"),
            P(),
            P(),
            P("sections", None, None),
            P("sections", None),
        ),
        out_specs=P("sections", "cache", "heads"),
        check_vma=False,
    )
```

```python
import functools
import math

import jax
import jax.numpy as jnp
from jax import lax
from jax.experimental import pallas as pl
from jax.experimental.pallas import tpu as pltpu
from jax.sharding import PartitionSpec as P

QBLOCK = 128
QB_DEV = 2
MOST = 8
GRANULE = 16
HEIGHTS = (576, 656)
BUFFERS = 8
CHUNK = 512
QTILE = 256

tiny_eps = 1e-06
masked_score = -1e30
lowest = -1e38


def lookup(entries, table):
    places = jnp.arange(table.shape[0], dtype=jnp.int32)
    return jnp.sum(jnp.where(entries[..., None] == places, table, 0), axis=-1)


def pick(picks, values):
    return jnp.sum(jnp.where(picks, values[..., None, :], 0), axis=-1)


def pack_kernel(rows_ref, page_ref, *refs, page_len, height):
    *head_refs, k_ref, v_ref, out_ref, buf, sems = refs
    homes, sent, _ = out_ref.shape
    head_size = k_ref.shape[1]
    for slot in range(BUFFERS):
        for head_ref in head_refs:
            buf[slot, pl.ds(page_len + height, GRANULE), :] = head_ref[...]

    def copies_of(home, slot):
        copies = [(0, height)] + [(page_len + height, GRANULE)] * len(head_refs)
        starts = (0, height)
        return [
            pltpu.make_async_copy(
                buf.at[slot, pl.ds(here, n), :], out_ref.at[home, pl.ds(there, n), :], sems.at[slot, i]
            )
            for i, ((here, n), there) in enumerate(zip(copies, starts))
        ]

    def one_home(home, carry):
        slot = lax.rem(home, BUFFERS)

        @pl.when(home >= BUFFERS)
        def _():
            for copy in copies_of(home - BUFFERS, slot):
                copy.wait()

        row = jnp.int32(0)
        for j in range(QB_DEV * MOST):
            at = home * (QB_DEV * MOST) + j
            here = pl.multiple_of(page_ref[at] * page_len, page_len)
            there = pl.multiple_of(row, GRANULE)
            buf[slot, pl.ds(there, page_len), 0:head_size] = k_ref[pl.ds(here, page_len), :]
            buf[slot, pl.ds(there, page_len), head_size : 2 * head_size] = v_ref[pl.ds(here, page_len), :]
            row = row + rows_ref[at]
        for copy in copies_of(home, slot):
            copy.start()
        return carry

    lax.fori_loop(0, homes, one_home, 0)
    for home in range(homes - BUFFERS, homes):
        for copy in copies_of(home, home % BUFFERS):
            copy.wait()


def pack(plan, heads, key_rows, value_rows, g, homes, height, page_len, head_size):
    tokens = key_rows.shape[0]
    sent = height + GRANULE * len(heads)
    return pl.pallas_call(
        functools.partial(pack_kernel, page_len=page_len, height=height),
        grid_spec=pltpu.PrefetchScalarGridSpec(
            num_scalar_prefetch=2,
            grid=(1,),
            in_specs=[pl.BlockSpec(h.shape, lambda i, *_: (0, 0)) for h in heads]
            + [
                pl.BlockSpec((tokens, head_size), lambda i, *_: (0, g)),
                pl.BlockSpec((tokens, head_size), lambda i, *_: (0, g)),
            ],
            out_specs=pl.BlockSpec(memory_space=pltpu.HBM),
            scratch_shapes=[
                pltpu.VMEM((BUFFERS, height + page_len + GRANULE, 2 * head_size), jnp.bfloat16),
                pltpu.SemaphoreType.DMA((BUFFERS, 2)),
            ],
        ),
        out_shape=jax.ShapeDtypeStruct((homes, sent, 2 * head_size), jnp.bfloat16),
        compiler_params=pltpu.CompilerParams(vmem_limit_bytes=60 << 20),
        cost_estimate=pl.CostEstimate(
            flops=0, transcendentals=0, bytes_accessed=homes * sent * 4 * head_size + tokens * 4 * head_size
        ),
    )(*plan, *heads, key_rows, value_rows)


def attend_kernel(
    cnt_ref, first_ref, height_ref, rows_ref, live_ref, kscale_ref, vscale_ref,
    qt_ref, recv_ref, out_ref,
    kv, kcol, vcol, bias, acc, top, total, sems, *, page_len,
):
    sources = recv_ref.shape[0]
    head_size, width = qt_ref.shape[1:]
    lists = pl.program_id(0) * sources

    def copy_of(s, at):
        n = pl.multiple_of(height_ref[lists + s], GRANULE)
        start = pl.multiple_of(first_ref[lists + s], GRANULE)
        at = pl.multiple_of(at, GRANULE)
        return pltpu.make_async_copy(
            recv_ref.at[s, pl.ds(start, n), :], kv.at[pl.ds(at, n), :], sems.at[s]
        )

    def start_one(s, at):
        @pl.when(height_ref[lists + s] > 0)
        def _():
            copy_of(s, at).start()

        return at + height_ref[lists + s]

    def wait_one(s, at):
        @pl.when(height_ref[lists + s] > 0)
        def _():
            copy_of(s, at).wait()

        return at + height_ref[lists + s]

    used = lax.fori_loop(0, sources, start_one, jnp.int32(0))
    token = lax.broadcasted_iota(jnp.int32, (page_len, 128), 0)

    def columns_of(s, at):
        def one_page(j, at):
            e = (lists + s) * MOST + j
            here = pl.ds(pl.multiple_of(at, GRANULE), page_len)
            kcol[here, :] = jnp.full((page_len, 128), kscale_ref[e], jnp.float32)
            vcol[here, :] = jnp.full((page_len, 128), vscale_ref[e], jnp.float32)
            bias[here, :] = jnp.where(token < live_ref[e], 0.0, masked_score)
            return at + rows_ref[e]

        return lax.fori_loop(0, cnt_ref[lists + s], one_page, at)

    lax.fori_loop(0, sources, columns_of, jnp.int32(0))
    rest = pl.ds(pl.multiple_of(used, GRANULE), CHUNK)
    kcol[rest, :] = jnp.zeros((CHUNK, 128), jnp.float32)
    vcol[rest, :] = jnp.zeros((CHUNK, 128), jnp.float32)
    bias[rest, :] = jnp.full((CHUNK, 128), masked_score, jnp.float32)
    kv[rest, :] = jnp.zeros((CHUNK, 2 * head_size), jnp.bfloat16)
    acc[...] = jnp.zeros_like(acc)
    total[...] = jnp.zeros_like(total)
    top[...] = jnp.full_like(top, lowest)
    lax.fori_loop(0, sources, wait_one, jnp.int32(0))

    def chunk(c, carry):
        here = pl.ds(pl.multiple_of(c * CHUNK, CHUNK), CHUNK)
        keys = kv[here, 0:head_size]
        values = kv[here, head_size : 2 * head_size].T
        for i in range(width // QTILE):
            cols = pl.ds(i * QTILE, QTILE)
            score = jnp.dot(keys, qt_ref[0, :, cols], preferred_element_type=jnp.float32)
            kc, bc, vc = kcol[here, :], bias[here, :], vcol[here, :]
            wide = lambda x: jnp.concatenate([x] * (QTILE // 128), axis=1)
            score = score * wide(kc) + wide(bc)
            old = top[0:1, cols]
            new = jnp.maximum(old, jnp.max(score, axis=0, keepdims=True))
            weight = jnp.exp2(score - new)
            fade = jnp.exp2(old - new)
            total[0:1, cols] = total[0:1, cols] * fade + jnp.sum(weight, axis=0, keepdims=True)
            scaled = (weight * wide(vc)).astype(jnp.bfloat16)
            acc[:, cols] = acc[:, cols] * fade + jnp.dot(values, scaled, preferred_element_type=jnp.float32)
            top[0:1, cols] = new
        return carry

    lax.fori_loop(0, (used + CHUNK - 1) // CHUNK, chunk, 0)
    for h in range(width // QBLOCK):
        cols = slice(h * QBLOCK, (h + 1) * QBLOCK)
        out_ref[:, h * head_size : (h + 1) * head_size] = (acc[:, cols] / total[0:1, cols]).T.astype(jnp.bfloat16)


def attend(plan, qt, received, page_len, most_rows):
    blocks, head_size, width = qt.shape
    sources = received.shape[0]
    rows_held = most_rows + CHUNK + page_len
    out_width = width // QBLOCK * head_size
    return pl.pallas_call(
        functools.partial(attend_kernel, page_len=page_len),
        grid_spec=pltpu.PrefetchScalarGridSpec(
            num_scalar_prefetch=7,
            grid=(blocks,),
            in_specs=[
                pl.BlockSpec((1, head_size, width), lambda b, *_: (b, 0, 0)),
                pl.BlockSpec(memory_space=pltpu.HBM),
            ],
            out_specs=pl.BlockSpec((QBLOCK, out_width), lambda b, *_: (b, 0)),
            scratch_shapes=[
                pltpu.VMEM((rows_held, 2 * head_size), jnp.bfloat16),
                pltpu.VMEM((rows_held, 128), jnp.float32),
                pltpu.VMEM((rows_held, 128), jnp.float32),
                pltpu.VMEM((rows_held, 128), jnp.float32),
                pltpu.VMEM((head_size, width), jnp.float32),
                pltpu.VMEM((8, width), jnp.float32),
                pltpu.VMEM((8, width), jnp.float32),
                pltpu.SemaphoreType.DMA((sources,)),
            ],
        ),
        out_shape=jax.ShapeDtypeStruct((blocks * QBLOCK, out_width), jnp.bfloat16),
        compiler_params=pltpu.CompilerParams(vmem_limit_bytes=24 << 20),
        cost_estimate=pl.CostEstimate(
            flops=4 * blocks * width * most_rows * head_size,
            transcendentals=blocks * width * most_rows,
            bytes_accessed=blocks * (most_rows + width) * 4 * head_size,
        ),
    )(*plan, qt, received)


def query_kernel(x_ref, gain_ref, w_ref, head_gain_ref, out_ref, normed):
    head_size = out_ref.shape[2]

    @pl.when(pl.program_id(0) == 0)
    def _():
        x = x_ref[...].astype(jnp.float32)
        inverse = lax.rsqrt(jnp.mean(x * x, axis=-1, keepdims=True) + tiny_eps)
        normed[...] = (x * inverse * gain_ref[...]).astype(jnp.bfloat16)

    projected = jnp.dot(normed[...], w_ref[...], preferred_element_type=jnp.float32)
    for h in range(w_ref.shape[1] // head_size):
        one = projected[:, h * head_size : (h + 1) * head_size]
        inverse = lax.rsqrt(jnp.mean(one * one, axis=-1, keepdims=True) + tiny_eps)
        query = (one * inverse * head_gain_ref[...] / math.sqrt(head_size)).T.astype(jnp.bfloat16)
        for b in range(QB_DEV):
            cols = slice(b * QBLOCK, (b + 1) * QBLOCK)
            out_ref[0, b, :, h * QBLOCK : (h + 1) * QBLOCK] = query[:, cols]


def project_queries(hidden, norm_gain, w_query, query_gain, kv_local):
    row_count, model_width = hidden.shape
    head_size = query_gain.shape[0]
    group_size = w_query.shape[1] // head_size // kv_local
    tile = 2 * head_size
    tiles = group_size // 2
    return pl.pallas_call(
        query_kernel,
        grid=(kv_local * tiles,),
        in_specs=[
            pl.BlockSpec((row_count, model_width), lambda i: (0, 0)),
            pl.BlockSpec((1, model_width), lambda i: (0, 0)),
            pl.BlockSpec((model_width, tile), lambda i: (0, i)),
            pl.BlockSpec((1, head_size), lambda i: (0, 0)),
        ],
        out_specs=pl.BlockSpec(
            (1, QB_DEV, head_size, 2 * QBLOCK), lambda i: (i // tiles, 0, 0, i % tiles)
        ),
        out_shape=jax.ShapeDtypeStruct((kv_local, QB_DEV, head_size, group_size * QBLOCK), jnp.bfloat16),
        scratch_shapes=[pltpu.VMEM((row_count, model_width), jnp.bfloat16)],
        compiler_params=pltpu.CompilerParams(vmem_limit_bytes=24 << 20),
        cost_estimate=pl.CostEstimate(
            flops=2 * row_count * model_width * w_query.shape[1],
            transcendentals=0,
            bytes_accessed=2 * (w_query.size + 2 * hidden.size),
        ),
    )(hidden, norm_gain[None], w_query, query_gain[None])


def in_three(x):
    high = lax.reduce_precision(x, 8, 7)
    middle = lax.reduce_precision(x - high, 8, 7)
    low = x - high - middle
    return jnp.stack([t.astype(jnp.bfloat16) for t in (high, middle, low)])


def home_plan(slots, counts, rows, used, both, rank, shard):
    shard_count = lax.axis_size("cache")
    first_block = lax.axis_index("cache") * QB_DEV

    def own(x):
        return lax.dynamic_slice_in_dim(x, first_block, QB_DEV, 0)

    own_counts, own_rows = own(counts)[:, None, :], own(rows)[:, None, :]
    sources = jnp.arange(shard_count, dtype=jnp.int32)
    theirs = (own(shard)[:, None, :] == sources[:, None]) & own(used)[:, None, :]
    wanted = jnp.arange(MOST, dtype=jnp.int32)
    picks = theirs[:, :, None, :] & (own(rank)[:, None, None, :] == wanted[:, None])
    got_cnt = jnp.sum(jnp.where(theirs, 1, 0), axis=-1)
    got_height = jnp.sum(jnp.where(theirs, own_rows, 0), axis=-1)
    alone = jnp.sum(jnp.where(theirs & ~own(both)[:, None, :], own_rows, 0), axis=-1)
    got_first = jnp.stack([jnp.zeros_like(alone[0]), alone[0]])
    plan = (got_cnt, got_first, got_height, pick(picks, own_rows), pick(picks, own_counts))
    return tuple(x.reshape(-1) for x in plan), picks, own(slots)


def attended_rows(
    hidden, norm_gain, w_query, query_gain, key_rows, value_rows, told, send_plan, lists, *, height, page_len
):
    head_size = query_gain.shape[0]
    kv_local = key_rows.shape[1] // head_size
    homes = lax.axis_size("cache")
    received = []
    for g in range(kv_local):
        heads = (told,) if g == 0 else ()
        out = pack(send_plan, heads, key_rows, value_rows, g, homes, height, page_len, head_size)
        if g > 0:
            out, received[-1] = lax.optimization_barrier((out, received[-1]))
        received.append(lax.all_to_all(out, "cache", split_axis=0, concat_axis=0, tiled=True))

    queries = project_queries(hidden, norm_gain, w_query, query_gain, kv_local)
    plan, own_picks, own_slots = home_plan(*lists)
    listed = own_slots.shape[-1]

    terms = received[0][:, height : height + 3, :].astype(jnp.float32)
    scales = (terms[:, 0] + terms[:, 1]) + terms[:, 2]
    pages_dev = key_rows.shape[0] // page_len
    scales = scales[:, : 2 * kv_local * pages_dev].reshape(homes, 2 * kv_local, pages_dev)
    scales = jnp.swapaxes(scales, 0, 1).reshape(2 * kv_local, homes * pages_dev)
    at_place = own_slots[..., None] == jnp.arange(homes * pages_dev, dtype=jnp.int32)
    found = [jnp.sum(jnp.where(at_place, scales[k], 0.0), axis=-1) for k in range(2 * kv_local)]
    found = [pick(own_picks, f[:, None, :]).reshape(-1) for f in found]

    attended = []
    for g in range(kv_local):
        full_plan = (*plan, found[g] * math.log2(math.e), found[kv_local + g])
        attended.append(attend(full_plan, queries[g], received[g], page_len, listed * page_len))
    return tuple(attended)


def body(
    hidden,
    norm_gain,
    w_query,
    query_gain,
    w_output,
    key_cache,
    value_cache,
    key_scale,
    value_scale,
    page_table,
    page_tokens,
    page_list,
    list_len,
):
    kv_local = key_scale.shape[2]
    pages_dev, page_len = key_cache.shape[1:3]
    listed = page_list.shape[2]
    shard_count = lax.axis_size("cache")
    own_shard = lax.axis_index("cache")

    told = jnp.concatenate([key_scale[0].T, value_scale[0].T], axis=0).reshape(-1)
    told = in_three(told)
    told = jnp.pad(told, ((0, GRANULE - 3), (0, key_cache.shape[3] // kv_local * 2 - told.shape[1])))

    entry = lookup(page_list[0], page_table * 128 + page_tokens)
    slots, counts = entry // 128, entry % 128
    used = jnp.arange(listed, dtype=jnp.int32) < list_len[0][:, None]
    rows = (counts + GRANULE - 1) // GRANULE * GRANULE
    homes = shard_count
    twin_slots = jnp.where(used, slots, -1).reshape(homes, QB_DEV, listed)[:, ::-1].reshape(-1, listed)
    both = jnp.any(slots[:, :, None] == twin_slots[:, None, :], axis=-1)
    second = (jnp.arange(homes * QB_DEV) % QB_DEV == 1)[:, None]
    shard, place = slots // pages_dev, slots % pages_dev
    order = jnp.where(used, place + jnp.where(both == second, 0, pages_dev), -1)
    earlier = (
        (shard[:, :, None] == shard[:, None, :])
        & used[:, :, None]
        & (order[:, :, None] < order[:, None, :])
    )
    rank = jnp.sum(jnp.where(earlier, 1, 0), axis=1)
    once = used & ~(both & second)
    sources = jnp.arange(shard_count, dtype=jnp.int32)
    at_source = shard[:, None, :] == sources[:, None]
    asked = jnp.sum(jnp.where(at_source & once[:, None, :], rows[:, None, :], 0), axis=-1)
    need = jnp.max(asked.reshape(homes, QB_DEV, shard_count).sum(axis=1))
    wanted = jnp.arange(MOST, dtype=jnp.int32)

    mine = (shard == own_shard) & once
    shared = jnp.sum(jnp.where(mine & both, 1, 0), axis=-1).reshape(homes, QB_DEV)[:, :1]
    behind = jnp.concatenate([jnp.zeros_like(shared), shared], axis=1).reshape(-1)
    picks = mine[:, None, :] & ((rank - behind[:, None])[:, None, :] == wanted[:, None])
    send_plan = (pick(picks, rows).reshape(-1), pick(picks, place).reshape(-1))

    devices = lax.axis_size("sections")
    agreed = need.astype(jnp.int32)[None]
    for step in range(1, devices):
        route = [(i, (i + step) % devices) for i in range(devices)]
        agreed = jnp.maximum(agreed, lax.ppermute(need.astype(jnp.int32)[None], "sections", route))
    agreed = agreed[0]

    key_rows = key_cache[0].reshape(pages_dev * page_len, -1)
    value_rows = value_cache[0].reshape(pages_dev * page_len, -1)
    most = QB_DEV * MOST * page_len
    heights = tuple(h for h in HEIGHTS if h < most) + (most,)
    branch = jnp.sum(jnp.where(agreed > jnp.array(heights[:-1], jnp.int32), 1, 0))
    send_plan, told, branch = lax.optimization_barrier((send_plan, told, branch))
    attended = lax.switch(
        branch,
        [functools.partial(attended_rows, height=h, page_len=page_len) for h in heights],
        hidden[0], norm_gain[0], w_query[0], query_gain[0], key_rows, value_rows, told, send_plan,
        (slots, counts, rows, used, both, rank, shard),
    )

    model_width = hidden.shape[2]
    heads_index = lax.axis_index("heads")
    half_width = model_width // lax.axis_size("heads")
    came, kept = [], []
    for b in range(QB_DEV):
        rows_here = slice(b * QBLOCK, (b + 1) * QBLOCK)
        both_heads = jnp.concatenate([a[rows_here] for a in attended], axis=1)
        if b > 0:
            both_heads, came[b - 1] = lax.optimization_barrier((both_heads, came[b - 1]))
        whole = jnp.dot(both_heads, w_output[0], preferred_element_type=jnp.float32)
        away = lax.dynamic_slice_in_dim(whole, (1 - heads_index) * half_width, half_width, 1)
        came.append(lax.ppermute(away.astype(jnp.bfloat16), "heads", [(0, 1), (1, 0)]))
        kept.append(lax.dynamic_slice_in_dim(whole, heads_index * half_width, half_width, 1))
    moved, result = [], None
    for b in range(QB_DEV):
        if result is not None:
            came[b], _ = lax.optimization_barrier((came[b], result))
        residual = lax.dynamic_slice(
            hidden[0], (b * QBLOCK, heads_index * half_width), (QBLOCK, half_width)
        ).astype(jnp.float32)
        result = (kept[b] + came[b].astype(jnp.float32) + residual).astype(jnp.bfloat16)
        moved.append(lax.ppermute(result, "sections", [((i - 1) % devices, i) for i in range(devices)]))
    return jnp.concatenate(moved, axis=0)[None]


def solution(mesh):
    return jax.shard_map(
        body,
        mesh=mesh,
        in_specs=(
            P("sections", "cache", None),
            P("sections", None),
            P("sections", None, "heads"),
            P("sections", None),
            P("sections", "heads", None),
            P("sections", "cache", None, "heads"),
            P("sections", "cache", None, "heads"),
            P("sections", "cache", "heads"),
            P("sections", "cache", "heads"),
            P(),
            P(),
            P("sections", None, None),
            P("sections", None),
        ),
        out_specs=P("sections", "cache", "heads"),
        check_vma=False,
    )
```

```python
import functools
import math

import jax
import jax.numpy as jnp
from jax import lax
from jax.experimental import pallas as pl
from jax.experimental.pallas import tpu as pltpu
from jax.sharding import PartitionSpec as P

QBLOCK = 128
QB_DEV = 2
MOST = 8
GRANULE = 8
GROUP = 2 * GRANULE
HEIGHTS = (544, 616)
BUFFERS = 8
CHUNK = 512
QTILE = 256

tiny_eps = 1e-06
masked_score = -1e30
lowest = -1e38


def lookup(entries, table):
    places = jnp.arange(table.shape[0], dtype=jnp.int32)
    return jnp.sum(jnp.where(entries[..., None] == places, table, 0), axis=-1)


def pick(picks, values):
    return jnp.sum(jnp.where(picks, values[..., None, :], 0), axis=-1)


def pack_kernel(rows_ref, page_ref, *refs, page_len, height):
    *head_refs, k_ref, v_ref, out_ref, mixed, buf, sems = refs
    homes = out_ref.shape[0]
    tokens, head_size = k_ref.shape
    page_rows, sent_rows = 2 * page_len, 2 * height
    for slot in range(BUFFERS):
        for head_ref in head_refs:
            buf[slot, pl.ds(page_rows + sent_rows, GROUP), :] = head_ref[...]

    def mix(p, carry):
        here = pl.ds(pl.multiple_of(p * page_len, page_len), page_len)
        keys, values = (
            ref[here, :].astype(jnp.float32).reshape(page_len // GRANULE, 1, GRANULE, head_size)
            for ref in (k_ref, v_ref)
        )
        pair = jnp.concatenate([keys, values], axis=1).reshape(page_rows, head_size)
        mixed[pl.ds(pl.multiple_of(p * page_rows, page_rows), page_rows), :] = pair.astype(jnp.bfloat16)
        return carry

    lax.fori_loop(0, tokens // page_len, mix, 0)

    def copies_of(home, slot):
        copies = [(0, sent_rows)] + [(page_rows + sent_rows, GROUP)] * len(head_refs)
        starts = (0, sent_rows)
        return [
            pltpu.make_async_copy(
                buf.at[slot, pl.ds(here, n), :], out_ref.at[home, pl.ds(there, n), :], sems.at[slot, i]
            )
            for i, ((here, n), there) in enumerate(zip(copies, starts))
        ]

    def one_home(home, carry):
        slot = lax.rem(home, BUFFERS)

        @pl.when(home >= BUFFERS)
        def _():
            for copy in copies_of(home - BUFFERS, slot):
                copy.wait()

        row = jnp.int32(0)
        for j in range(QB_DEV * MOST):
            at = home * (QB_DEV * MOST) + j
            here = pl.multiple_of(page_ref[at] * page_rows, page_rows)
            there = pl.multiple_of(row * 2, GROUP)
            buf[slot, pl.ds(there, page_rows), :] = mixed[pl.ds(here, page_rows), :]
            row = row + rows_ref[at]
        for copy in copies_of(home, slot):
            copy.start()
        return carry

    lax.fori_loop(0, homes, one_home, 0)
    for home in range(homes - BUFFERS, homes):
        for copy in copies_of(home, home % BUFFERS):
            copy.wait()


def pack(plan, heads, key_rows, value_rows, g, homes, height, page_len, head_size):
    tokens = key_rows.shape[0]
    sent = 2 * height + GROUP * len(heads)
    return pl.pallas_call(
        functools.partial(pack_kernel, page_len=page_len, height=height),
        grid_spec=pltpu.PrefetchScalarGridSpec(
            num_scalar_prefetch=2,
            grid=(1,),
            in_specs=[pl.BlockSpec(h.shape, lambda i, *_: (0, 0)) for h in heads]
            + [
                pl.BlockSpec((tokens, head_size), lambda i, *_: (0, g)),
                pl.BlockSpec((tokens, head_size), lambda i, *_: (0, g)),
            ],
            out_specs=pl.BlockSpec(memory_space=pltpu.HBM),
            scratch_shapes=[
                pltpu.VMEM((2 * tokens, head_size), jnp.bfloat16),
                pltpu.VMEM((BUFFERS, 2 * (height + page_len) + GROUP, head_size), jnp.bfloat16),
                pltpu.SemaphoreType.DMA((BUFFERS, 2)),
            ],
        ),
        out_shape=jax.ShapeDtypeStruct((homes, sent, head_size), jnp.bfloat16),
        compiler_params=pltpu.CompilerParams(vmem_limit_bytes=60 << 20),
        cost_estimate=pl.CostEstimate(
            flops=0, transcendentals=0, bytes_accessed=homes * sent * 2 * head_size + tokens * 4 * head_size
        ),
    )(*plan, *heads, key_rows, value_rows)


def attend_kernel(
    cnt_ref, first_ref, height_ref, rows_ref, live_ref, kscale_ref, vscale_ref,
    qt_ref, recv_ref, out_ref,
    kv, kcol, vcol, bias, acc, top, total, sems, *, page_len,
):
    sources = recv_ref.shape[0]
    head_size, width = qt_ref.shape[1:]
    lists = pl.program_id(0) * sources

    def copy_of(s, at):
        n = pl.multiple_of(height_ref[lists + s] * 2, GROUP)
        start = pl.multiple_of(first_ref[lists + s] * 2, GROUP)
        at = pl.multiple_of(at * 2, GROUP)
        return pltpu.make_async_copy(
            recv_ref.at[s, pl.ds(start, n), :], kv.at[pl.ds(at, n), :], sems.at[s]
        )

    def start_one(s, at):
        @pl.when(height_ref[lists + s] > 0)
        def _():
            copy_of(s, at).start()

        return at + height_ref[lists + s]

    def wait_one(s, at):
        @pl.when(height_ref[lists + s] > 0)
        def _():
            copy_of(s, at).wait()

        return at + height_ref[lists + s]

    used = lax.fori_loop(0, sources, start_one, jnp.int32(0))
    token = lax.broadcasted_iota(jnp.int32, (page_len, 128), 0)

    def columns_of(s, at):
        def one_page(j, at):
            e = (lists + s) * MOST + j
            here = pl.ds(pl.multiple_of(at, GRANULE), page_len)
            kcol[here, :] = jnp.full((page_len, 128), kscale_ref[e], jnp.float32)
            vcol[here, :] = jnp.full((page_len, 128), vscale_ref[e], jnp.float32)
            bias[here, :] = jnp.where(token < live_ref[e], 0.0, masked_score)
            return at + rows_ref[e]

        return lax.fori_loop(0, cnt_ref[lists + s], one_page, at)

    lax.fori_loop(0, sources, columns_of, jnp.int32(0))
    rest = pl.ds(pl.multiple_of(used, GRANULE), CHUNK)
    kcol[rest, :] = jnp.zeros((CHUNK, 128), jnp.float32)
    vcol[rest, :] = jnp.zeros((CHUNK, 128), jnp.float32)
    bias[rest, :] = jnp.full((CHUNK, 128), masked_score, jnp.float32)
    kv[pl.ds(pl.multiple_of(used * 2, GROUP), 2 * CHUNK), :] = jnp.zeros((2 * CHUNK, head_size), jnp.bfloat16)
    acc[...] = jnp.zeros_like(acc)
    total[...] = jnp.zeros_like(total)
    top[...] = jnp.full_like(top, lowest)
    lax.fori_loop(0, sources, wait_one, jnp.int32(0))

    def chunk(c, carry):
        here = pl.ds(pl.multiple_of(c * CHUNK, CHUNK), CHUNK)
        pair = kv[pl.ds(pl.multiple_of(c * 2 * CHUNK, 2 * CHUNK), 2 * CHUNK), :].astype(jnp.float32)
        pair = pair.reshape(CHUNK // GRANULE, 2, GRANULE, head_size)
        keys = pair[:, 0].reshape(CHUNK, head_size).astype(jnp.bfloat16)
        values = pair[:, 1].reshape(CHUNK, head_size).astype(jnp.bfloat16).T
        for i in range(width // QTILE):
            cols = pl.ds(i * QTILE, QTILE)
            score = jnp.dot(keys, qt_ref[0, :, cols], preferred_element_type=jnp.float32)
            kc, bc, vc = kcol[here, :], bias[here, :], vcol[here, :]
            wide = lambda x: jnp.concatenate([x] * (QTILE // 128), axis=1)
            score = score * wide(kc) + wide(bc)
            old = top[0:1, cols]
            new = jnp.maximum(old, jnp.max(score, axis=0, keepdims=True))
            weight = jnp.exp2(score - new)
            fade = jnp.exp2(old - new)
            total[0:1, cols] = total[0:1, cols] * fade + jnp.sum(weight, axis=0, keepdims=True)
            scaled = (weight * wide(vc)).astype(jnp.bfloat16)
            acc[:, cols] = acc[:, cols] * fade + jnp.dot(values, scaled, preferred_element_type=jnp.float32)
            top[0:1, cols] = new
        return carry

    lax.fori_loop(0, (used + CHUNK - 1) // CHUNK, chunk, 0)
    for h in range(width // QBLOCK):
        cols = slice(h * QBLOCK, (h + 1) * QBLOCK)
        out_ref[:, h * head_size : (h + 1) * head_size] = (acc[:, cols] / total[0:1, cols]).T.astype(jnp.bfloat16)


def attend(plan, qt, received, page_len, most_rows):
    blocks, head_size, width = qt.shape
    sources = received.shape[0]
    rows_held = most_rows + CHUNK + page_len
    out_width = width // QBLOCK * head_size
    return pl.pallas_call(
        functools.partial(attend_kernel, page_len=page_len),
        grid_spec=pltpu.PrefetchScalarGridSpec(
            num_scalar_prefetch=7,
            grid=(blocks,),
            in_specs=[
                pl.BlockSpec((1, head_size, width), lambda b, *_: (b, 0, 0)),
                pl.BlockSpec(memory_space=pltpu.HBM),
            ],
            out_specs=pl.BlockSpec((QBLOCK, out_width), lambda b, *_: (b, 0)),
            scratch_shapes=[
                pltpu.VMEM((2 * rows_held, head_size), jnp.bfloat16),
                pltpu.VMEM((rows_held, 128), jnp.float32),
                pltpu.VMEM((rows_held, 128), jnp.float32),
                pltpu.VMEM((rows_held, 128), jnp.float32),
                pltpu.VMEM((head_size, width), jnp.float32),
                pltpu.VMEM((8, width), jnp.float32),
                pltpu.VMEM((8, width), jnp.float32),
                pltpu.SemaphoreType.DMA((sources,)),
            ],
        ),
        out_shape=jax.ShapeDtypeStruct((blocks * QBLOCK, out_width), jnp.bfloat16),
        compiler_params=pltpu.CompilerParams(vmem_limit_bytes=24 << 20),
        cost_estimate=pl.CostEstimate(
            flops=4 * blocks * width * most_rows * head_size,
            transcendentals=blocks * width * most_rows,
            bytes_accessed=blocks * (most_rows + width) * 4 * head_size,
        ),
    )(*plan, qt, received)


def query_kernel(x_ref, gain_ref, w_ref, head_gain_ref, out_ref, normed):
    head_size = out_ref.shape[2]

    @pl.when(pl.program_id(0) == 0)
    def _():
        x = x_ref[...].astype(jnp.float32)
        inverse = lax.rsqrt(jnp.mean(x * x, axis=-1, keepdims=True) + tiny_eps)
        normed[...] = (x * inverse * gain_ref[...]).astype(jnp.bfloat16)

    projected = jnp.dot(normed[...], w_ref[...], preferred_element_type=jnp.float32)
    for h in range(w_ref.shape[1] // head_size):
        one = projected[:, h * head_size : (h + 1) * head_size]
        inverse = lax.rsqrt(jnp.mean(one * one, axis=-1, keepdims=True) + tiny_eps)
        query = (one * inverse * head_gain_ref[...] / math.sqrt(head_size)).T.astype(jnp.bfloat16)
        for b in range(QB_DEV):
            cols = slice(b * QBLOCK, (b + 1) * QBLOCK)
            out_ref[0, b, :, h * QBLOCK : (h + 1) * QBLOCK] = query[:, cols]


def project_queries(hidden, norm_gain, w_query, query_gain, kv_local):
    row_count, model_width = hidden.shape
    head_size = query_gain.shape[0]
    group_size = w_query.shape[1] // head_size // kv_local
    tile = 2 * head_size
    tiles = group_size // 2
    return pl.pallas_call(
        query_kernel,
        grid=(kv_local * tiles,),
        in_specs=[
            pl.BlockSpec((row_count, model_width), lambda i: (0, 0)),
            pl.BlockSpec((1, model_width), lambda i: (0, 0)),
            pl.BlockSpec((model_width, tile), lambda i: (0, i)),
            pl.BlockSpec((1, head_size), lambda i: (0, 0)),
        ],
        out_specs=pl.BlockSpec(
            (1, QB_DEV, head_size, 2 * QBLOCK), lambda i: (i // tiles, 0, 0, i % tiles)
        ),
        out_shape=jax.ShapeDtypeStruct((kv_local, QB_DEV, head_size, group_size * QBLOCK), jnp.bfloat16),
        scratch_shapes=[pltpu.VMEM((row_count, model_width), jnp.bfloat16)],
        compiler_params=pltpu.CompilerParams(vmem_limit_bytes=24 << 20),
        cost_estimate=pl.CostEstimate(
            flops=2 * row_count * model_width * w_query.shape[1],
            transcendentals=0,
            bytes_accessed=2 * (w_query.size + 2 * hidden.size),
        ),
    )(hidden, norm_gain[None], w_query, query_gain[None])


def in_three(x):
    high = lax.reduce_precision(x, 8, 7)
    middle = lax.reduce_precision(x - high, 8, 7)
    low = x - high - middle
    return jnp.stack([t.astype(jnp.bfloat16) for t in (high, middle, low)])


def home_plan(slots, counts, rows, used, both, rank, shard):
    shard_count = lax.axis_size("cache")
    first_block = lax.axis_index("cache") * QB_DEV

    def own(x):
        return lax.dynamic_slice_in_dim(x, first_block, QB_DEV, 0)

    own_counts, own_rows = own(counts)[:, None, :], own(rows)[:, None, :]
    sources = jnp.arange(shard_count, dtype=jnp.int32)
    theirs = (own(shard)[:, None, :] == sources[:, None]) & own(used)[:, None, :]
    wanted = jnp.arange(MOST, dtype=jnp.int32)
    picks = theirs[:, :, None, :] & (own(rank)[:, None, None, :] == wanted[:, None])
    got_cnt = jnp.sum(jnp.where(theirs, 1, 0), axis=-1)
    got_height = jnp.sum(jnp.where(theirs, own_rows, 0), axis=-1)
    alone = jnp.sum(jnp.where(theirs & ~own(both)[:, None, :], own_rows, 0), axis=-1)
    got_first = jnp.stack([jnp.zeros_like(alone[0]), alone[0]])
    plan = (got_cnt, got_first, got_height, pick(picks, own_rows), pick(picks, own_counts))
    return tuple(x.reshape(-1) for x in plan), picks, own(slots)


def attended_rows(
    hidden, norm_gain, w_query, query_gain, key_rows, value_rows, told, send_plan, lists, *, height, page_len
):
    head_size = query_gain.shape[0]
    kv_local = key_rows.shape[1] // head_size
    homes = lax.axis_size("cache")
    received = []
    for g in range(kv_local):
        heads = (told,) if g == 0 else ()
        out = pack(send_plan, heads, key_rows, value_rows, g, homes, height, page_len, head_size)
        if g > 0:
            out, received[-1] = lax.optimization_barrier((out, received[-1]))
        received.append(lax.all_to_all(out, "cache", split_axis=0, concat_axis=0, tiled=True))

    queries = project_queries(hidden, norm_gain, w_query, query_gain, kv_local)
    plan, own_picks, own_slots = home_plan(*lists)
    listed = own_slots.shape[-1]

    terms = received[0][:, 2 * height : 2 * height + 3, :].astype(jnp.float32)
    scales = (terms[:, 0] + terms[:, 1]) + terms[:, 2]
    pages_dev = key_rows.shape[0] // page_len
    scales = scales[:, : 2 * kv_local * pages_dev].reshape(homes, 2 * kv_local, pages_dev)
    scales = jnp.swapaxes(scales, 0, 1).reshape(2 * kv_local, homes * pages_dev)
    at_place = own_slots[..., None] == jnp.arange(homes * pages_dev, dtype=jnp.int32)
    found = [jnp.sum(jnp.where(at_place, scales[k], 0.0), axis=-1) for k in range(2 * kv_local)]
    found = [pick(own_picks, f[:, None, :]).reshape(-1) for f in found]

    attended = []
    for g in range(kv_local):
        full_plan = (*plan, found[g] * math.log2(math.e), found[kv_local + g])
        attended.append(attend(full_plan, queries[g], received[g], page_len, listed * page_len))
    return tuple(attended)


def body(
    hidden,
    norm_gain,
    w_query,
    query_gain,
    w_output,
    key_cache,
    value_cache,
    key_scale,
    value_scale,
    page_table,
    page_tokens,
    page_list,
    list_len,
):
    kv_local = key_scale.shape[2]
    pages_dev, page_len = key_cache.shape[1:3]
    listed = page_list.shape[2]
    shard_count = lax.axis_size("cache")
    own_shard = lax.axis_index("cache")

    told = jnp.concatenate([key_scale[0].T, value_scale[0].T], axis=0).reshape(-1)
    told = in_three(told)
    told = jnp.pad(told, ((0, GROUP - 3), (0, key_cache.shape[3] // kv_local - told.shape[1])))

    entry = lookup(page_list[0], page_table * 128 + page_tokens)
    slots, counts = entry // 128, entry % 128
    used = jnp.arange(listed, dtype=jnp.int32) < list_len[0][:, None]
    rows = (counts + GRANULE - 1) // GRANULE * GRANULE
    homes = shard_count
    twin_slots = jnp.where(used, slots, -1).reshape(homes, QB_DEV, listed)[:, ::-1].reshape(-1, listed)
    both = jnp.any(slots[:, :, None] == twin_slots[:, None, :], axis=-1)
    second = (jnp.arange(homes * QB_DEV) % QB_DEV == 1)[:, None]
    shard, place = slots // pages_dev, slots % pages_dev
    order = jnp.where(used, place + jnp.where(both == second, 0, pages_dev), -1)
    earlier = (
        (shard[:, :, None] == shard[:, None, :])
        & used[:, :, None]
        & (order[:, :, None] < order[:, None, :])
    )
    rank = jnp.sum(jnp.where(earlier, 1, 0), axis=1)
    once = used & ~(both & second)
    sources = jnp.arange(shard_count, dtype=jnp.int32)
    at_source = shard[:, None, :] == sources[:, None]
    asked = jnp.sum(jnp.where(at_source & once[:, None, :], rows[:, None, :], 0), axis=-1)
    need = jnp.max(asked.reshape(homes, QB_DEV, shard_count).sum(axis=1))
    wanted = jnp.arange(MOST, dtype=jnp.int32)

    mine = (shard == own_shard) & once
    shared = jnp.sum(jnp.where(mine & both, 1, 0), axis=-1).reshape(homes, QB_DEV)[:, :1]
    behind = jnp.concatenate([jnp.zeros_like(shared), shared], axis=1).reshape(-1)
    picks = mine[:, None, :] & ((rank - behind[:, None])[:, None, :] == wanted[:, None])
    send_plan = (pick(picks, rows).reshape(-1), pick(picks, place).reshape(-1))

    devices = lax.axis_size("sections")
    agreed = need.astype(jnp.int32)[None]
    for step in range(1, devices):
        route = [(i, (i + step) % devices) for i in range(devices)]
        agreed = jnp.maximum(agreed, lax.ppermute(need.astype(jnp.int32)[None], "sections", route))
    agreed = agreed[0]

    key_rows = key_cache[0].reshape(pages_dev * page_len, -1)
    value_rows = value_cache[0].reshape(pages_dev * page_len, -1)
    most = QB_DEV * MOST * page_len
    heights = tuple(h for h in HEIGHTS if h < most) + (most,)
    branch = jnp.sum(jnp.where(agreed > jnp.array(heights[:-1], jnp.int32), 1, 0))
    send_plan, told, branch = lax.optimization_barrier((send_plan, told, branch))
    attended = lax.switch(
        branch,
        [functools.partial(attended_rows, height=h, page_len=page_len) for h in heights],
        hidden[0], norm_gain[0], w_query[0], query_gain[0], key_rows, value_rows, told, send_plan,
        (slots, counts, rows, used, both, rank, shard),
    )

    model_width = hidden.shape[2]
    heads_index = lax.axis_index("heads")
    half_width = model_width // lax.axis_size("heads")
    came, kept = [], []
    for b in range(QB_DEV):
        rows_here = slice(b * QBLOCK, (b + 1) * QBLOCK)
        both_heads = jnp.concatenate([a[rows_here] for a in attended], axis=1)
        if b > 0:
            both_heads, came[b - 1] = lax.optimization_barrier((both_heads, came[b - 1]))
        whole = jnp.dot(both_heads, w_output[0], preferred_element_type=jnp.float32)
        away = lax.dynamic_slice_in_dim(whole, (1 - heads_index) * half_width, half_width, 1)
        came.append(lax.ppermute(away.astype(jnp.bfloat16), "heads", [(0, 1), (1, 0)]))
        kept.append(lax.dynamic_slice_in_dim(whole, heads_index * half_width, half_width, 1))
    moved, result = [], None
    for b in range(QB_DEV):
        if result is not None:
            came[b], _ = lax.optimization_barrier((came[b], result))
        residual = lax.dynamic_slice(
            hidden[0], (b * QBLOCK, heads_index * half_width), (QBLOCK, half_width)
        ).astype(jnp.float32)
        result = (kept[b] + came[b].astype(jnp.float32) + residual).astype(jnp.bfloat16)
        moved.append(lax.ppermute(result, "sections", [((i - 1) % devices, i) for i in range(devices)]))
    return jnp.concatenate(moved, axis=0)[None]


def solution(mesh):
    return jax.shard_map(
        body,
        mesh=mesh,
        in_specs=(
            P("sections", "cache", None),
            P("sections", None),
            P("sections", None, "heads"),
            P("sections", None),
            P("sections", "heads", None),
            P("sections", "cache", None, "heads"),
            P("sections", "cache", None, "heads"),
            P("sections", "cache", "heads"),
            P("sections", "cache", "heads"),
            P(),
            P(),
            P("sections", None, None),
            P("sections", None),
        ),
        out_specs=P("sections", "cache", "heads"),
        check_vma=False,
    )
```

```python
import functools
import math

import jax
import jax.numpy as jnp
from jax import lax
from jax.experimental import pallas as pl
from jax.experimental.pallas import tpu as pltpu
from jax.sharding import PartitionSpec as P

QBLOCK = 128
QB_DEV = 2
MOST = 8
GRANULE = 8
GROUP = 2 * GRANULE
HEIGHTS = (544, 576, 664)
BUFFERS = 8
CHUNK = 256
QTILE = 256

tiny_eps = 1e-06
masked_score = -1e30
lowest = -1e38


def lookup(entries, table):
    places = jnp.arange(table.shape[0], dtype=jnp.int32)
    return jnp.sum(jnp.where(entries[..., None] == places, table, 0), axis=-1)


def pick(picks, values):
    return jnp.sum(jnp.where(picks, values[..., None, :], 0), axis=-1)


def pack_kernel(rows_ref, page_ref, *refs, page_len, height):
    *head_refs, k_ref, v_ref, out_ref, mixed, buf, sems = refs
    homes = out_ref.shape[0]
    tokens, head_size = k_ref.shape
    page_rows, sent_rows = 2 * page_len, 2 * height
    for slot in range(BUFFERS):
        for head_ref in head_refs:
            buf[slot, pl.ds(page_rows + sent_rows, GROUP), :] = head_ref[...]

    def mix(p, carry):
        here = pl.ds(pl.multiple_of(p * page_len, page_len), page_len)
        keys, values = (
            ref[here, :].astype(jnp.float32).reshape(page_len // GRANULE, 1, GRANULE, head_size)
            for ref in (k_ref, v_ref)
        )
        pair = jnp.concatenate([keys, values], axis=1).reshape(page_rows, head_size)
        mixed[pl.ds(pl.multiple_of(p * page_rows, page_rows), page_rows), :] = pair.astype(jnp.bfloat16)
        return carry

    lax.fori_loop(0, tokens // page_len, mix, 0)

    def copies_of(home, slot):
        copies = [(0, sent_rows)] + [(page_rows + sent_rows, GROUP)] * len(head_refs)
        starts = (0, sent_rows)
        return [
            pltpu.make_async_copy(
                buf.at[slot, pl.ds(here, n), :], out_ref.at[home, pl.ds(there, n), :], sems.at[slot, i]
            )
            for i, ((here, n), there) in enumerate(zip(copies, starts))
        ]

    def one_home(home, carry):
        slot = lax.rem(home, BUFFERS)

        @pl.when(home >= BUFFERS)
        def _():
            for copy in copies_of(home - BUFFERS, slot):
                copy.wait()

        row = jnp.int32(0)
        for j in range(QB_DEV * MOST):
            at = home * (QB_DEV * MOST) + j
            here = pl.multiple_of(page_ref[at] * page_rows, page_rows)
            there = pl.multiple_of(row * 2, GROUP)
            buf[slot, pl.ds(there, page_rows), :] = mixed[pl.ds(here, page_rows), :]
            row = row + rows_ref[at]
        for copy in copies_of(home, slot):
            copy.start()
        return carry

    lax.fori_loop(0, homes, one_home, 0)
    for home in range(homes - BUFFERS, homes):
        for copy in copies_of(home, home % BUFFERS):
            copy.wait()


def pack(plan, heads, key_rows, value_rows, g, homes, height, page_len, head_size):
    tokens = key_rows.shape[0]
    sent = 2 * height + GROUP * len(heads)
    return pl.pallas_call(
        functools.partial(pack_kernel, page_len=page_len, height=height),
        grid_spec=pltpu.PrefetchScalarGridSpec(
            num_scalar_prefetch=2,
            grid=(1,),
            in_specs=[pl.BlockSpec(h.shape, lambda i, *_: (0, 0)) for h in heads]
            + [
                pl.BlockSpec((tokens, head_size), lambda i, *_: (0, g)),
                pl.BlockSpec((tokens, head_size), lambda i, *_: (0, g)),
            ],
            out_specs=pl.BlockSpec(memory_space=pltpu.HBM),
            scratch_shapes=[
                pltpu.VMEM((2 * tokens, head_size), jnp.bfloat16),
                pltpu.VMEM((BUFFERS, 2 * (height + page_len) + GROUP, head_size), jnp.bfloat16),
                pltpu.SemaphoreType.DMA((BUFFERS, 2)),
            ],
        ),
        out_shape=jax.ShapeDtypeStruct((homes, sent, head_size), jnp.bfloat16),
        compiler_params=pltpu.CompilerParams(vmem_limit_bytes=60 << 20),
        cost_estimate=pl.CostEstimate(
            flops=0, transcendentals=0, bytes_accessed=homes * sent * 2 * head_size + tokens * 4 * head_size
        ),
    )(*plan, *heads, key_rows, value_rows)


def attend_kernel(
    cnt_ref, first_ref, height_ref, rows_ref, live_ref, kscale_ref, vscale_ref,
    qt_ref, recv_ref, out_ref,
    kv, kcol, vcol, bias, acc, top, total, sems, *, page_len,
):
    sources = recv_ref.shape[0]
    head_size, width = qt_ref.shape[1:]
    lists = pl.program_id(0) * sources

    def copy_of(s, at):
        n = pl.multiple_of(height_ref[lists + s] * 2, GROUP)
        start = pl.multiple_of(first_ref[lists + s] * 2, GROUP)
        at = pl.multiple_of(at * 2, GROUP)
        return pltpu.make_async_copy(
            recv_ref.at[s, pl.ds(start, n), :], kv.at[pl.ds(at, n), :], sems.at[s]
        )

    def start_one(s, at):
        @pl.when(height_ref[lists + s] > 0)
        def _():
            copy_of(s, at).start()

        return at + height_ref[lists + s]

    def wait_one(s, at):
        @pl.when(height_ref[lists + s] > 0)
        def _():
            copy_of(s, at).wait()

        return at + height_ref[lists + s]

    used = lax.fori_loop(0, sources, start_one, jnp.int32(0))
    token = lax.broadcasted_iota(jnp.int32, (page_len, 128), 0)

    def columns_of(s, at):
        def one_page(j, at):
            e = (lists + s) * MOST + j
            here = pl.ds(pl.multiple_of(at, GRANULE), page_len)
            kcol[here, :] = jnp.full((page_len, 128), kscale_ref[e], jnp.float32)
            vcol[here, :] = jnp.full((page_len, 128), vscale_ref[e], jnp.float32)
            bias[here, :] = jnp.where(token < live_ref[e], 0.0, masked_score)
            return at + rows_ref[e]

        return lax.fori_loop(0, cnt_ref[lists + s], one_page, at)

    lax.fori_loop(0, sources, columns_of, jnp.int32(0))
    rest = pl.ds(pl.multiple_of(used, GRANULE), CHUNK)
    kcol[rest, :] = jnp.zeros((CHUNK, 128), jnp.float32)
    vcol[rest, :] = jnp.zeros((CHUNK, 128), jnp.float32)
    bias[rest, :] = jnp.full((CHUNK, 128), masked_score, jnp.float32)
    kv[pl.ds(pl.multiple_of(used * 2, GROUP), 2 * CHUNK), :] = jnp.zeros((2 * CHUNK, head_size), jnp.bfloat16)
    acc[...] = jnp.zeros_like(acc)
    total[...] = jnp.zeros_like(total)
    top[...] = jnp.full_like(top, lowest)
    lax.fori_loop(0, sources, wait_one, jnp.int32(0))

    def chunk(c, carry):
        here = pl.ds(pl.multiple_of(c * CHUNK, CHUNK), CHUNK)
        pair = kv[pl.ds(pl.multiple_of(c * 2 * CHUNK, 2 * CHUNK), 2 * CHUNK), :].astype(jnp.float32)
        pair = pair.reshape(CHUNK // GRANULE, 2, GRANULE, head_size)
        keys = pair[:, 0].reshape(CHUNK, head_size).astype(jnp.bfloat16)
        values = pair[:, 1].reshape(CHUNK, head_size).astype(jnp.bfloat16).T
        for i in range(width // QTILE):
            cols = pl.ds(i * QTILE, QTILE)
            score = jnp.dot(keys, qt_ref[0, :, cols], preferred_element_type=jnp.float32)
            kc, bc, vc = kcol[here, :], bias[here, :], vcol[here, :]
            wide = lambda x: jnp.concatenate([x] * (QTILE // 128), axis=1)
            score = score * wide(kc) + wide(bc)
            old = top[0:1, cols]
            new = jnp.maximum(old, jnp.max(score, axis=0, keepdims=True))
            weight = jnp.exp2(score - new)
            fade = jnp.exp2(old - new)
            total[0:1, cols] = total[0:1, cols] * fade + jnp.sum(weight, axis=0, keepdims=True)
            scaled = (weight * wide(vc)).astype(jnp.bfloat16)
            acc[:, cols] = acc[:, cols] * fade + jnp.dot(values, scaled, preferred_element_type=jnp.float32)
            top[0:1, cols] = new
        return carry

    lax.fori_loop(0, (used + CHUNK - 1) // CHUNK, chunk, 0)
    for h in range(width // QBLOCK):
        cols = slice(h * QBLOCK, (h + 1) * QBLOCK)
        out_ref[:, h * head_size : (h + 1) * head_size] = (acc[:, cols] / total[0:1, cols]).T.astype(jnp.bfloat16)


def attend(plan, qt, received, page_len, most_rows):
    blocks, head_size, width = qt.shape
    sources = received.shape[0]
    rows_held = most_rows + CHUNK + page_len
    out_width = width // QBLOCK * head_size
    return pl.pallas_call(
        functools.partial(attend_kernel, page_len=page_len),
        grid_spec=pltpu.PrefetchScalarGridSpec(
            num_scalar_prefetch=7,
            grid=(blocks,),
            in_specs=[
                pl.BlockSpec((1, head_size, width), lambda b, *_: (b, 0, 0)),
                pl.BlockSpec(memory_space=pltpu.HBM),
            ],
            out_specs=pl.BlockSpec((QBLOCK, out_width), lambda b, *_: (b, 0)),
            scratch_shapes=[
                pltpu.VMEM((2 * rows_held, head_size), jnp.bfloat16),
                pltpu.VMEM((rows_held, 128), jnp.float32),
                pltpu.VMEM((rows_held, 128), jnp.float32),
                pltpu.VMEM((rows_held, 128), jnp.float32),
                pltpu.VMEM((head_size, width), jnp.float32),
                pltpu.VMEM((8, width), jnp.float32),
                pltpu.VMEM((8, width), jnp.float32),
                pltpu.SemaphoreType.DMA((sources,)),
            ],
        ),
        out_shape=jax.ShapeDtypeStruct((blocks * QBLOCK, out_width), jnp.bfloat16),
        compiler_params=pltpu.CompilerParams(vmem_limit_bytes=24 << 20),
        cost_estimate=pl.CostEstimate(
            flops=4 * blocks * width * most_rows * head_size,
            transcendentals=blocks * width * most_rows,
            bytes_accessed=blocks * (most_rows + width) * 4 * head_size,
        ),
    )(*plan, qt, received)


def query_kernel(x_ref, gain_ref, w_ref, head_gain_ref, out_ref, normed):
    head_size = out_ref.shape[2]

    @pl.when(pl.program_id(0) == 0)
    def _():
        x = x_ref[...].astype(jnp.float32)
        inverse = lax.rsqrt(jnp.mean(x * x, axis=-1, keepdims=True) + tiny_eps)
        normed[...] = (x * inverse * gain_ref[...]).astype(jnp.bfloat16)

    projected = jnp.dot(normed[...], w_ref[...], preferred_element_type=jnp.float32)
    for h in range(w_ref.shape[1] // head_size):
        one = projected[:, h * head_size : (h + 1) * head_size]
        inverse = lax.rsqrt(jnp.mean(one * one, axis=-1, keepdims=True) + tiny_eps)
        query = (one * inverse * head_gain_ref[...] / math.sqrt(head_size)).T.astype(jnp.bfloat16)
        for b in range(QB_DEV):
            cols = slice(b * QBLOCK, (b + 1) * QBLOCK)
            out_ref[0, b, :, h * QBLOCK : (h + 1) * QBLOCK] = query[:, cols]


def project_queries(hidden, norm_gain, w_query, query_gain, kv_local):
    row_count, model_width = hidden.shape
    head_size = query_gain.shape[0]
    group_size = w_query.shape[1] // head_size // kv_local
    tile = 2 * head_size
    tiles = group_size // 2
    return pl.pallas_call(
        query_kernel,
        grid=(kv_local * tiles,),
        in_specs=[
            pl.BlockSpec((row_count, model_width), lambda i: (0, 0)),
            pl.BlockSpec((1, model_width), lambda i: (0, 0)),
            pl.BlockSpec((model_width, tile), lambda i: (0, i)),
            pl.BlockSpec((1, head_size), lambda i: (0, 0)),
        ],
        out_specs=pl.BlockSpec(
            (1, QB_DEV, head_size, 2 * QBLOCK), lambda i: (i // tiles, 0, 0, i % tiles)
        ),
        out_shape=jax.ShapeDtypeStruct((kv_local, QB_DEV, head_size, group_size * QBLOCK), jnp.bfloat16),
        scratch_shapes=[pltpu.VMEM((row_count, model_width), jnp.bfloat16)],
        compiler_params=pltpu.CompilerParams(vmem_limit_bytes=24 << 20),
        cost_estimate=pl.CostEstimate(
            flops=2 * row_count * model_width * w_query.shape[1],
            transcendentals=0,
            bytes_accessed=2 * (w_query.size + 2 * hidden.size),
        ),
    )(hidden, norm_gain[None], w_query, query_gain[None])


def in_three(x):
    high = lax.reduce_precision(x, 8, 7)
    middle = lax.reduce_precision(x - high, 8, 7)
    low = x - high - middle
    return jnp.stack([t.astype(jnp.bfloat16) for t in (high, middle, low)])


def home_plan(slots, counts, rows, used, both, rank, shard):
    shard_count = lax.axis_size("cache")
    first_block = lax.axis_index("cache") * QB_DEV

    def own(x):
        return lax.dynamic_slice_in_dim(x, first_block, QB_DEV, 0)

    own_counts, own_rows = own(counts)[:, None, :], own(rows)[:, None, :]
    sources = jnp.arange(shard_count, dtype=jnp.int32)
    theirs = (own(shard)[:, None, :] == sources[:, None]) & own(used)[:, None, :]
    wanted = jnp.arange(MOST, dtype=jnp.int32)
    picks = theirs[:, :, None, :] & (own(rank)[:, None, None, :] == wanted[:, None])
    got_cnt = jnp.sum(jnp.where(theirs, 1, 0), axis=-1)
    got_height = jnp.sum(jnp.where(theirs, own_rows, 0), axis=-1)
    alone = jnp.sum(jnp.where(theirs & ~own(both)[:, None, :], own_rows, 0), axis=-1)
    got_first = jnp.stack([jnp.zeros_like(alone[0]), alone[0]])
    plan = (got_cnt, got_first, got_height, pick(picks, own_rows), pick(picks, own_counts))
    return tuple(x.reshape(-1) for x in plan), picks, own(slots)


def attended_rows(
    hidden, norm_gain, w_query, query_gain, key_rows, value_rows, told, send_plan, lists, *, height, page_len
):
    head_size = query_gain.shape[0]
    kv_local = key_rows.shape[1] // head_size
    homes = lax.axis_size("cache")
    received = []
    for g in range(kv_local):
        heads = (told,) if g == 0 else ()
        out = pack(send_plan, heads, key_rows, value_rows, g, homes, height, page_len, head_size)
        if g > 0:
            out, received[-1] = lax.optimization_barrier((out, received[-1]))
        received.append(lax.all_to_all(out, "cache", split_axis=0, concat_axis=0, tiled=True))

    queries = project_queries(hidden, norm_gain, w_query, query_gain, kv_local)
    plan, own_picks, own_slots = lists
    listed = own_slots.shape[-1]

    terms = received[0][:, 2 * height : 2 * height + 3, :].astype(jnp.float32)
    scales = (terms[:, 0] + terms[:, 1]) + terms[:, 2]
    pages_dev = key_rows.shape[0] // page_len
    scales = scales[:, : 2 * kv_local * pages_dev].reshape(homes, 2 * kv_local, pages_dev)
    scales = jnp.swapaxes(scales, 0, 1).reshape(2 * kv_local, homes * pages_dev)
    at_place = own_slots[..., None] == jnp.arange(homes * pages_dev, dtype=jnp.int32)
    found = [jnp.sum(jnp.where(at_place, scales[k], 0.0), axis=-1) for k in range(2 * kv_local)]
    found = [pick(own_picks, f[:, None, :]).reshape(-1) for f in found]

    attended = []
    for g in range(kv_local):
        full_plan = (*plan, found[g] * math.log2(math.e), found[kv_local + g])
        attended.append(attend(full_plan, queries[g], received[g], page_len, listed * page_len))
    return tuple(attended)


def body(
    hidden,
    norm_gain,
    w_query,
    query_gain,
    w_output,
    key_cache,
    value_cache,
    key_scale,
    value_scale,
    page_table,
    page_tokens,
    page_list,
    list_len,
):
    kv_local = key_scale.shape[2]
    pages_dev, page_len = key_cache.shape[1:3]
    listed = page_list.shape[2]
    shard_count = lax.axis_size("cache")
    own_shard = lax.axis_index("cache")

    told = jnp.concatenate([key_scale[0].T, value_scale[0].T], axis=0).reshape(-1)
    told = in_three(told)
    told = jnp.pad(told, ((0, GROUP - 3), (0, key_cache.shape[3] // kv_local - told.shape[1])))

    entry = lookup(page_list[0], page_table * 128 + page_tokens)
    slots, counts = entry // 128, entry % 128
    used = jnp.arange(listed, dtype=jnp.int32) < list_len[0][:, None]
    rows = (counts + GRANULE - 1) // GRANULE * GRANULE
    homes = shard_count
    twin_slots = jnp.where(used, slots, -1).reshape(homes, QB_DEV, listed)[:, ::-1].reshape(-1, listed)
    both = jnp.any(slots[:, :, None] == twin_slots[:, None, :], axis=-1)
    second = (jnp.arange(homes * QB_DEV) % QB_DEV == 1)[:, None]
    shard, place = slots // pages_dev, slots % pages_dev
    order = jnp.where(used, place + jnp.where(both == second, 0, pages_dev), -1)
    earlier = (
        (shard[:, :, None] == shard[:, None, :])
        & used[:, :, None]
        & (order[:, :, None] < order[:, None, :])
    )
    rank = jnp.sum(jnp.where(earlier, 1, 0), axis=1)
    once = used & ~(both & second)
    sources = jnp.arange(shard_count, dtype=jnp.int32)
    at_source = shard[:, None, :] == sources[:, None]
    asked = jnp.sum(jnp.where(at_source & once[:, None, :], rows[:, None, :], 0), axis=-1)
    need = jnp.max(asked.reshape(homes, QB_DEV, shard_count).sum(axis=1))
    wanted = jnp.arange(MOST, dtype=jnp.int32)

    mine = (shard == own_shard) & once
    shared = jnp.sum(jnp.where(mine & both, 1, 0), axis=-1).reshape(homes, QB_DEV)[:, :1]
    behind = jnp.concatenate([jnp.zeros_like(shared), shared], axis=1).reshape(-1)
    picks = mine[:, None, :] & ((rank - behind[:, None])[:, None, :] == wanted[:, None])
    send_plan = (pick(picks, rows).reshape(-1), pick(picks, place).reshape(-1))

    devices = lax.axis_size("sections")
    agreed = need.astype(jnp.int32)[None]
    for step in range(1, devices):
        route = [(i, (i + step) % devices) for i in range(devices)]
        agreed = jnp.maximum(agreed, lax.ppermute(need.astype(jnp.int32)[None], "sections", route))
    agreed = agreed[0]

    key_rows = key_cache[0].reshape(pages_dev * page_len, -1)
    value_rows = value_cache[0].reshape(pages_dev * page_len, -1)
    most = QB_DEV * MOST * page_len
    heights = tuple(h for h in HEIGHTS if h < most) + (most,)
    branch = jnp.sum(jnp.where(agreed > jnp.array(heights[:-1], jnp.int32), 1, 0))
    send_plan, told, branch = lax.optimization_barrier((send_plan, told, branch))
    attended = lax.switch(
        branch,
        [functools.partial(attended_rows, height=h, page_len=page_len) for h in heights],
        hidden[0], norm_gain[0], w_query[0], query_gain[0], key_rows, value_rows, told, send_plan,
        home_plan(slots, counts, rows, used, both, rank, shard),
    )

    model_width = hidden.shape[2]
    heads_index = lax.axis_index("heads")
    half_width = model_width // lax.axis_size("heads")
    came, kept = [], []
    for b in range(QB_DEV):
        rows_here = slice(b * QBLOCK, (b + 1) * QBLOCK)
        both_heads = jnp.concatenate([a[rows_here] for a in attended], axis=1)
        if b > 0:
            both_heads, came[b - 1] = lax.optimization_barrier((both_heads, came[b - 1]))
        whole = jnp.dot(both_heads, w_output[0], preferred_element_type=jnp.float32)
        away = lax.dynamic_slice_in_dim(whole, (1 - heads_index) * half_width, half_width, 1)
        came.append(lax.ppermute(away.astype(jnp.bfloat16), "heads", [(0, 1), (1, 0)]))
        kept.append(lax.dynamic_slice_in_dim(whole, heads_index * half_width, half_width, 1))
    moved, result = [], None
    for b in range(QB_DEV):
        if result is not None:
            came[b], _ = lax.optimization_barrier((came[b], result))
        residual = lax.dynamic_slice(
            hidden[0], (b * QBLOCK, heads_index * half_width), (QBLOCK, half_width)
        ).astype(jnp.float32)
        result = (kept[b] + came[b].astype(jnp.float32) + residual).astype(jnp.bfloat16)
        moved.append(lax.ppermute(result, "sections", [((i - 1) % devices, i) for i in range(devices)]))
    return jnp.concatenate(moved, axis=0)[None]


def solution(mesh):
    return jax.shard_map(
        body,
        mesh=mesh,
        in_specs=(
            P("sections", "cache", None),
            P("sections", None),
            P("sections", None, "heads"),
            P("sections", None),
            P("sections", "heads", None),
            P("sections", "cache", None, "heads"),
            P("sections", "cache", None, "heads"),
            P("sections", "cache", "heads"),
            P("sections", "cache", "heads"),
            P(),
            P(),
            P("sections", None, None),
            P("sections", None),
        ),
        out_specs=P("sections", "cache", "heads"),
        check_vma=False,
    )
```

```python
import functools
import math

import jax
import jax.numpy as jnp
from jax import lax
from jax.experimental import pallas as pl
from jax.experimental.pallas import tpu as pltpu
from jax.sharding import PartitionSpec as P

QBLOCK = 128
QB_DEV = 2
MOST = 8
GRANULE = 8
GROUP = 2 * GRANULE
HEIGHTS = (576, 656)
BUFFERS = 8
CHUNK = 512
QTILE = 256

tiny_eps = 1e-06
masked_score = -1e30
lowest = -1e38


def lookup(entries, table):
    places = jnp.arange(table.shape[0], dtype=jnp.int32)
    return jnp.sum(jnp.where(entries[..., None] == places, table, 0), axis=-1)


def pick(picks, values):
    return jnp.sum(jnp.where(picks, values[..., None, :], 0), axis=-1)


def pack_kernel(rows_ref, page_ref, *refs, page_len, height):
    *head_refs, k_ref, v_ref, out_ref, mixed, buf, sems = refs
    homes = out_ref.shape[0]
    tokens, head_size = k_ref.shape
    page_rows, sent_rows = 2 * page_len, 2 * height
    for slot in range(BUFFERS):
        for head_ref in head_refs:
            buf[slot, pl.ds(page_rows + sent_rows, GROUP), :] = head_ref[...]

    def mix(p, carry):
        here = pl.ds(pl.multiple_of(p * page_len, page_len), page_len)
        keys, values = (
            ref[here, :].astype(jnp.float32).reshape(page_len // GRANULE, 1, GRANULE, head_size)
            for ref in (k_ref, v_ref)
        )
        pair = jnp.concatenate([keys, values], axis=1).reshape(page_rows, head_size)
        mixed[pl.ds(pl.multiple_of(p * page_rows, page_rows), page_rows), :] = pair.astype(jnp.bfloat16)
        return carry

    lax.fori_loop(0, tokens // page_len, mix, 0)

    def copies_of(home, slot):
        copies = [(0, sent_rows)] + [(page_rows + sent_rows, GROUP)] * len(head_refs)
        starts = (0, sent_rows)
        return [
            pltpu.make_async_copy(
                buf.at[slot, pl.ds(here, n), :], out_ref.at[home, pl.ds(there, n), :], sems.at[slot, i]
            )
            for i, ((here, n), there) in enumerate(zip(copies, starts))
        ]

    def one_home(home, carry):
        slot = lax.rem(home, BUFFERS)

        @pl.when(home >= BUFFERS)
        def _():
            for copy in copies_of(home - BUFFERS, slot):
                copy.wait()

        row = jnp.int32(0)
        for j in range(QB_DEV * MOST):
            at = home * (QB_DEV * MOST) + j
            here = pl.multiple_of(page_ref[at] * page_rows, page_rows)
            there = pl.multiple_of(row * 2, GROUP)
            buf[slot, pl.ds(there, page_rows), :] = mixed[pl.ds(here, page_rows), :]
            row = row + rows_ref[at]
        for copy in copies_of(home, slot):
            copy.start()
        return carry

    lax.fori_loop(0, homes, one_home, 0)
    for home in range(homes - BUFFERS, homes):
        for copy in copies_of(home, home % BUFFERS):
            copy.wait()


def pack(plan, heads, key_rows, value_rows, g, homes, height, page_len, head_size):
    tokens = key_rows.shape[0]
    sent = 2 * height + GROUP * len(heads)
    return pl.pallas_call(
        functools.partial(pack_kernel, page_len=page_len, height=height),
        grid_spec=pltpu.PrefetchScalarGridSpec(
            num_scalar_prefetch=2,
            grid=(1,),
            in_specs=[pl.BlockSpec(h.shape, lambda i, *_: (0, 0)) for h in heads]
            + [
                pl.BlockSpec((tokens, head_size), lambda i, *_: (0, g)),
                pl.BlockSpec((tokens, head_size), lambda i, *_: (0, g)),
            ],
            out_specs=pl.BlockSpec(memory_space=pltpu.HBM),
            scratch_shapes=[
                pltpu.VMEM((2 * tokens, head_size), jnp.bfloat16),
                pltpu.VMEM((BUFFERS, 2 * (height + page_len) + GROUP, head_size), jnp.bfloat16),
                pltpu.SemaphoreType.DMA((BUFFERS, 2)),
            ],
        ),
        out_shape=jax.ShapeDtypeStruct((homes, sent, head_size), jnp.bfloat16),
        compiler_params=pltpu.CompilerParams(vmem_limit_bytes=60 << 20),
        cost_estimate=pl.CostEstimate(
            flops=0, transcendentals=0, bytes_accessed=homes * sent * 2 * head_size + tokens * 4 * head_size
        ),
    )(*plan, *heads, key_rows, value_rows)


def attend_kernel(
    cnt_ref, first_ref, height_ref, rows_ref, live_ref, kscale_ref, vscale_ref,
    qt_ref, recv_ref, out_ref,
    kv, kcol, vcol, bias, acc, top, total, sems, *, page_len,
):
    sources = recv_ref.shape[0]
    head_size, width = qt_ref.shape[1:]
    lists = pl.program_id(0) * sources

    def copy_of(s, at):
        n = pl.multiple_of(height_ref[lists + s] * 2, GROUP)
        start = pl.multiple_of(first_ref[lists + s] * 2, GROUP)
        at = pl.multiple_of(at * 2, GROUP)
        return pltpu.make_async_copy(
            recv_ref.at[s, pl.ds(start, n), :], kv.at[pl.ds(at, n), :], sems.at[s]
        )

    def start_one(s, at):
        @pl.when(height_ref[lists + s] > 0)
        def _():
            copy_of(s, at).start()

        return at + height_ref[lists + s]

    def wait_one(s, at):
        @pl.when(height_ref[lists + s] > 0)
        def _():
            copy_of(s, at).wait()

        return at + height_ref[lists + s]

    used = lax.fori_loop(0, sources, start_one, jnp.int32(0))
    token = lax.broadcasted_iota(jnp.int32, (page_len, 128), 0)

    def columns_of(s, at):
        def one_page(j, at):
            e = (lists + s) * MOST + j
            here = pl.ds(pl.multiple_of(at, GRANULE), page_len)
            kcol[here, :] = jnp.full((page_len, 128), kscale_ref[e], jnp.float32)
            vcol[here, :] = jnp.full((page_len, 128), vscale_ref[e], jnp.float32)
            bias[here, :] = jnp.where(token < live_ref[e], 0.0, masked_score)
            return at + rows_ref[e]

        return lax.fori_loop(0, cnt_ref[lists + s], one_page, at)

    lax.fori_loop(0, sources, columns_of, jnp.int32(0))
    rest = pl.ds(pl.multiple_of(used, GRANULE), CHUNK)
    kcol[rest, :] = jnp.zeros((CHUNK, 128), jnp.float32)
    vcol[rest, :] = jnp.zeros((CHUNK, 128), jnp.float32)
    bias[rest, :] = jnp.full((CHUNK, 128), masked_score, jnp.float32)
    kv[pl.ds(pl.multiple_of(used * 2, GROUP), 2 * CHUNK), :] = jnp.zeros((2 * CHUNK, head_size), jnp.bfloat16)
    acc[...] = jnp.zeros_like(acc)
    total[...] = jnp.zeros_like(total)
    top[...] = jnp.full_like(top, lowest)
    lax.fori_loop(0, sources, wait_one, jnp.int32(0))

    def chunk(c, carry):
        here = pl.ds(pl.multiple_of(c * CHUNK, CHUNK), CHUNK)
        pair = kv[pl.ds(pl.multiple_of(c * 2 * CHUNK, 2 * CHUNK), 2 * CHUNK), :].astype(jnp.float32)
        pair = pair.reshape(CHUNK // GRANULE, 2, GRANULE, head_size)
        keys = pair[:, 0].reshape(CHUNK, head_size).astype(jnp.bfloat16)
        values = pair[:, 1].reshape(CHUNK, head_size).astype(jnp.bfloat16).T
        for i in range(width // QTILE):
            cols = pl.ds(i * QTILE, QTILE)
            score = jnp.dot(keys, qt_ref[0, :, cols], preferred_element_type=jnp.float32)
            kc, bc, vc = kcol[here, :], bias[here, :], vcol[here, :]
            wide = lambda x: jnp.concatenate([x] * (QTILE // 128), axis=1)
            score = score * wide(kc) + wide(bc)
            old = top[0:1, cols]
            new = jnp.maximum(old, jnp.max(score, axis=0, keepdims=True))
            weight = jnp.exp2(score - new)
            fade = jnp.exp2(old - new)
            total[0:1, cols] = total[0:1, cols] * fade + jnp.sum(weight, axis=0, keepdims=True)
            scaled = (weight * wide(vc)).astype(jnp.bfloat16)
            acc[:, cols] = acc[:, cols] * fade + jnp.dot(values, scaled, preferred_element_type=jnp.float32)
            top[0:1, cols] = new
        return carry

    lax.fori_loop(0, (used + CHUNK - 1) // CHUNK, chunk, 0)
    for h in range(width // QBLOCK):
        cols = slice(h * QBLOCK, (h + 1) * QBLOCK)
        out_ref[:, h * head_size : (h + 1) * head_size] = (acc[:, cols] / total[0:1, cols]).T.astype(jnp.bfloat16)


def attend(plan, qt, received, page_len, most_rows):
    blocks, head_size, width = qt.shape
    sources = received.shape[0]
    rows_held = most_rows + CHUNK + page_len
    out_width = width // QBLOCK * head_size
    return pl.pallas_call(
        functools.partial(attend_kernel, page_len=page_len),
        grid_spec=pltpu.PrefetchScalarGridSpec(
            num_scalar_prefetch=7,
            grid=(blocks,),
            in_specs=[
                pl.BlockSpec((1, head_size, width), lambda b, *_: (b, 0, 0)),
                pl.BlockSpec(memory_space=pltpu.HBM),
            ],
            out_specs=pl.BlockSpec((QBLOCK, out_width), lambda b, *_: (b, 0)),
            scratch_shapes=[
                pltpu.VMEM((2 * rows_held, head_size), jnp.bfloat16),
                pltpu.VMEM((rows_held, 128), jnp.float32),
                pltpu.VMEM((rows_held, 128), jnp.float32),
                pltpu.VMEM((rows_held, 128), jnp.float32),
                pltpu.VMEM((head_size, width), jnp.float32),
                pltpu.VMEM((8, width), jnp.float32),
                pltpu.VMEM((8, width), jnp.float32),
                pltpu.SemaphoreType.DMA((sources,)),
            ],
        ),
        out_shape=jax.ShapeDtypeStruct((blocks * QBLOCK, out_width), jnp.bfloat16),
        compiler_params=pltpu.CompilerParams(vmem_limit_bytes=24 << 20),
        cost_estimate=pl.CostEstimate(
            flops=4 * blocks * width * most_rows * head_size,
            transcendentals=blocks * width * most_rows,
            bytes_accessed=blocks * (most_rows + width) * 4 * head_size,
        ),
    )(*plan, qt, received)


def query_kernel(x_ref, gain_ref, w_ref, head_gain_ref, out_ref, normed):
    head_size = out_ref.shape[2]

    @pl.when(pl.program_id(0) == 0)
    def _():
        x = x_ref[...].astype(jnp.float32)
        inverse = lax.rsqrt(jnp.mean(x * x, axis=-1, keepdims=True) + tiny_eps)
        normed[...] = (x * inverse * gain_ref[...]).astype(jnp.bfloat16)

    projected = jnp.dot(normed[...], w_ref[...], preferred_element_type=jnp.float32)
    for h in range(w_ref.shape[1] // head_size):
        one = projected[:, h * head_size : (h + 1) * head_size]
        inverse = lax.rsqrt(jnp.mean(one * one, axis=-1, keepdims=True) + tiny_eps)
        query = (one * inverse * head_gain_ref[...] / math.sqrt(head_size)).T.astype(jnp.bfloat16)
        for b in range(QB_DEV):
            cols = slice(b * QBLOCK, (b + 1) * QBLOCK)
            out_ref[0, b, :, h * QBLOCK : (h + 1) * QBLOCK] = query[:, cols]


def project_queries(hidden, norm_gain, w_query, query_gain, kv_local):
    row_count, model_width = hidden.shape
    head_size = query_gain.shape[0]
    group_size = w_query.shape[1] // head_size // kv_local
    tile = 2 * head_size
    tiles = group_size // 2
    return pl.pallas_call(
        query_kernel,
        grid=(kv_local * tiles,),
        in_specs=[
            pl.BlockSpec((row_count, model_width), lambda i: (0, 0)),
            pl.BlockSpec((1, model_width), lambda i: (0, 0)),
            pl.BlockSpec((model_width, tile), lambda i: (0, i)),
            pl.BlockSpec((1, head_size), lambda i: (0, 0)),
        ],
        out_specs=pl.BlockSpec(
            (1, QB_DEV, head_size, 2 * QBLOCK), lambda i: (i // tiles, 0, 0, i % tiles)
        ),
        out_shape=jax.ShapeDtypeStruct((kv_local, QB_DEV, head_size, group_size * QBLOCK), jnp.bfloat16),
        scratch_shapes=[pltpu.VMEM((row_count, model_width), jnp.bfloat16)],
        compiler_params=pltpu.CompilerParams(vmem_limit_bytes=24 << 20),
        cost_estimate=pl.CostEstimate(
            flops=2 * row_count * model_width * w_query.shape[1],
            transcendentals=0,
            bytes_accessed=2 * (w_query.size + 2 * hidden.size),
        ),
    )(hidden, norm_gain[None], w_query, query_gain[None])


def in_three(x):
    high = lax.reduce_precision(x, 8, 7)
    middle = lax.reduce_precision(x - high, 8, 7)
    low = x - high - middle
    return jnp.stack([t.astype(jnp.bfloat16) for t in (high, middle, low)])


def home_plan(slots, counts, rows, used, both, rank, shard):
    shard_count = lax.axis_size("cache")
    first_block = lax.axis_index("cache") * QB_DEV

    def own(x):
        return lax.dynamic_slice_in_dim(x, first_block, QB_DEV, 0)

    own_counts, own_rows = own(counts)[:, None, :], own(rows)[:, None, :]
    sources = jnp.arange(shard_count, dtype=jnp.int32)
    theirs = (own(shard)[:, None, :] == sources[:, None]) & own(used)[:, None, :]
    wanted = jnp.arange(MOST, dtype=jnp.int32)
    picks = theirs[:, :, None, :] & (own(rank)[:, None, None, :] == wanted[:, None])
    got_cnt = jnp.sum(jnp.where(theirs, 1, 0), axis=-1)
    got_height = jnp.sum(jnp.where(theirs, own_rows, 0), axis=-1)
    alone = jnp.sum(jnp.where(theirs & ~own(both)[:, None, :], own_rows, 0), axis=-1)
    got_first = jnp.stack([jnp.zeros_like(alone[0]), alone[0]])
    plan = (got_cnt, got_first, got_height, pick(picks, own_rows), pick(picks, own_counts))
    return tuple(x.reshape(-1) for x in plan), picks, own(slots)


def attended_rows(
    hidden, norm_gain, w_query, query_gain, key_rows, value_rows, told, send_plan, lists, *, height, page_len
):
    head_size = query_gain.shape[0]
    kv_local = key_rows.shape[1] // head_size
    homes = lax.axis_size("cache")
    received = []
    for g in range(kv_local):
        heads = (told,) if g == 0 else ()
        out = pack(send_plan, heads, key_rows, value_rows, g, homes, height, page_len, head_size)
        if g > 0:
            out, received[-1] = lax.optimization_barrier((out, received[-1]))
        received.append(lax.all_to_all(out, "cache", split_axis=0, concat_axis=0, tiled=True))

    queries = project_queries(hidden, norm_gain, w_query, query_gain, kv_local)
    plan, own_picks, own_slots = home_plan(*lists)
    listed = own_slots.shape[-1]

    terms = received[0][:, 2 * height : 2 * height + 3, :].astype(jnp.float32)
    scales = (terms[:, 0] + terms[:, 1]) + terms[:, 2]
    pages_dev = key_rows.shape[0] // page_len
    scales = scales[:, : 2 * kv_local * pages_dev].reshape(homes, 2 * kv_local, pages_dev)
    scales = jnp.swapaxes(scales, 0, 1).reshape(2 * kv_local, homes * pages_dev)
    at_place = own_slots[..., None] == jnp.arange(homes * pages_dev, dtype=jnp.int32)
    found = [jnp.sum(jnp.where(at_place, scales[k], 0.0), axis=-1) for k in range(2 * kv_local)]
    found = [pick(own_picks, f[:, None, :]).reshape(-1) for f in found]

    attended = []
    for g in range(kv_local):
        full_plan = (*plan, found[g] * math.log2(math.e), found[kv_local + g])
        attended.append(attend(full_plan, queries[g], received[g], page_len, listed * page_len))
    return tuple(attended)


def body(
    hidden,
    norm_gain,
    w_query,
    query_gain,
    w_output,
    key_cache,
    value_cache,
    key_scale,
    value_scale,
    page_table,
    page_tokens,
    page_list,
    list_len,
):
    kv_local = key_scale.shape[2]
    pages_dev, page_len = key_cache.shape[1:3]
    listed = page_list.shape[2]
    shard_count = lax.axis_size("cache")
    own_shard = lax.axis_index("cache")

    told = jnp.concatenate([key_scale[0].T, value_scale[0].T], axis=0).reshape(-1)
    told = in_three(told)
    told = jnp.pad(told, ((0, GROUP - 3), (0, key_cache.shape[3] // kv_local - told.shape[1])))

    entry = lookup(page_list[0], page_table * 128 + page_tokens)
    slots, counts = entry // 128, entry % 128
    used = jnp.arange(listed, dtype=jnp.int32) < list_len[0][:, None]
    rows = (counts + GRANULE - 1) // GRANULE * GRANULE
    homes = shard_count
    twin_slots = jnp.where(used, slots, -1).reshape(homes, QB_DEV, listed)[:, ::-1].reshape(-1, listed)
    both = jnp.any(slots[:, :, None] == twin_slots[:, None, :], axis=-1)
    second = (jnp.arange(homes * QB_DEV) % QB_DEV == 1)[:, None]
    shard, place = slots // pages_dev, slots % pages_dev
    order = jnp.where(used, place + jnp.where(both == second, 0, pages_dev), -1)
    earlier = (
        (shard[:, :, None] == shard[:, None, :])
        & used[:, :, None]
        & (order[:, :, None] < order[:, None, :])
    )
    rank = jnp.sum(jnp.where(earlier, 1, 0), axis=1)
    once = used & ~(both & second)
    sources = jnp.arange(shard_count, dtype=jnp.int32)
    at_source = shard[:, None, :] == sources[:, None]
    asked = jnp.sum(jnp.where(at_source & once[:, None, :], rows[:, None, :], 0), axis=-1)
    need = jnp.max(asked.reshape(homes, QB_DEV, shard_count).sum(axis=1))
    wanted = jnp.arange(MOST, dtype=jnp.int32)

    mine = (shard == own_shard) & once
    shared = jnp.sum(jnp.where(mine & both, 1, 0), axis=-1).reshape(homes, QB_DEV)[:, :1]
    behind = jnp.concatenate([jnp.zeros_like(shared), shared], axis=1).reshape(-1)
    picks = mine[:, None, :] & ((rank - behind[:, None])[:, None, :] == wanted[:, None])
    send_plan = (pick(picks, rows).reshape(-1), pick(picks, place).reshape(-1))

    devices = lax.axis_size("sections")
    agreed = need.astype(jnp.int32)[None]
    for step in range(1, devices):
        route = [(i, (i + step) % devices) for i in range(devices)]
        agreed = jnp.maximum(agreed, lax.ppermute(need.astype(jnp.int32)[None], "sections", route))
    agreed = agreed[0]

    key_rows = key_cache[0].reshape(pages_dev * page_len, -1)
    value_rows = value_cache[0].reshape(pages_dev * page_len, -1)
    most = QB_DEV * MOST * page_len
    heights = tuple(h for h in HEIGHTS if h < most) + (most,)
    branch = jnp.sum(jnp.where(agreed > jnp.array(heights[:-1], jnp.int32), 1, 0))
    send_plan, told, branch = lax.optimization_barrier((send_plan, told, branch))
    attended = lax.switch(
        branch,
        [functools.partial(attended_rows, height=h, page_len=page_len) for h in heights],
        hidden[0], norm_gain[0], w_query[0], query_gain[0], key_rows, value_rows, told, send_plan,
        (slots, counts, rows, used, both, rank, shard),
    )

    model_width = hidden.shape[2]
    heads_index = lax.axis_index("heads")
    half_width = model_width // lax.axis_size("heads")
    came, kept = [], []
    for b in range(QB_DEV):
        rows_here = slice(b * QBLOCK, (b + 1) * QBLOCK)
        both_heads = jnp.concatenate([a[rows_here] for a in attended], axis=1)
        if b > 0:
            both_heads, came[b - 1] = lax.optimization_barrier((both_heads, came[b - 1]))
        whole = jnp.dot(both_heads, w_output[0], preferred_element_type=jnp.float32)
        away = lax.dynamic_slice_in_dim(whole, (1 - heads_index) * half_width, half_width, 1)
        came.append(lax.ppermute(away.astype(jnp.bfloat16), "heads", [(0, 1), (1, 0)]))
        kept.append(lax.dynamic_slice_in_dim(whole, heads_index * half_width, half_width, 1))
    moved, result = [], None
    for b in range(QB_DEV):
        if result is not None:
            came[b], _ = lax.optimization_barrier((came[b], result))
        residual = lax.dynamic_slice(
            hidden[0], (b * QBLOCK, heads_index * half_width), (QBLOCK, half_width)
        ).astype(jnp.float32)
        result = (kept[b] + came[b].astype(jnp.float32) + residual).astype(jnp.bfloat16)
        moved.append(lax.ppermute(result, "sections", [((i - 1) % devices, i) for i in range(devices)]))
    return jnp.concatenate(moved, axis=0)[None]


def solution(mesh):
    return jax.shard_map(
        body,
        mesh=mesh,
        in_specs=(
            P("sections", "cache", None),
            P("sections", None),
            P("sections", None, "heads"),
            P("sections", None),
            P("sections", "heads", None),
            P("sections", "cache", None, "heads"),
            P("sections", "cache", None, "heads"),
            P("sections", "cache", "heads"),
            P("sections", "cache", "heads"),
            P(),
            P(),
            P("sections", None, None),
            P("sections", None),
        ),
        out_specs=P("sections", "cache", "heads"),
        check_vma=False,
    )
```

```python
import functools
import math

import jax
import jax.numpy as jnp
from jax import lax
from jax.experimental import pallas as pl
from jax.experimental.pallas import tpu as pltpu
from jax.sharding import PartitionSpec as P

QBLOCK = 128
QB_DEV = 2
MOST = 8
GRANULE = 8
GROUP = 2 * GRANULE
HEIGHTS = (576, 656)
BUFFERS = 8
CHUNK = 512
QTILE = 512

tiny_eps = 1e-06
masked_score = -1e30
lowest = -1e38


def lookup(entries, table):
    places = jnp.arange(table.shape[0], dtype=jnp.int32)
    return jnp.sum(jnp.where(entries[..., None] == places, table, 0), axis=-1)


def pick(picks, values):
    return jnp.sum(jnp.where(picks, values[..., None, :], 0), axis=-1)


def pack_kernel(rows_ref, page_ref, *refs, page_len, height):
    *head_refs, k_ref, v_ref, out_ref, mixed, buf, sems = refs
    homes = out_ref.shape[0]
    tokens, head_size = k_ref.shape
    page_rows, sent_rows = 2 * page_len, 2 * height
    for slot in range(BUFFERS):
        for head_ref in head_refs:
            buf[slot, pl.ds(page_rows + sent_rows, GROUP), :] = head_ref[...]

    def mix(p, carry):
        here = pl.ds(pl.multiple_of(p * page_len, page_len), page_len)
        keys, values = (
            ref[here, :].astype(jnp.float32).reshape(page_len // GRANULE, 1, GRANULE, head_size)
            for ref in (k_ref, v_ref)
        )
        pair = jnp.concatenate([keys, values], axis=1).reshape(page_rows, head_size)
        mixed[pl.ds(pl.multiple_of(p * page_rows, page_rows), page_rows), :] = pair.astype(jnp.bfloat16)
        return carry

    lax.fori_loop(0, tokens // page_len, mix, 0)

    def copies_of(home, slot):
        copies = [(0, sent_rows)] + [(page_rows + sent_rows, GROUP)] * len(head_refs)
        starts = (0, sent_rows)
        return [
            pltpu.make_async_copy(
                buf.at[slot, pl.ds(here, n), :], out_ref.at[home, pl.ds(there, n), :], sems.at[slot, i]
            )
            for i, ((here, n), there) in enumerate(zip(copies, starts))
        ]

    def one_home(home, carry):
        slot = lax.rem(home, BUFFERS)

        @pl.when(home >= BUFFERS)
        def _():
            for copy in copies_of(home - BUFFERS, slot):
                copy.wait()

        row = jnp.int32(0)
        for j in range(QB_DEV * MOST):
            at = home * (QB_DEV * MOST) + j
            here = pl.multiple_of(page_ref[at] * page_rows, page_rows)
            there = pl.multiple_of(row * 2, GROUP)
            buf[slot, pl.ds(there, page_rows), :] = mixed[pl.ds(here, page_rows), :]
            row = row + rows_ref[at]
        for copy in copies_of(home, slot):
            copy.start()
        return carry

    lax.fori_loop(0, homes, one_home, 0)
    for home in range(homes - BUFFERS, homes):
        for copy in copies_of(home, home % BUFFERS):
            copy.wait()


def pack(plan, heads, key_rows, value_rows, g, homes, height, page_len, head_size):
    tokens = key_rows.shape[0]
    sent = 2 * height + GROUP * len(heads)
    return pl.pallas_call(
        functools.partial(pack_kernel, page_len=page_len, height=height),
        grid_spec=pltpu.PrefetchScalarGridSpec(
            num_scalar_prefetch=2,
            grid=(1,),
            in_specs=[pl.BlockSpec(h.shape, lambda i, *_: (0, 0)) for h in heads]
            + [
                pl.BlockSpec((tokens, head_size), lambda i, *_: (0, g)),
                pl.BlockSpec((tokens, head_size), lambda i, *_: (0, g)),
            ],
            out_specs=pl.BlockSpec(memory_space=pltpu.HBM),
            scratch_shapes=[
                pltpu.VMEM((2 * tokens, head_size), jnp.bfloat16),
                pltpu.VMEM((BUFFERS, 2 * (height + page_len) + GROUP, head_size), jnp.bfloat16),
                pltpu.SemaphoreType.DMA((BUFFERS, 2)),
            ],
        ),
        out_shape=jax.ShapeDtypeStruct((homes, sent, head_size), jnp.bfloat16),
        compiler_params=pltpu.CompilerParams(vmem_limit_bytes=60 << 20),
        cost_estimate=pl.CostEstimate(
            flops=0, transcendentals=0, bytes_accessed=homes * sent * 2 * head_size + tokens * 4 * head_size
        ),
    )(*plan, *heads, key_rows, value_rows)


def attend_kernel(
    cnt_ref, first_ref, height_ref, rows_ref, live_ref, kscale_ref, vscale_ref,
    qt_ref, recv_ref, out_ref,
    kv, kcol, vcol, bias, acc, top, total, sems, *, page_len,
):
    sources = recv_ref.shape[0]
    head_size, width = qt_ref.shape[1:]
    lists = pl.program_id(0) * sources

    def copy_of(s, at):
        n = pl.multiple_of(height_ref[lists + s] * 2, GROUP)
        start = pl.multiple_of(first_ref[lists + s] * 2, GROUP)
        at = pl.multiple_of(at * 2, GROUP)
        return pltpu.make_async_copy(
            recv_ref.at[s, pl.ds(start, n), :], kv.at[pl.ds(at, n), :], sems.at[s]
        )

    def start_one(s, at):
        @pl.when(height_ref[lists + s] > 0)
        def _():
            copy_of(s, at).start()

        return at + height_ref[lists + s]

    def wait_one(s, at):
        @pl.when(height_ref[lists + s] > 0)
        def _():
            copy_of(s, at).wait()

        return at + height_ref[lists + s]

    used = lax.fori_loop(0, sources, start_one, jnp.int32(0))
    token = lax.broadcasted_iota(jnp.int32, (page_len, 128), 0)

    def columns_of(s, at):
        def one_page(j, at):
            e = (lists + s) * MOST + j
            here = pl.ds(pl.multiple_of(at, GRANULE), page_len)
            kcol[here, :] = jnp.full((page_len, 128), kscale_ref[e], jnp.float32)
            vcol[here, :] = jnp.full((page_len, 128), vscale_ref[e], jnp.float32)
            bias[here, :] = jnp.where(token < live_ref[e], 0.0, masked_score)
            return at + rows_ref[e]

        return lax.fori_loop(0, cnt_ref[lists + s], one_page, at)

    lax.fori_loop(0, sources, columns_of, jnp.int32(0))
    rest = pl.ds(pl.multiple_of(used, GRANULE), CHUNK)
    kcol[rest, :] = jnp.zeros((CHUNK, 128), jnp.float32)
    vcol[rest, :] = jnp.zeros((CHUNK, 128), jnp.float32)
    bias[rest, :] = jnp.full((CHUNK, 128), masked_score, jnp.float32)
    kv[pl.ds(pl.multiple_of(used * 2, GROUP), 2 * CHUNK), :] = jnp.zeros((2 * CHUNK, head_size), jnp.bfloat16)
    acc[...] = jnp.zeros_like(acc)
    total[...] = jnp.zeros_like(total)
    top[...] = jnp.full_like(top, lowest)
    lax.fori_loop(0, sources, wait_one, jnp.int32(0))

    def chunk(c, carry):
        here = pl.ds(pl.multiple_of(c * CHUNK, CHUNK), CHUNK)
        pair = kv[pl.ds(pl.multiple_of(c * 2 * CHUNK, 2 * CHUNK), 2 * CHUNK), :].astype(jnp.float32)
        pair = pair.reshape(CHUNK // GRANULE, 2, GRANULE, head_size)
        keys = pair[:, 0].reshape(CHUNK, head_size).astype(jnp.bfloat16)
        values = pair[:, 1].reshape(CHUNK, head_size).astype(jnp.bfloat16).T
        for i in range(width // QTILE):
            cols = pl.ds(i * QTILE, QTILE)
            score = jnp.dot(keys, qt_ref[0, :, cols], preferred_element_type=jnp.float32)
            kc, bc, vc = kcol[here, :], bias[here, :], vcol[here, :]
            wide = lambda x: jnp.concatenate([x] * (QTILE // 128), axis=1)
            score = score * wide(kc) + wide(bc)
            old = top[0:1, cols]
            new = jnp.maximum(old, jnp.max(score, axis=0, keepdims=True))
            weight = jnp.exp2(score - new)
            fade = jnp.exp2(old - new)
            total[0:1, cols] = total[0:1, cols] * fade + jnp.sum(weight, axis=0, keepdims=True)
            scaled = (weight * wide(vc)).astype(jnp.bfloat16)
            acc[:, cols] = acc[:, cols] * fade + jnp.dot(values, scaled, preferred_element_type=jnp.float32)
            top[0:1, cols] = new
        return carry

    lax.fori_loop(0, (used + CHUNK - 1) // CHUNK, chunk, 0)
    for h in range(width // QBLOCK):
        cols = slice(h * QBLOCK, (h + 1) * QBLOCK)
        out_ref[:, h * head_size : (h + 1) * head_size] = (acc[:, cols] / total[0:1, cols]).T.astype(jnp.bfloat16)


def attend(plan, qt, received, page_len, most_rows):
    blocks, head_size, width = qt.shape
    sources = received.shape[0]
    rows_held = most_rows + CHUNK + page_len
    out_width = width // QBLOCK * head_size
    return pl.pallas_call(
        functools.partial(attend_kernel, page_len=page_len),
        grid_spec=pltpu.PrefetchScalarGridSpec(
            num_scalar_prefetch=7,
            grid=(blocks,),
            in_specs=[
                pl.BlockSpec((1, head_size, width), lambda b, *_: (b, 0, 0)),
                pl.BlockSpec(memory_space=pltpu.HBM),
            ],
            out_specs=pl.BlockSpec((QBLOCK, out_width), lambda b, *_: (b, 0)),
            scratch_shapes=[
                pltpu.VMEM((2 * rows_held, head_size), jnp.bfloat16),
                pltpu.VMEM((rows_held, 128), jnp.float32),
                pltpu.VMEM((rows_held, 128), jnp.float32),
                pltpu.VMEM((rows_held, 128), jnp.float32),
                pltpu.VMEM((head_size, width), jnp.float32),
                pltpu.VMEM((8, width), jnp.float32),
                pltpu.VMEM((8, width), jnp.float32),
                pltpu.SemaphoreType.DMA((sources,)),
            ],
        ),
        out_shape=jax.ShapeDtypeStruct((blocks * QBLOCK, out_width), jnp.bfloat16),
        compiler_params=pltpu.CompilerParams(vmem_limit_bytes=24 << 20),
        cost_estimate=pl.CostEstimate(
            flops=4 * blocks * width * most_rows * head_size,
            transcendentals=blocks * width * most_rows,
            bytes_accessed=blocks * (most_rows + width) * 4 * head_size,
        ),
    )(*plan, qt, received)


def query_kernel(x_ref, gain_ref, w_ref, head_gain_ref, out_ref, normed):
    head_size = out_ref.shape[2]

    @pl.when(pl.program_id(0) == 0)
    def _():
        x = x_ref[...].astype(jnp.float32)
        inverse = lax.rsqrt(jnp.mean(x * x, axis=-1, keepdims=True) + tiny_eps)
        normed[...] = (x * inverse * gain_ref[...]).astype(jnp.bfloat16)

    projected = jnp.dot(normed[...], w_ref[...], preferred_element_type=jnp.float32)
    for h in range(w_ref.shape[1] // head_size):
        one = projected[:, h * head_size : (h + 1) * head_size]
        inverse = lax.rsqrt(jnp.mean(one * one, axis=-1, keepdims=True) + tiny_eps)
        query = (one * inverse * head_gain_ref[...] / math.sqrt(head_size)).T.astype(jnp.bfloat16)
        for b in range(QB_DEV):
            cols = slice(b * QBLOCK, (b + 1) * QBLOCK)
            out_ref[0, b, :, h * QBLOCK : (h + 1) * QBLOCK] = query[:, cols]


def project_queries(hidden, norm_gain, w_query, query_gain, kv_local):
    row_count, model_width = hidden.shape
    head_size = query_gain.shape[0]
    group_size = w_query.shape[1] // head_size // kv_local
    tile = 2 * head_size
    tiles = group_size // 2
    return pl.pallas_call(
        query_kernel,
        grid=(kv_local * tiles,),
        in_specs=[
            pl.BlockSpec((row_count, model_width), lambda i: (0, 0)),
            pl.BlockSpec((1, model_width), lambda i: (0, 0)),
            pl.BlockSpec((model_width, tile), lambda i: (0, i)),
            pl.BlockSpec((1, head_size), lambda i: (0, 0)),
        ],
        out_specs=pl.BlockSpec(
            (1, QB_DEV, head_size, 2 * QBLOCK), lambda i: (i // tiles, 0, 0, i % tiles)
        ),
        out_shape=jax.ShapeDtypeStruct((kv_local, QB_DEV, head_size, group_size * QBLOCK), jnp.bfloat16),
        scratch_shapes=[pltpu.VMEM((row_count, model_width), jnp.bfloat16)],
        compiler_params=pltpu.CompilerParams(vmem_limit_bytes=24 << 20),
        cost_estimate=pl.CostEstimate(
            flops=2 * row_count * model_width * w_query.shape[1],
            transcendentals=0,
            bytes_accessed=2 * (w_query.size + 2 * hidden.size),
        ),
    )(hidden, norm_gain[None], w_query, query_gain[None])


def in_three(x):
    high = lax.reduce_precision(x, 8, 7)
    middle = lax.reduce_precision(x - high, 8, 7)
    low = x - high - middle
    return jnp.stack([t.astype(jnp.bfloat16) for t in (high, middle, low)])


def home_plan(slots, counts, rows, used, both, rank, shard):
    shard_count = lax.axis_size("cache")
    first_block = lax.axis_index("cache") * QB_DEV

    def own(x):
        return lax.dynamic_slice_in_dim(x, first_block, QB_DEV, 0)

    own_counts, own_rows = own(counts)[:, None, :], own(rows)[:, None, :]
    sources = jnp.arange(shard_count, dtype=jnp.int32)
    theirs = (own(shard)[:, None, :] == sources[:, None]) & own(used)[:, None, :]
    wanted = jnp.arange(MOST, dtype=jnp.int32)
    picks = theirs[:, :, None, :] & (own(rank)[:, None, None, :] == wanted[:, None])
    got_cnt = jnp.sum(jnp.where(theirs, 1, 0), axis=-1)
    got_height = jnp.sum(jnp.where(theirs, own_rows, 0), axis=-1)
    alone = jnp.sum(jnp.where(theirs & ~own(both)[:, None, :], own_rows, 0), axis=-1)
    got_first = jnp.stack([jnp.zeros_like(alone[0]), alone[0]])
    plan = (got_cnt, got_first, got_height, pick(picks, own_rows), pick(picks, own_counts))
    return tuple(x.reshape(-1) for x in plan), picks, own(slots)


def attended_rows(
    hidden, norm_gain, w_query, query_gain, key_rows, value_rows, told, send_plan, lists, *, height, page_len
):
    head_size = query_gain.shape[0]
    kv_local = key_rows.shape[1] // head_size
    homes = lax.axis_size("cache")
    received = []
    for g in range(kv_local):
        heads = (told,) if g == 0 else ()
        out = pack(send_plan, heads, key_rows, value_rows, g, homes, height, page_len, head_size)
        if g > 0:
            out, received[-1] = lax.optimization_barrier((out, received[-1]))
        received.append(lax.all_to_all(out, "cache", split_axis=0, concat_axis=0, tiled=True))

    queries = project_queries(hidden, norm_gain, w_query, query_gain, kv_local)
    plan, own_picks, own_slots = home_plan(*lists)
    listed = own_slots.shape[-1]

    terms = received[0][:, 2 * height : 2 * height + 3, :].astype(jnp.float32)
    scales = (terms[:, 0] + terms[:, 1]) + terms[:, 2]
    pages_dev = key_rows.shape[0] // page_len
    scales = scales[:, : 2 * kv_local * pages_dev].reshape(homes, 2 * kv_local, pages_dev)
    scales = jnp.swapaxes(scales, 0, 1).reshape(2 * kv_local, homes * pages_dev)
    at_place = own_slots[..., None] == jnp.arange(homes * pages_dev, dtype=jnp.int32)
    found = [jnp.sum(jnp.where(at_place, scales[k], 0.0), axis=-1) for k in range(2 * kv_local)]
    found = [pick(own_picks, f[:, None, :]).reshape(-1) for f in found]

    attended = []
    for g in range(kv_local):
        full_plan = (*plan, found[g] * math.log2(math.e), found[kv_local + g])
        attended.append(attend(full_plan, queries[g], received[g], page_len, listed * page_len))
    return tuple(attended)


def body(
    hidden,
    norm_gain,
    w_query,
    query_gain,
    w_output,
    key_cache,
    value_cache,
    key_scale,
    value_scale,
    page_table,
    page_tokens,
    page_list,
    list_len,
):
    kv_local = key_scale.shape[2]
    pages_dev, page_len = key_cache.shape[1:3]
    listed = page_list.shape[2]
    shard_count = lax.axis_size("cache")
    own_shard = lax.axis_index("cache")

    told = jnp.concatenate([key_scale[0].T, value_scale[0].T], axis=0).reshape(-1)
    told = in_three(told)
    told = jnp.pad(told, ((0, GROUP - 3), (0, key_cache.shape[3] // kv_local - told.shape[1])))

    entry = lookup(page_list[0], page_table * 128 + page_tokens)
    slots, counts = entry // 128, entry % 128
    used = jnp.arange(listed, dtype=jnp.int32) < list_len[0][:, None]
    rows = (counts + GRANULE - 1) // GRANULE * GRANULE
    homes = shard_count
    twin_slots = jnp.where(used, slots, -1).reshape(homes, QB_DEV, listed)[:, ::-1].reshape(-1, listed)
    both = jnp.any(slots[:, :, None] == twin_slots[:, None, :], axis=-1)
    second = (jnp.arange(homes * QB_DEV) % QB_DEV == 1)[:, None]
    shard, place = slots // pages_dev, slots % pages_dev
    order = jnp.where(used, place + jnp.where(both == second, 0, pages_dev), -1)
    earlier = (
        (shard[:, :, None] == shard[:, None, :])
        & used[:, :, None]
        & (order[:, :, None] < order[:, None, :])
    )
    rank = jnp.sum(jnp.where(earlier, 1, 0), axis=1)
    once = used & ~(both & second)
    sources = jnp.arange(shard_count, dtype=jnp.int32)
    at_source = shard[:, None, :] == sources[:, None]
    asked = jnp.sum(jnp.where(at_source & once[:, None, :], rows[:, None, :], 0), axis=-1)
    need = jnp.max(asked.reshape(homes, QB_DEV, shard_count).sum(axis=1))
    wanted = jnp.arange(MOST, dtype=jnp.int32)

    mine = (shard == own_shard) & once
    shared = jnp.sum(jnp.where(mine & both, 1, 0), axis=-1).reshape(homes, QB_DEV)[:, :1]
    behind = jnp.concatenate([jnp.zeros_like(shared), shared], axis=1).reshape(-1)
    picks = mine[:, None, :] & ((rank - behind[:, None])[:, None, :] == wanted[:, None])
    send_plan = (pick(picks, rows).reshape(-1), pick(picks, place).reshape(-1))

    devices = lax.axis_size("sections")
    agreed = need.astype(jnp.int32)[None]
    for step in range(1, devices):
        route = [(i, (i + step) % devices) for i in range(devices)]
        agreed = jnp.maximum(agreed, lax.ppermute(need.astype(jnp.int32)[None], "sections", route))
    agreed = agreed[0]

    key_rows = key_cache[0].reshape(pages_dev * page_len, -1)
    value_rows = value_cache[0].reshape(pages_dev * page_len, -1)
    most = QB_DEV * MOST * page_len
    heights = tuple(h for h in HEIGHTS if h < most) + (most,)
    branch = jnp.sum(jnp.where(agreed > jnp.array(heights[:-1], jnp.int32), 1, 0))
    send_plan, told, branch = lax.optimization_barrier((send_plan, told, branch))
    attended = lax.switch(
        branch,
        [functools.partial(attended_rows, height=h, page_len=page_len) for h in heights],
        hidden[0], norm_gain[0], w_query[0], query_gain[0], key_rows, value_rows, told, send_plan,
        (slots, counts, rows, used, both, rank, shard),
    )

    model_width = hidden.shape[2]
    heads_index = lax.axis_index("heads")
    half_width = model_width // lax.axis_size("heads")
    came, kept = [], []
    for b in range(QB_DEV):
        rows_here = slice(b * QBLOCK, (b + 1) * QBLOCK)
        both_heads = jnp.concatenate([a[rows_here] for a in attended], axis=1)
        if b > 0:
            both_heads, came[b - 1] = lax.optimization_barrier((both_heads, came[b - 1]))
        whole = jnp.dot(both_heads, w_output[0], preferred_element_type=jnp.float32)
        away = lax.dynamic_slice_in_dim(whole, (1 - heads_index) * half_width, half_width, 1)
        came.append(lax.ppermute(away.astype(jnp.bfloat16), "heads", [(0, 1), (1, 0)]))
        kept.append(lax.dynamic_slice_in_dim(whole, heads_index * half_width, half_width, 1))
    moved, result = [], None
    for b in range(QB_DEV):
        if result is not None:
            came[b], _ = lax.optimization_barrier((came[b], result))
        residual = lax.dynamic_slice(
            hidden[0], (b * QBLOCK, heads_index * half_width), (QBLOCK, half_width)
        ).astype(jnp.float32)
        result = (kept[b] + came[b].astype(jnp.float32) + residual).astype(jnp.bfloat16)
        moved.append(lax.ppermute(result, "sections", [((i - 1) % devices, i) for i in range(devices)]))
    return jnp.concatenate(moved, axis=0)[None]


def solution(mesh):
    return jax.shard_map(
        body,
        mesh=mesh,
        in_specs=(
            P("sections", "cache", None),
            P("sections", None),
            P("sections", None, "heads"),
            P("sections", None),
            P("sections", "heads", None),
            P("sections", "cache", None, "heads"),
            P("sections", "cache", None, "heads"),
            P("sections", "cache", "heads"),
            P("sections", "cache", "heads"),
            P(),
            P(),
            P("sections", None, None),
            P("sections", None),
        ),
        out_specs=P("sections", "cache", "heads"),
        check_vma=False,
    )
```
